32 devices in a mesh: dp: 4 (over y, x), mp: 8 (over z, core).
Axes of the slice: x: 2, y: 2, z: 4, core: 2. Of those that a mesh axis runs over, the one named last changes fastest.
Arguments:
- inputs: bfloat16 [4, 2304, 1024], P('dp', 'mp'), may hold values from -6 to 6
- resets: int32 [4, 1024], P('dp'), may hold values from 0 to 1
- owners: int32 [57], replicated, may hold values from 0 to 3, as said below
- kernel: float32 [96, 2304, 256], P('dp', 'mp'), may hold values from -0.09375 to 0.09375
- kernel_first: float32 [96, 2304, 256], P('dp', 'mp'), may hold values from -0.00011799647 to 0.00011799647
- kernel_second: float32 [96, 2304, 256], P('dp', 'mp'), may hold values from 3.1389873e-11 to 1.255595e-10
- bias_rows: float32 [12, 2304], P('dp', 'mp'), may hold values from -0.18 to 0.18
- bias_first: float32 [12, 2304], P('dp', 'mp'), may hold values from -0.00011799647 to 0.00011799647
- bias_second: float32 [12, 2304], P('dp', 'mp'), may hold values from 3.1389873e-11 to 1.255595e-10
- cotangent: bfloat16 [4, 2304, 1024], P('dp', 'mp'), may hold values from -15 to 15
Outputs:
- outputs: bfloat16 [4, 2304, 1024], P('dp', 'mp')
- input_grads: bfloat16 [4, 2304, 1024], P('dp', 'mp')
- kernel_new: float32 [96, 2304, 256], P('dp', 'mp')
- kernel_first_new: float32 [96, 2304, 256], P('dp', 'mp')
- kernel_second_new: float32 [96, 2304, 256], P('dp', 'mp')
- bias_new: float32 [12, 2304], P('dp', 'mp')
- bias_first_new: float32 [12, 2304], P('dp', 'mp')
- bias_second_new: float32 [12, 2304], P('dp', 'mp')
- grad_norm: float32 [], replicated
The draws below stay inside these ranges and needn't reach their ends.
Inputs may be any that keep to these rules, and one draw needn't show every extreme that they name: Entries 0 to 53 name the dp index owning each kernel block, the last 3 the owners of the three gates' biases. Each dp index owns at most 24 kernel blocks, and one owns exactly 24.
All inputs are finite; a program needn't handle non-finite values.
Results may differ from the reference program's by a relative error of at most 0.0065.
Values may be sent and summed in bfloat16 or wider, within the bound.
A program may use at most 256 MiB of HBM per device.

```python
import math
import jax
import jax.numpy as jnp
from jax import lax

D = 2304
BR = 256
LEN = 1024
S_DEV = 1
STEP = 10
STREAMS = 4
KB = 18
NKB = 54
CAP = 24
KSLOTS = 96
NPARAM = 31857408
N_DP = 4


def draw_owners(key, part):
    keys = jax.random.split(jax.random.fold_in(key, 11), 5)
    remain = NKB - CAP
    first = jax.random.randint(keys[0], (), remain // 5, remain // 3 + 1)
    second = jax.random.randint(keys[1], (), remain // 5, remain // 3 + 1)
    counts = jnp.stack([jnp.int32(CAP), first, second, remain - first - second]).astype(jnp.int32)
    ends = jnp.cumsum(counts)
    places = jnp.arange(NKB, dtype=jnp.int32)
    device = jnp.sum((places[:, None] >= ends[None, :]).astype(jnp.int32), axis=1)
    offset = jax.random.randint(keys[2], (), 0, N_DP)
    device = (device + offset) % N_DP
    order = jax.random.permutation(keys[3], NKB)
    kernel_owner = device[jnp.argsort(order, stable=True)]
    bias_owner = jax.random.randint(keys[4], (3,), 0, N_DP)
    return jnp.concatenate([kernel_owner, bias_owner]).astype(jnp.int32)


def draw_resets(key, part):
    draws = jax.random.randint(jax.random.fold_in(key, 23), (STREAMS, LEN), 0, LEN * STREAMS)
    limit = 2 * STREAMS + 6 * jnp.arange(STREAMS, dtype=jnp.int32)[:, None]
    return (draws < limit).astype(jnp.int32)


def draw_cotangent(key, part):
    inner = jax.random.fold_in(key, 37)
    column = jnp.arange(D, dtype=jnp.float32) / (D - 1)
    base = jnp.clip(jax.random.normal(inner, (STREAMS, D, LEN), jnp.float32), -5.0, 5.0)
    rising = 1.0 + 2.0 * column
    return (base * rising[:, None]).astype(jnp.bfloat16)


def level_of(rng, extent, cuts, least, high):
    def one(position, shards_of):
        heights = jax.random.uniform(jax.random.fold_in(jax.random.fold_in(rng, 6), position), (shards_of,), jnp.float32, least / len(cuts), high / len(cuts))
        return jnp.repeat(jnp.exp(heights), extent[position] // shards_of).reshape((-1,) + (1,) * (len(extent) - position - 1))

    factor_of = one(*cuts[0])
    for cut in cuts[1:]:
        factor_of = factor_of * one(*cut)
    return factor_of


def noise(key, extent, width, bound, cuts=(), held_as=jnp.bfloat16):
    values = width * jax.random.normal(key, extent, jnp.float32)
    if cuts:
        values = values * level_of(key, extent, cuts, -0.22, 0.18)
    return jnp.clip(values, -bound, bound).astype(held_as)


def setup_inputs(seed: int = 0) -> dict:
    seeds = jax.random.split(jax.random.key(seed), 11)
    return {
        "inputs": noise(seeds[0], (STREAMS, D, LEN), 1.0, 6.0, ((0, 4), (1, 8))),
        "resets": draw_resets(jax.random.fold_in(seeds[10], 71), 0),
        "owners": draw_owners(jax.random.fold_in(seeds[10], 71), 0),
        "kernel": noise(seeds[3], (KSLOTS, D, BR), (2 * D) ** -0.5, 0.09375, ((0, 4), (1, 8)), jnp.float32),
        "kernel_first": noise(seeds[4], (KSLOTS, D, BR), (0.111 * NPARAM ** -0.5), 0.00011799647, ((0, 4), (1, 8)), jnp.float32),
        "kernel_second": jnp.clip(jnp.exp(math.log(1.2555949335801841e-10) - 1.3862944 * jax.random.uniform(seeds[5], (KSLOTS, D, BR), jnp.float32) ** level_of(seeds[5], (KSLOTS, D, BR), ((0, 4), (1, 8)), -0.2, 0.2)), 3.1389873339504604e-11, 1.2555949335801841e-10),
        "bias_rows": noise(seeds[6], (N_DP * 3, D), 0.03, 0.18, ((0, 4), (1, 8)), jnp.float32),
        "bias_first": noise(seeds[7], (N_DP * 3, D), (0.111 * NPARAM ** -0.5), 0.00011799647, ((0, 4), (1, 8)), jnp.float32),
        "bias_second": jnp.clip(jnp.exp(math.log(1.2555949335801841e-10) - 1.3862944 * jax.random.uniform(seeds[8], (N_DP * 3, D), jnp.float32) ** level_of(seeds[8], (N_DP * 3, D), ((0, 4), (1, 8)), -0.2, 0.2)), 3.1389873339504604e-11, 1.2555949335801841e-10),
        "cotangent": draw_cotangent(jax.random.fold_in(seeds[10], 71), 0),
    }


@jax.custom_vjp
def low(v):
    return lax.optimization_barrier(v.astype(jnp.bfloat16)).astype(jnp.float32)

@jax.custom_vjp
def low_back(v):
    return v

def low_keep(v):
    return (low(v), None)

def low_pass(kept, grad):
    return (grad,)

def back_keep(v):
    return (v, None)

def back_low(kept, grad):
    return (low(grad),)
low.defvjp(low_keep, low_pass)
low_back.defvjp(back_keep, back_low)

def earlier_count(owned):
    number = owned.shape[0]
    places = jnp.arange(number, dtype=jnp.int32)
    earlier = (owned[:, None] == owned[None, :]) & (places[None, :] < places[:, None])
    return lax.optimization_barrier(jnp.sum(earlier.astype(jnp.int32), axis=1)).astype(jnp.int32)

def combine(earlier, later):
    return (earlier[0] * later[0], later[0] * earlier[1] + later[1])

def group_output(stream_inputs, keeping, weights, biases):
    earlier_inputs = jnp.pad(stream_inputs, ((0, 0), (1, 0), (0, 0)))[:, :-1]
    paired = jnp.concatenate([stream_inputs, earlier_inputs], axis=2)
    preact = jnp.einsum('slk,gkc->slgc', paired, weights, precision=lax.Precision.HIGHEST) + biases[None, None]
    preact = low_back(preact)
    candidate = jnp.tanh(preact[:, :, 0])
    forget = jax.nn.sigmoid(preact[:, :, 1])
    output_gate = jax.nn.sigmoid(preact[:, :, 2])
    decay = forget * keeping[:, :, None]
    _, cells = lax.associative_scan(combine, (decay, (1.0 - forget) * candidate), axis=1)
    return output_gate * cells

def adam_step(weights, first, second, grad, decay_rate):
    rate = (2.0 * D) ** (-0.5)
    first_new = 0.9 * first + 0.1 * grad
    second_new = 0.999 * second + 0.001 * grad * grad
    first_hat = first_new / (1.0 - 0.9 ** STEP)
    second_hat = second_new / (1.0 - 0.999 ** STEP)
    weights_new = weights - rate * (first_hat / (jnp.sqrt(second_hat) + 1e-08) + decay_rate * weights)
    return (weights_new, first_new, second_new)

def placed(store, slot, rows):
    return jnp.zeros_like(store).at[slot].set(rows)

def reference(inputs, resets, owners, kernel, kernel_first, kernel_second, bias_rows, bias_first, bias_second, cotangent):
    kernel_owner = owners[:NKB]
    bias_owner = owners[NKB:]
    kernel_slot = (kernel_owner * CAP + earlier_count(kernel_owner)).astype(jnp.int32)
    bias_slot = (bias_owner * 3 + earlier_count(bias_owner)).astype(jnp.int32)
    weights = kernel[kernel_slot].reshape(3, KB, D, BR).transpose(0, 2, 1, 3).reshape(3, D, 2 * D).transpose(0, 2, 1)
    biases = bias_rows[bias_slot]
    keeping = (1 - resets).astype(jnp.float32).reshape(N_DP, S_DEV, LEN)

    def forward(features, weights, biases):
        rounded_w = low(weights)
        rounded_b = low(biases)

        def one_group(carry, item):
            return (carry, group_output(item[0], item[1], rounded_w, rounded_b))
        _, result = lax.scan(jax.checkpoint(one_group), jnp.zeros((), jnp.float32), (features.reshape(N_DP, S_DEV, LEN, D), keeping))
        return result.reshape(STREAMS, LEN, D)
    features = jnp.transpose(inputs.astype(jnp.float32), (0, 2, 1))
    result, pullback = jax.vjp(forward, features, weights, biases)
    feature_grad, weight_grad, bias_grad = pullback(jnp.transpose(cotangent.astype(jnp.float32), (0, 2, 1)))
    kernel_grad = weight_grad.transpose(0, 2, 1).reshape(3, D, KB, BR).transpose(0, 2, 1, 3).reshape(NKB, D, BR)
    total = jnp.sum(kernel_grad * kernel_grad) + jnp.sum(bias_grad * bias_grad)
    grad_norm = jnp.sqrt(total)
    factor = 1.0 / jnp.maximum(grad_norm, 1.0)
    kernel_w, kernel_m, kernel_v = adam_step(kernel[kernel_slot], kernel_first[kernel_slot], kernel_second[kernel_slot], kernel_grad * factor, 0.1)
    bias_w, bias_m, bias_v = adam_step(bias_rows[bias_slot], bias_first[bias_slot], bias_second[bias_slot], bias_grad * factor, 0.0)
    return (jnp.transpose(result, (0, 2, 1)).astype(jnp.bfloat16), jnp.transpose(feature_grad, (0, 2, 1)).astype(jnp.bfloat16), placed(kernel, kernel_slot, kernel_w), placed(kernel, kernel_slot, kernel_m), placed(kernel, kernel_slot, kernel_v), placed(bias_rows, bias_slot, bias_w), placed(bias_rows, bias_slot, bias_m), placed(bias_rows, bias_slot, bias_v), grad_norm)
```

```python
import jax
import jax.numpy as jnp
from jax import lax
from jax.experimental import pallas as pl
from jax.experimental.pallas import tpu as pltpu
from jax.sharding import PartitionSpec as P

D = 2304
STEP = 10


def earlier_count(owned):
    number = owned.shape[0]
    places = jnp.arange(number, dtype=jnp.int32)
    earlier = (owned[:, None] == owned[None, :]) & (places[None, :] < places[:, None])
    return jnp.sum(earlier.astype(jnp.int32), axis=1)


def slot_sources(slot, count):
    places = jnp.arange(slot.shape[0], dtype=jnp.int32)
    hits = slot[None, :] == jnp.arange(count, dtype=jnp.int32)[:, None]
    source = jnp.sum(jnp.where(hits, places[None, :], 0), axis=1)
    return (source, jnp.any(hits, axis=1).astype(jnp.float32))


def shift_later(values):
    return jnp.pad(values, ((0, 0), (0, 0), (1, 0)))[:, :, :-1]


def shift_earlier(values):
    return jnp.pad(values, ((0, 0), (0, 0), (0, 1)))[:, :, 1:]


def combine(earlier, later):
    return (earlier[0] * later[0], later[0] * earlier[1] + later[1])


def pooled(preact, keeping):
    channels = preact.shape[1] // 3
    candidate = jnp.tanh(preact[:, :channels])
    forget = jax.nn.sigmoid(preact[:, channels : 2 * channels])
    output_gate = jax.nn.sigmoid(preact[:, 2 * channels :])
    decay = forget * keeping[:, None, :]
    _, cells = lax.associative_scan(combine, (decay, (1.0 - forget) * candidate), axis=2)
    return output_gate * cells


def adam_step(weights, first, second, grad, decay_rate):
    rate = (2.0 * D) ** (-0.5)
    first_new = 0.9 * first + 0.1 * grad
    second_new = 0.999 * second + 0.001 * grad * grad
    first_hat = first_new / (1.0 - 0.9**STEP)
    second_hat = second_new / (1.0 - 0.999**STEP)
    weights_new = weights - rate * (
        first_hat / (jnp.sqrt(second_hat) + 1e-08) + decay_rate * weights
    )
    return (weights_new, first_new, second_new)


def shards(
    inputs,
    resets,
    owners,
    kernel,
    kernel_first,
    kernel_second,
    bias_rows,
    bias_first,
    bias_second,
    cotangent,
):
    streams, local_width, length = inputs.shape
    slots_own, _, block_rows = kernel.shape
    block_count = owners.shape[0] - 3
    dp_size = lax.axis_size("dp")
    dp_index = lax.axis_index("dp")
    kernel_owner = owners[:block_count]
    bias_owner = owners[block_count:]
    kernel_slot = kernel_owner * slots_own + earlier_count(kernel_owner)
    bias_slot = bias_owner * 3 + earlier_count(bias_owner)
    all_kernel, all_bias = (
        lax.all_gather(kernel.astype(jnp.bfloat16), "dp", axis=0, tiled=True),
        lax.all_gather(bias_rows.astype(jnp.bfloat16), "dp", axis=0, tiled=True),
    )
    per_gate = block_count // 3
    double_width = per_gate * block_rows
    full_width = double_width // 2
    gate_cols = 3 * local_width
    arranged = (
        all_kernel[kernel_slot]
        .reshape(3, per_gate, local_width, block_rows)
        .transpose(0, 2, 1, 3)
        .reshape(gate_cols, double_width)
    )
    paired_t = jnp.concatenate([arranged[:, :full_width], arranged[:, full_width:]], axis=0)
    bias_vec = all_bias[bias_slot].astype(jnp.float32).reshape(gate_cols)
    rows = paired_t
    projected = jnp.einsum(
        "ok,skl->sol",
        rows,
        lax.all_gather(inputs, "mp", axis=1, tiled=True),
        preferred_element_type=jnp.float32,
    )
    preact = (
        projected[:, :gate_cols] + shift_later(projected[:, gate_cols:]) + bias_vec[None, :, None]
    )
    keeping = (1 - resets).astype(jnp.float32)
    result, pullback = jax.vjp(lambda values: pooled(values, keeping), preact)
    pre_grad = pullback(cotangent.astype(jnp.float32))[0].astype(jnp.bfloat16)
    joined = jnp.concatenate([pre_grad, shift_earlier(pre_grad)], axis=1)
    bias_grad = jnp.sum(pre_grad.astype(jnp.float32), axis=(0, 2)).reshape(3, local_width)
    pair_grad = jnp.einsum(
        "sol,skl->ok",
        joined,
        lax.all_gather(inputs, "mp", axis=1, tiled=True),
        preferred_element_type=jnp.float32,
    )
    rows = paired_t
    term_rows = lax.psum_scatter(
        jnp.einsum("ok,sol->ksl", rows, joined, preferred_element_type=jnp.float32),
        "mp",
        scatter_dimension=0,
        tiled=True,
    )
    input_grads = jnp.transpose(term_rows.astype(jnp.bfloat16), (1, 0, 2))
    block_grad = pair_grad.reshape(2, 3, local_width, full_width).transpose(1, 2, 0, 3)
    block_grad = (
        block_grad.reshape(3, local_width, per_gate, block_rows)
        .transpose(0, 2, 1, 3)
        .reshape(block_count, local_width, block_rows)
    )
    kernel_source, kernel_valid = slot_sources(kernel_slot, dp_size * slots_own)
    bias_source, bias_valid = slot_sources(bias_slot, dp_size * 3)
    own_kernel_valid = lax.dynamic_slice_in_dim(kernel_valid, dp_index * slots_own, slots_own)
    own_bias_valid = lax.dynamic_slice_in_dim(bias_valid, dp_index * 3, 3)
    total_kernel, total_bias = lax.psum((block_grad, bias_grad), "dp")
    own_kernel_source = lax.dynamic_slice_in_dim(kernel_source, dp_index * slots_own, slots_own)
    own_bias_source = lax.dynamic_slice_in_dim(bias_source, dp_index * 3, 3)
    own_kernel = total_kernel[own_kernel_source] * own_kernel_valid[:, None, None]
    own_bias = total_bias[own_bias_source] * own_bias_valid[:, None]
    squares = jnp.sum(own_kernel * own_kernel) + jnp.sum(own_bias * own_bias)
    grad_norm = jnp.sqrt(lax.psum(squares, ("dp", "mp")))
    factor = 1.0 / jnp.maximum(grad_norm, 1.0)
    kernel_w, kernel_m, kernel_v = adam_step(
        kernel, kernel_first, kernel_second, own_kernel * factor, 0.1
    )
    bias_w, bias_m, bias_v = adam_step(bias_rows, bias_first, bias_second, own_bias * factor, 0.0)
    kernel_mask = own_kernel_valid[:, None, None] > 0.5
    bias_mask = own_bias_valid[:, None] > 0.5
    return (
        result.astype(jnp.bfloat16),
        input_grads,
        jnp.where(kernel_mask, kernel_w, 0.0),
        jnp.where(kernel_mask, kernel_m, 0.0),
        jnp.where(kernel_mask, kernel_v, 0.0),
        jnp.where(bias_mask, bias_w, 0.0),
        jnp.where(bias_mask, bias_m, 0.0),
        jnp.where(bias_mask, bias_v, 0.0),
        grad_norm,
    )


MESH_ID = pl.DeviceIdType.MESH
LANES = 128
CHUNKS = 4


def place():
    dp, mp = lax.axis_index("dp"), lax.axis_index("mp")
    return dp // 2, lax.rem(dp, 2), mp // 2, lax.rem(mp, 2)


def partners(y, x, z, c):
    dp, mp = y * 2 + x, z * 2 + c
    return {
        "x": (y * 2 + 1 - x, mp),
        "y": ((1 - y) * 2 + x, mp),
        "xy": ((1 - y) * 2 + 1 - x, mp),
        "core": (dp, z * 2 + 1 - c),
        "up": (dp, mp + 2),
        "down": (dp, mp - 2),
    }


def greet(who, names, z, depth):
    barrier = pltpu.get_barrier_semaphore()
    for name in names:
        pl.semaphore_signal(barrier, inc=1, device_id=who[name], device_id_type=MESH_ID)

    @pl.when(z < depth - 1)
    def _():
        pl.semaphore_signal(barrier, inc=1, device_id=who["up"], device_id_type=MESH_ID)

    @pl.when(z > 0)
    def _():
        pl.semaphore_signal(barrier, inc=1, device_id=who["down"], device_id_type=MESH_ID)

    both = (z < depth - 1).astype(jnp.int32) + (z > 0).astype(jnp.int32)
    pl.semaphore_wait(barrier, len(names) + both)


class Sends:
    def __init__(self, sems):
        self.sems, self.number, self.made = sems, 0, []

    def start(self, src, dst, recv, device, when=None):
        slot = self.number
        self.number += 1

        def build():
            return pltpu.make_async_remote_copy(
                src_ref=src(),
                dst_ref=dst(),
                send_sem=self.sems.at[slot],
                recv_sem=recv,
                device_id=device,
                device_id_type=MESH_ID,
            )

        def go():
            build().start()

        if when is None:
            go()
        else:
            pl.when(when)(go)
        self.made.append((build, when))

    def finish(self):
        for build, when in self.made:
            if when is None:
                build().wait_send()
            else:
                pl.when(when)(lambda build=build: build().wait_send())


def landed(ref, sem, device):
    pltpu.make_async_remote_copy(
        src_ref=ref, dst_ref=ref, send_sem=sem, recv_sem=sem, device_id=device, device_id_type=MESH_ID
    ).wait_recv()


def gather_kernel(
    w_ref, x_ref, cot_ref, res_ref, bias_ref,
    wg, xg, cg, rg, bg,
    wf, wb, load_sem, own_sem, send_sem, w_sem, x_sem, c_sem, r_sem, b_sem,
):
    y, x, z, c = place()
    dp, mp = y * 2 + x, z * 2 + c
    who = partners(y, x, z, c)
    slots, width, _ = w_ref.shape
    half = width // 2
    depth = xg.shape[1] // width // 2
    rows = slots // CHUNKS

    def part(index):
        return pl.ds(pl.multiple_of(index * half, half), half)

    def rows_of(index):
        return pl.ds(pl.multiple_of(index * width, width), width)

    loads = [
        pltpu.make_async_copy(
            w_ref.at[pl.ds(i * rows, rows)], wf.at[pl.ds(i * rows, rows)], load_sem.at[i]
        )
        for i in range(CHUNKS)
    ]
    for load in loads:
        load.start()
    own = [
        pltpu.make_async_copy(x_ref, xg.at[x, rows_of(mp)], own_sem.at[0]),
        pltpu.make_async_copy(cot_ref.at[part(x)], cg.at[x], own_sem.at[1]),
        pltpu.make_async_copy(res_ref, rg.at[x], own_sem.at[2]),
        pltpu.make_async_copy(bias_ref, bg.at[dp], own_sem.at[3]),
    ]
    for copy in own:
        copy.start()
    greet(who, ("x", "y", "xy", "core"), z, depth)
    sends = Sends(send_sem)

    def spread(stream, place_z, src, up, down, core=True):
        number = place_z * 2 + c

        def dst():
            return xg.at[stream, rows_of(number)]

        recv = x_sem.at[stream, number]
        if up is not False:
            sends.start(src, dst, recv, who["up"], up)
        if down is not False:
            sends.start(src, dst, recv, who["down"], down)
        sends.start(src, dst, recv, who["core"], core)

    spread(x, z, lambda: x_ref, z < depth - 1, z > 0, None)
    sends.start(lambda: x_ref, lambda: xg.at[x, rows_of(mp)], x_sem.at[x, mp], who["x"])
    for name in ("x", "y", "xy"):
        sends.start(lambda: bias_ref, lambda: bg.at[dp], b_sem.at[dp], who[name])
    sends.start(lambda: res_ref, lambda: rg.at[x], r_sem, who["x"])
    for i in range(CHUNKS):
        loads[i].wait()

        def cast(r, _, i=i):
            wb[i * rows + r] = wf[i * rows + r].astype(jnp.bfloat16)
            return 0

        lax.fori_loop(0, rows, cast, 0)

        def dst(i=i):
            return wg.at[pl.ds(dp * slots + i * rows, rows)]

        sends.start(lambda i=i: wb.at[pl.ds(i * rows, rows), part(x)], dst, w_sem.at[dp, i], who["y"])
        sends.start(
            lambda i=i: wb.at[pl.ds(i * rows, rows), part(1 - x)], dst, w_sem.at[dp, i], who["x"]
        )
        copy = pltpu.make_async_copy(wb.at[pl.ds(i * rows, rows), part(x)], dst(), own_sem.at[4 + i])
        copy.start()
        own.append(copy)
    sends.start(lambda: cot_ref.at[part(1 - x)], lambda: cg.at[x], c_sem, who["x"])

    def along_z(stream, d):
        @pl.when(z >= d)
        def _():
            landed(xg.at[stream, rows_of((z - d) * 2 + c)], x_sem.at[stream, (z - d) * 2 + c], who["down"])

        src = lambda: xg.at[stream, rows_of((z - d) * 2 + c)]
        spread(stream, z - d, src, (z >= d) & (z < depth - 1), False, z >= d)

        @pl.when(z + d < depth)
        def _():
            landed(xg.at[stream, rows_of((z + d) * 2 + c)], x_sem.at[stream, (z + d) * 2 + c], who["up"])

        src = lambda: xg.at[stream, rows_of((z + d) * 2 + c)]
        spread(stream, z + d, src, False, (z + d < depth) & (z > 0), z + d < depth)

    def pass_on(i):
        def ref():
            return wg.at[pl.ds((y * 2 + 1 - x) * slots + i * rows, rows)]

        sem = w_sem.at[y * 2 + 1 - x, i]
        landed(ref(), sem, who["x"])
        sends.start(ref, ref, sem, who["y"])

    def other_stream():
        ref = lambda: xg.at[1 - x, rows_of(mp)]
        landed(ref(), x_sem.at[1 - x, mp], who["x"])
        spread(1 - x, z, ref, z < depth - 1, z > 0, None)

    steps = [lambda d=d: along_z(x, d) for d in range(1, depth)]
    steps += [lambda d=d: along_z(1 - x, d) for d in range(1, depth)]
    steps.insert(1, other_stream)
    after = [2, 4, 5, 7]
    for i in range(CHUNKS):
        steps.insert(min(after[i] + 1, len(steps)), lambda i=i: pass_on(i))
    for step in steps:
        step()
    for source in ((1 - y) * 2 + x, (1 - y) * 2 + 1 - x):
        for i in range(CHUNKS):
            landed(wg.at[pl.ds(source * slots + i * rows, rows)], w_sem.at[source, i], who["y"])
    for stream in (x, 1 - x):
        for k in range(depth):
            number = k * 2 + 1 - c
            landed(xg.at[stream, rows_of(number)], x_sem.at[stream, number], who["core"])
    landed(cg.at[1 - x], c_sem, who["x"])
    landed(rg.at[1 - x], r_sem, who["x"])
    for source in (y * 2 + 1 - x, (1 - y) * 2 + x, (1 - y) * 2 + 1 - x):
        landed(bg.at[source], b_sem.at[source], who["x"])
    for copy in own:
        copy.wait()
    sends.finish()


def slot_table(owners, slot, count, blocks, slots):
    for d in range(4):
        count[d] = 0

    def one(i, _):
        owner = owners[i]
        slot[i] = owner * slots + count[owner]
        count[owner] = count[owner] + 1
        return 0

    lax.fori_loop(0, blocks, one, 0)


def bias_rank(owners, blocks, g):
    owner = owners[blocks + g]
    rank = jnp.int32(0)
    for h in range(g):
        rank += (owners[blocks + h] == owner).astype(jnp.int32)
    return owner, rank


def scan_later(a, b, length):
    d = 1
    while d < length:
        b = b + a * pltpu.roll(b, d, 1)
        if 2 * d < length:
            a = a * pltpu.roll(a, d, 1)
        d *= 2
    return b


def scan_earlier(a, b, length):
    d = 1
    while d < length:
        b = b + a * pltpu.roll(b, length - d, 1)
        if 2 * d < length:
            a = a * pltpu.roll(a, length - d, 1)
        d *= 2
    return b


def layer_kernel(
    owners, wg, xg, cg, rg, bg,
    h_out, gs, j_out, w_out, bgrad,
    slot, count, wv, xv, p, joined, gb, bcol, w_sem, x_sem, o_sem,
):
    half, block_rows = wg.shape[1], wg.shape[2]
    slots = wg.shape[0] // 4
    streams, full, length = xg.shape
    per_half = full // block_rows
    blocks = 6 * per_half
    x = lax.rem(lax.axis_index("dp"), 2)
    x_loads = [pltpu.make_async_copy(xg.at[s], xv.at[s], x_sem.at[s]) for s in range(2)]
    slot_table(owners, slot, count, blocks, slots)
    for h in range(2):
        for g in range(3):

            def fetch(k, _, h=h, g=g):
                pltpu.make_async_copy(
                    wg.at[slot[g * 2 * per_half + h * per_half + k]],
                    wv.at[
                        pl.ds((h * 3 + g) * half, half),
                        pl.ds(pl.multiple_of(k * block_rows, block_rows), block_rows),
                    ],
                    w_sem,
                ).start()
                return 0

            lax.fori_loop(0, per_half, fetch, 0)
    for load in x_loads:
        load.start()
    lane_of = lax.broadcasted_iota(jnp.int32, (half, 2 * half), 1)
    row_of = lax.broadcasted_iota(jnp.int32, (half, 2 * half), 0)
    diagonal = lane_of == row_of + x * half
    for g in range(3):
        owner, rank = bias_rank(owners, blocks, g)
        held = bg[owner]
        line = jnp.zeros((1, 2 * half), jnp.float32)
        for r in range(3):
            line = jnp.where(rank == r, held[r : r + 1], line)
        line = line.astype(jnp.bfloat16).astype(jnp.float32)
        column = jnp.sum(jnp.where(diagonal, line, 0.0), axis=1, keepdims=True)
        bcol[pl.ds(g * half, half), :] = jnp.broadcast_to(column, (half, LANES))
    bgrad[...] = jnp.zeros_like(bgrad)
    pltpu.make_async_copy(wv, wv, w_sem).wait()
    w_back = pltpu.make_async_copy(wv, w_out, o_sem.at[0])
    w_back.start()
    tile = 16
    moment = lax.broadcasted_iota(jnp.int32, (tile, length), 1)
    lane = lax.broadcasted_iota(jnp.int32, (tile, LANES), 1)
    for s in range(2):
        x_loads[s].wait()

        def project(n, _, s=s):
            columns = pl.ds(pl.multiple_of(n * 256, 256), 256)
            p[:, columns] = jnp.dot(wv[...], xv[s, :, columns], preferred_element_type=jnp.float32)
            return 0

        lax.fori_loop(0, length // 256, project, 0)
        keep = 1.0 - jnp.broadcast_to(rg[s], (tile, length)).astype(jnp.float32)
        keep = jnp.where(moment == 0, 0.0, keep)

        def gates(i, _, s=s, keep=keep):
            base = pl.multiple_of(i * tile, tile)

            def pre(g):
                now = p[pl.ds(g * half + base, tile), :]
                before = pltpu.roll(p[pl.ds((3 + g) * half + base, tile), :], 1, 1)
                return (
                    now
                    + jnp.where(moment == 0, 0.0, before)
                    + bcol[pl.ds(g * half + base, tile), :][:, :1]
                )

            cand = jnp.tanh(pre(0))
            forget = jax.nn.sigmoid(pre(1))
            gate = jax.nn.sigmoid(pre(2))
            decay = forget * keep
            cells = scan_later(decay, (1.0 - forget) * cand, length)
            h_out[s, pl.ds(base, tile), :] = (gate * cells).astype(jnp.bfloat16)
            dh = cg[s, pl.ds(base, tile), :].astype(jnp.float32)
            dc = scan_earlier(pltpu.roll(decay, length - 1, 1), dh * gate, length)
            d_gate = dh * cells * gate * (1.0 - gate)
            d_cand = dc * (1.0 - forget) * (1.0 - cand * cand)
            d_forget = (
                dc * (keep * pltpu.roll(cells, 1, 1) - cand) * forget * (1.0 - forget)
            )
            total = bgrad[pl.ds(base, tile), :]
            for g, value in enumerate((d_cand, d_forget, d_gate)):
                value = value.astype(jnp.bfloat16)
                wide = value.astype(jnp.float32)
                joined[pl.ds(g * half + base, tile), pl.ds(s * length, length)] = value
                ahead = jnp.where(moment == length - 1, 0.0, pltpu.roll(wide, length - 1, 1))
                joined[pl.ds((3 + g) * half + base, tile), pl.ds(s * length, length)] = ahead.astype(
                    jnp.bfloat16
                )
                total += jnp.where(lane == g, jnp.sum(wide, axis=1, keepdims=True), 0.0)
            bgrad[pl.ds(base, tile), :] = total
            return 0

        lax.fori_loop(0, half // tile, gates, 0)
    j_back = pltpu.make_async_copy(joined, j_out, o_sem.at[1])
    j_back.start()

    def weight_grad(k, _):
        rows = pl.ds(pl.multiple_of(k * block_rows, block_rows), block_rows)
        both = (((1,), (1,)), ((), ()))
        total = lax.dot_general(
            joined[:, pl.ds(0, length)], xv[0, rows, :], both, preferred_element_type=jnp.float32
        )
        total += lax.dot_general(
            joined[:, pl.ds(length, length)], xv[1, rows, :], both, preferred_element_type=jnp.float32
        )
        gb[k] = total.astype(jnp.bfloat16)
        for h in range(2):
            for g in range(3):
                pltpu.make_async_copy(
                    gb.at[k, pl.ds((h * 3 + g) * half, half)],
                    gs.at[slot[g * 2 * per_half + h * per_half + k]],
                    w_sem,
                ).start()
        return 0

    lax.fori_loop(0, per_half, weight_grad, 0)
    pltpu.make_async_copy(gb, gb, w_sem).wait()
    w_back.wait()
    j_back.wait()


def reduce_kernel(
    owners, gs, w_hbm, j_hbm, h_in, bgrad,
    gt, h_out, ig_out, bt, norm,
    wv, jv, ig, up_got, down_got, core_got, x_got, y_got, y_own, x_give, b_got, squares, s_got,
    load_sem, own_sem, send_sem, y_sem, x_sem, core_sem, up_sem, down_sem, ix_sem, h_sem, b_sem, s_sem,
):
    y, x, z, c = place()
    who = partners(y, x, z, c)
    slots, width, block_rows = gt.shape
    half = width // 2
    length = h_out.shape[1]
    full = w_hbm.shape[1]
    depth = full // width // 2
    rows = slots // CHUNKS
    blocks = 6 * (full // block_rows)
    tile = 16

    def part(index):
        return pl.ds(pl.multiple_of(index * half, half), half)

    def rows_of(place_z, core):
        return pl.ds(pl.multiple_of((place_z * 2 + core) * width, width), width)

    loads = [
        pltpu.make_async_copy(w_hbm, wv, load_sem.at[0]),
        pltpu.make_async_copy(j_hbm, jv, load_sem.at[1]),
    ]
    for load in loads:
        load.start()
    owner_x = (1 - x, x)
    own_loads = []
    for q in range(2):
        copy = pltpu.make_async_copy(
            gs.at[pl.ds((y * 2 + owner_x[q]) * slots, slots)], y_own.at[q], load_sem.at[2 + q]
        )
        copy.start()
        own_loads.append(copy)
    h_own = pltpu.make_async_copy(h_in.at[x], h_out.at[part(x)], own_sem.at[0])
    h_own.start()
    greet_extra = jnp.bitwise_xor(z, 2) * 2 + c
    barrier = pltpu.get_barrier_semaphore()
    flip_near = (y * 2 + x, jnp.bitwise_xor(z, 1) * 2 + c)
    flip_far = (y * 2 + x, greet_extra)
    pl.semaphore_signal(barrier, inc=1, device_id=flip_near, device_id_type=MESH_ID)
    pl.semaphore_signal(barrier, inc=1, device_id=flip_far, device_id_type=MESH_ID)
    for name in ("x", "y", "core"):
        pl.semaphore_signal(barrier, inc=1, device_id=who[name], device_id_type=MESH_ID)

    @pl.when(z < depth - 1)
    def _():
        pl.semaphore_signal(barrier, inc=1, device_id=who["up"], device_id_type=MESH_ID)

    @pl.when(z > 0)
    def _():
        pl.semaphore_signal(barrier, inc=1, device_id=who["down"], device_id_type=MESH_ID)

    both = (z < depth - 1).astype(jnp.int32) + (z > 0).astype(jnp.int32)
    pl.semaphore_wait(barrier, 5 + both)

    sends = Sends(send_sem)
    sends.start(lambda: bgrad, lambda: b_got.at[0], b_sem.at[0], who["y"])
    for q in range(2):
        for i in range(CHUNKS):
            sends.start(
                lambda q=q, i=i: gs.at[
                    pl.ds(((1 - y) * 2 + owner_x[q]) * slots + i * rows, rows)
                ],
                lambda q=q, i=i: y_got.at[q, pl.ds(i * rows, rows)],
                y_sem.at[q, i],
                who["y"],
            )
    sends.start(lambda: h_in.at[1 - x], lambda: h_out.at[part(x)], h_sem, who["x"])
    for load in loads:
        load.wait()
    streams = (1 - x, x)
    for q in range(2):

        def input_grad(k, _, q=q):
            columns = pl.ds(pl.multiple_of(k * 256, 256), 256)
            lanes = pl.ds(pl.multiple_of(streams[q] * length, length), length)
            ig[q, columns, :] = lax.dot_general(
                wv[:, columns],
                jv[:, lanes],
                (((0,), (0,)), ((), ())),
                preferred_element_type=jnp.float32,
            ).astype(jnp.bfloat16)
            return 0

        lax.fori_loop(0, full // 256, input_grad, 0)
        for k in range(depth):
            sends.start(
                lambda q=q, k=k: ig.at[q, rows_of(k, 1 - c)],
                lambda q=q, k=k: core_got.at[q, k],
                core_sem.at[q, k],
                who["core"],
            )

    def add_tiles(dst, refs):
        def one(i, _):
            at = pl.ds(pl.multiple_of(i * tile, tile), tile)
            total = refs[0][at, :].astype(jnp.float32)
            for ref in refs[1:]:
                total += ref[at, :].astype(jnp.float32)
            dst[at, :] = total.astype(jnp.bfloat16)
            return 0

        lax.fori_loop(0, width // tile, one, 0)

    def chip_sum(q, k):
        landed(core_got.at[q, k], core_sem.at[q, k], who["core"])
        mine = ig.at[q, rows_of(k, c)]
        add_tiles(mine, (mine, core_got.at[q, k]))

    def z_step(q, k):
        far = depth - 1 - k

        @pl.when((z > 0) & (z < far))
        def _():
            mine = ig.at[q, rows_of(far, c)]
            landed(up_got.at[q, far], up_sem.at[q, far], who["down"])
            add_tiles(mine, (mine, up_got.at[q, far]))

        sends.start(
            lambda: ig.at[q, rows_of(far, c)],
            lambda: up_got.at[q, far],
            up_sem.at[q, far],
            who["up"],
            z < far,
        )

        @pl.when((z < depth - 1) & (z > k))
        def _():
            mine = ig.at[q, rows_of(k, c)]
            landed(down_got.at[q, k], down_sem.at[q, k], who["up"])
            add_tiles(mine, (mine, down_got.at[q, k]))

        sends.start(
            lambda: ig.at[q, rows_of(k, c)],
            lambda: down_got.at[q, k],
            down_sem.at[q, k],
            who["down"],
            z > k,
        )

    def z_last(q):
        mine = ig.at[q, rows_of(z, c)]

        @pl.when(z > 0)
        def _():
            landed(up_got.at[q, z], up_sem.at[q, z], who["down"])
            add_tiles(mine, (mine, up_got.at[q, z]))

        @pl.when(z < depth - 1)
        def _():
            landed(down_got.at[q, z], down_sem.at[q, z], who["up"])
            add_tiles(mine, (mine, down_got.at[q, z]))

        if q == 0:
            sends.start(lambda: mine, lambda: x_got, ix_sem, who["x"])

    squares[...] = jnp.zeros_like(squares)
    owned = []
    for q in range(2):
        number = jnp.int32(0)
        for j in range(blocks):
            number += (owners[j] == y * 2 + owner_x[q]).astype(jnp.int32)
        owned.append(number)

    def own_chunk(q, i):
        if i == 0:
            own_loads[q].wait()
        landed(y_got.at[q, pl.ds(i * rows, rows)], y_sem.at[q, i], who["y"])

        def one(r, _):
            valid = jnp.broadcast_to(i * rows + r < owned[q], (half, block_rows))
            total = y_own[q, i * rows + r].astype(jnp.float32) + y_got[q, i * rows + r].astype(
                jnp.float32
            )
            total = jnp.where(valid, total, 0.0)
            x_give[q, i * rows + r] = total.astype(jnp.bfloat16)
            squares[...] += jnp.sum((total * total).reshape(half // 8, 8, block_rows), axis=0)
            return 0

        lax.fori_loop(0, rows, one, 0)
        if q == 0:
            sends.start(
                lambda: x_give.at[0, pl.ds(i * rows, rows)],
                lambda: gt.at[pl.ds(i * rows, rows), part(x)],
                x_sem.at[i],
                who["x"],
            )
        else:
            copy = pltpu.make_async_copy(
                x_give.at[1, pl.ds(i * rows, rows)],
                gt.at[pl.ds(i * rows, rows), part(x)],
                own_sem.at[1 + i],
            )
            copy.start()
            own_copies.append(copy)

    own_copies = [h_own]

    def bias_sum():
        landed(b_got.at[0], b_sem.at[0], who["y"])
        total = bgrad[...] + b_got[0]
        b_got[1] = total
        bt[x] = total
        sends.start(lambda: b_got.at[1], lambda: bt.at[x], b_sem.at[1], who["x"])
        counted = jnp.broadcast_to(y == 0, (half, LANES))
        each = jnp.where(counted, total * total, 0.0)
        squares[:, pl.ds(0, LANES)] += jnp.sum(each.reshape(half // 8, 8, LANES), axis=0)

    bias_sum()
    for k in range(depth):
        chip_sum(0, k)
    z_step(0, 0)
    own_chunk(0, 0)
    for k in range(depth):
        chip_sum(1, k)
    z_step(0, 1)
    z_step(1, 0)
    own_chunk(0, 1)
    z_step(0, 2)
    z_step(1, 1)
    own_chunk(0, 2)
    z_last(0)
    own_chunk(0, 3)
    z_step(1, 2)
    own_chunk(1, 0)
    z_last(1)
    own_chunk(1, 1)
    own_chunk(1, 2)
    landed(x_got, ix_sem, who["x"])
    mine = ig.at[1, rows_of(z, c)]
    add_tiles(mine, (mine, x_got))
    copy = pltpu.make_async_copy(mine, ig_out, own_sem.at[1 + CHUNKS])
    copy.start()
    own_copies.append(copy)
    own_chunk(1, 3)
    total = squares[:, pl.ds(0, LANES)] + squares[:, pl.ds(LANES, LANES)]
    for step, device in enumerate((who["core"], flip_near, flip_far, who["x"], who["y"])):
        s_got[0, step] = total
        sends.start(
            lambda step=step: s_got.at[0, step],
            lambda step=step: s_got.at[1, step],
            s_sem.at[step],
            device,
        )
        landed(s_got.at[1, step], s_sem.at[step], device)
        total = total + s_got[1, step]
    norm[...] = jnp.broadcast_to(jnp.sqrt(jnp.sum(total, keepdims=True)), norm.shape)
    for i in range(CHUNKS):
        landed(gt.at[pl.ds(i * rows, rows), part(1 - x)], x_sem.at[i], who["x"])
    landed(h_out.at[part(1 - x)], h_sem, who["x"])
    landed(bt.at[1 - x], b_sem.at[1], who["x"])
    for copy in own_copies:
        copy.wait()
    sends.finish()


def adam_kernel(
    owners, norm, bt, bw, bm, bv, g, w, m, v,
    w_new, m_new, v_new, bw_new, bm_new, bv_new,
):
    step = pl.program_id(0)
    per_step, width, block_rows = w.shape
    half = width // 2
    blocks = owners.shape[0] - 3
    me = lax.axis_index("dp")
    number = jnp.int32(0)
    for j in range(blocks):
        number += (owners[j] == me).astype(jnp.int32)
    factor = 1.0 / jnp.maximum(norm[:1, :1], 1.0)
    for r in range(per_step):
        grad = g[r].astype(jnp.float32) * factor
        valid = jnp.broadcast_to(step * per_step + r < number, (width, block_rows))
        news = adam_step(w[r], m[r], v[r], grad, 0.1)
        for ref, new in zip((w_new, m_new, v_new), news):
            ref[r] = jnp.where(valid, new, 0.0)

    @pl.when(step == 0)
    def _():
        lane_of = lax.broadcasted_iota(jnp.int32, (half, width), 1)
        row_of = lax.broadcasted_iota(jnp.int32, (half, width), 0)
        row = lax.broadcasted_iota(jnp.int32, (3, width), 0)
        grads = jnp.zeros((3, width), jnp.float32)
        valid = jnp.zeros((3, width), jnp.int32)
        for gate in range(3):
            owner, rank = bias_rank(owners, blocks, gate)
            line = jnp.zeros((1, width), jnp.float32)
            for h in range(2):
                column = bt[h][:, gate : gate + 1]
                line += jnp.sum(
                    jnp.where(lane_of == row_of + h * half, column, 0.0), axis=0, keepdims=True
                )
            here = (row == rank) & jnp.broadcast_to(owner == me, (3, width))
            grads = jnp.where(here, line, grads)
            valid = jnp.where(here, 1, valid)
        news = adam_step(bw[...], bm[...], bv[...], grads * factor, 0.0)
        for ref, new in zip((bw_new, bm_new, bv_new), news):
            ref[...] = jnp.where(valid > 0, new, 0.0)


def paired(
    inputs, resets, owners, kernel, kernel_first, kernel_second, bias_rows, bias_first, bias_second, cotangent
):
    _, width, length = inputs.shape
    slots, _, block_rows = kernel.shape
    blocks = owners.shape[0] - 3
    full = width * lax.axis_size("mp")
    depth = lax.axis_size("mp") // 2
    half = width // 2
    bf16, f32 = jnp.bfloat16, jnp.float32
    shape = jax.ShapeDtypeStruct
    hbm = pl.BlockSpec(memory_space=pltpu.MemorySpace.HBM)
    vmem = pl.BlockSpec(memory_space=pltpu.VMEM)
    smem = pl.BlockSpec(memory_space=pltpu.SMEM)
    dma = pltpu.SemaphoreType.DMA
    wg, xg, cg, rg, bg = pl.pallas_call(
        gather_kernel,
        out_shape=(
            shape((4 * slots, half, block_rows), bf16),
            shape((2, full, length), bf16),
            shape((2, half, length), bf16),
            shape((2, 1, length), jnp.int32),
            shape((4, 3, width), f32),
        ),
        in_specs=[hbm] * 5,
        out_specs=[hbm] * 5,
        scratch_shapes=[
            pltpu.VMEM((slots, width, block_rows), f32),
            pltpu.VMEM((slots, width, block_rows), bf16),
            dma((CHUNKS,)),
            dma((4 + CHUNKS,)),
            dma((64,)),
            dma((4, CHUNKS)),
            dma((2, 2 * depth)),
            dma,
            dma,
            dma((4,)),
        ],
        compiler_params=pltpu.CompilerParams(
            collective_id=0, has_side_effects=True, vmem_limit_bytes=24 * 2**20
        ),
        name="gather",
    )(
        kernel,
        inputs.reshape(width, length),
        cotangent.reshape(width, length),
        resets,
        bias_rows,
    )
    h, gs, joined, wv, bgrad = pl.pallas_call(
        layer_kernel,
        out_shape=(
            shape((2, half, length), bf16),
            shape((4 * slots, half, block_rows), bf16),
            shape((6 * half, 2 * length), bf16),
            shape((6 * half, full), bf16),
            shape((half, LANES), f32),
        ),
        in_specs=[smem, hbm, hbm, vmem, vmem, vmem],
        out_specs=[vmem, hbm, hbm, hbm, vmem],
        scratch_shapes=[
            pltpu.SMEM((blocks,), jnp.int32),
            pltpu.SMEM((4,), jnp.int32),
            pltpu.VMEM((6 * half, full), bf16),
            pltpu.VMEM((2, full, length), bf16),
            pltpu.VMEM((6 * half, length), f32),
            pltpu.VMEM((6 * half, 2 * length), bf16),
            pltpu.VMEM((full // block_rows, 6 * half, block_rows), bf16),
            pltpu.VMEM((3 * half, LANES), f32),
            dma,
            dma((2,)),
            dma((2,)),
        ],
        compiler_params=pltpu.CompilerParams(vmem_limit_bytes=56 * 2**20),
        name="layer",
    )(owners, wg, xg, cg, rg, bg)
    gt, h_new, ig, bt, norm = pl.pallas_call(
        reduce_kernel,
        out_shape=(
            shape((slots, width, block_rows), bf16),
            shape((width, length), bf16),
            shape((width, length), bf16),
            shape((2, half, LANES), f32),
            shape((8, LANES), f32),
        ),
        in_specs=[smem, hbm, hbm, hbm, hbm, vmem],
        out_specs=[hbm, hbm, hbm, vmem, vmem],
        scratch_shapes=[
            pltpu.VMEM((6 * half, full), bf16),
            pltpu.VMEM((6 * half, 2 * length), bf16),
            pltpu.VMEM((2, full, length), bf16),
            pltpu.VMEM((2, depth, width, length), bf16),
            pltpu.VMEM((2, depth, width, length), bf16),
            pltpu.VMEM((2, depth, width, length), bf16),
            pltpu.VMEM((width, length), bf16),
            pltpu.VMEM((2, slots, half, block_rows), bf16),
            pltpu.VMEM((2, slots, half, block_rows), bf16),
            pltpu.VMEM((2, slots, half, block_rows), bf16),
            pltpu.VMEM((2, half, LANES), f32),
            pltpu.VMEM((8, block_rows), f32),
            pltpu.VMEM((2, 5, 8, LANES), f32),
            dma((4,)),
            dma((2 + CHUNKS,)),
            dma((64,)),
            dma((2, CHUNKS)),
            dma((CHUNKS,)),
            dma((2, depth)),
            dma((2, depth)),
            dma((2, depth)),
            dma,
            dma,
            dma((2,)),
            dma((5,)),
        ],
        compiler_params=pltpu.CompilerParams(
            collective_id=1, has_side_effects=True, vmem_limit_bytes=61 * 2**20
        ),
        name="reduce",
    )(owners, gs, wv, joined, h, bgrad)
    per_step = 2
    block = pl.BlockSpec((per_step, width, block_rows), lambda i: (i, 0, 0))
    whole = lambda *dims: pl.BlockSpec(dims, lambda i: (0,) * len(dims))
    news = pl.pallas_call(
        adam_kernel,
        grid=(slots // per_step,),
        out_shape=(shape(kernel.shape, f32),) * 3 + (shape(bias_rows.shape, f32),) * 3,
        in_specs=[smem, whole(8, LANES), whole(2, half, LANES)]
        + [whole(*bias_rows.shape)] * 3
        + [block] * 4,
        out_specs=[block] * 3 + [whole(*bias_rows.shape)] * 3,
        compiler_params=pltpu.CompilerParams(vmem_limit_bytes=32 * 2**20),
        name="adam",
    )(owners, norm, bt, bias_rows, bias_first, bias_second, gt, kernel, kernel_first, kernel_second)
    kernel_w, kernel_m, kernel_v, bias_w, bias_m, bias_v = news
    return (h_new[None], ig[None], kernel_w, kernel_m, kernel_v, bias_w, bias_m, bias_v, norm[0, 0])


def solution(mesh):
    placed = (
        P("dp", "mp", None),
        P("dp", None),
        P(),
        P("dp", "mp", None),
        P("dp", "mp", None),
        P("dp", "mp", None),
        P("dp", "mp"),
        P("dp", "mp"),
        P("dp", "mp"),
        P("dp", "mp", None),
    )
    fits = mesh.shape["dp"] == 4 and mesh.shape["mp"] == 8
    return jax.shard_map(
        paired if fits else shards,
        mesh=mesh,
        in_specs=placed,
        out_specs=(
            P("dp", "mp", None),
            P("dp", "mp", None),
            P("dp", "mp", None),
            P("dp", "mp", None),
            P("dp", "mp", None),
            P("dp", "mp"),
            P("dp", "mp"),
            P("dp", "mp"),
            P(),
        ),
        check_vma=False,
    )
```

```python
import jax
import jax.numpy as jnp
from jax import lax
from jax.experimental import pallas as pl
from jax.experimental.pallas import tpu as pltpu
from jax.sharding import PartitionSpec as P

D = 2304
STEP = 10


def earlier_count(owned):
    number = owned.shape[0]
    places = jnp.arange(number, dtype=jnp.int32)
    earlier = (owned[:, None] == owned[None, :]) & (places[None, :] < places[:, None])
    return jnp.sum(earlier.astype(jnp.int32), axis=1)


def slot_sources(slot, count):
    places = jnp.arange(slot.shape[0], dtype=jnp.int32)
    hits = slot[None, :] == jnp.arange(count, dtype=jnp.int32)[:, None]
    source = jnp.sum(jnp.where(hits, places[None, :], 0), axis=1)
    return (source, jnp.any(hits, axis=1).astype(jnp.float32))


def shift_later(values):
    return jnp.pad(values, ((0, 0), (0, 0), (1, 0)))[:, :, :-1]


def shift_earlier(values):
    return jnp.pad(values, ((0, 0), (0, 0), (0, 1)))[:, :, 1:]


def combine(earlier, later):
    return (earlier[0] * later[0], later[0] * earlier[1] + later[1])


def pooled(preact, keeping):
    channels = preact.shape[1] // 3
    candidate = jnp.tanh(preact[:, :channels])
    forget = jax.nn.sigmoid(preact[:, channels : 2 * channels])
    output_gate = jax.nn.sigmoid(preact[:, 2 * channels :])
    decay = forget * keeping[:, None, :]
    _, cells = lax.associative_scan(combine, (decay, (1.0 - forget) * candidate), axis=2)
    return output_gate * cells


def adam_step(weights, first, second, grad, decay_rate):
    rate = (2.0 * D) ** (-0.5)
    first_new = 0.9 * first + 0.1 * grad
    second_new = 0.999 * second + 0.001 * grad * grad
    first_hat = first_new / (1.0 - 0.9**STEP)
    second_hat = second_new / (1.0 - 0.999**STEP)
    weights_new = weights - rate * (
        first_hat / (jnp.sqrt(second_hat) + 1e-08) + decay_rate * weights
    )
    return (weights_new, first_new, second_new)


def shards(
    inputs,
    resets,
    owners,
    kernel,
    kernel_first,
    kernel_second,
    bias_rows,
    bias_first,
    bias_second,
    cotangent,
):
    streams, local_width, length = inputs.shape
    slots_own, _, block_rows = kernel.shape
    block_count = owners.shape[0] - 3
    dp_size = lax.axis_size("dp")
    dp_index = lax.axis_index("dp")
    kernel_owner = owners[:block_count]
    bias_owner = owners[block_count:]
    kernel_slot = kernel_owner * slots_own + earlier_count(kernel_owner)
    bias_slot = bias_owner * 3 + earlier_count(bias_owner)
    all_kernel, all_bias = (
        lax.all_gather(kernel.astype(jnp.bfloat16), "dp", axis=0, tiled=True),
        lax.all_gather(bias_rows.astype(jnp.bfloat16), "dp", axis=0, tiled=True),
    )
    per_gate = block_count // 3
    double_width = per_gate * block_rows
    full_width = double_width // 2
    gate_cols = 3 * local_width
    arranged = (
        all_kernel[kernel_slot]
        .reshape(3, per_gate, local_width, block_rows)
        .transpose(0, 2, 1, 3)
        .reshape(gate_cols, double_width)
    )
    paired_t = jnp.concatenate([arranged[:, :full_width], arranged[:, full_width:]], axis=0)
    bias_vec = all_bias[bias_slot].astype(jnp.float32).reshape(gate_cols)
    rows = paired_t
    projected = jnp.einsum(
        "ok,skl->sol",
        rows,
        lax.all_gather(inputs, "mp", axis=1, tiled=True),
        preferred_element_type=jnp.float32,
    )
    preact = (
        projected[:, :gate_cols] + shift_later(projected[:, gate_cols:]) + bias_vec[None, :, None]
    )
    keeping = (1 - resets).astype(jnp.float32)
    result, pullback = jax.vjp(lambda values: pooled(values, keeping), preact)
    pre_grad = pullback(cotangent.astype(jnp.float32))[0].astype(jnp.bfloat16)
    joined = jnp.concatenate([pre_grad, shift_earlier(pre_grad)], axis=1)
    bias_grad = jnp.sum(pre_grad.astype(jnp.float32), axis=(0, 2)).reshape(3, local_width)
    pair_grad = jnp.einsum(
        "sol,skl->ok",
        joined,
        lax.all_gather(inputs, "mp", axis=1, tiled=True),
        preferred_element_type=jnp.float32,
    )
    rows = paired_t
    term_rows = lax.psum_scatter(
        jnp.einsum("ok,sol->ksl", rows, joined, preferred_element_type=jnp.float32),
        "mp",
        scatter_dimension=0,
        tiled=True,
    )
    input_grads = jnp.transpose(term_rows.astype(jnp.bfloat16), (1, 0, 2))
    block_grad = pair_grad.reshape(2, 3, local_width, full_width).transpose(1, 2, 0, 3)
    block_grad = (
        block_grad.reshape(3, local_width, per_gate, block_rows)
        .transpose(0, 2, 1, 3)
        .reshape(block_count, local_width, block_rows)
    )
    kernel_source, kernel_valid = slot_sources(kernel_slot, dp_size * slots_own)
    bias_source, bias_valid = slot_sources(bias_slot, dp_size * 3)
    own_kernel_valid = lax.dynamic_slice_in_dim(kernel_valid, dp_index * slots_own, slots_own)
    own_bias_valid = lax.dynamic_slice_in_dim(bias_valid, dp_index * 3, 3)
    total_kernel, total_bias = lax.psum((block_grad, bias_grad), "dp")
    own_kernel_source = lax.dynamic_slice_in_dim(kernel_source, dp_index * slots_own, slots_own)
    own_bias_source = lax.dynamic_slice_in_dim(bias_source, dp_index * 3, 3)
    own_kernel = total_kernel[own_kernel_source] * own_kernel_valid[:, None, None]
    own_bias = total_bias[own_bias_source] * own_bias_valid[:, None]
    squares = jnp.sum(own_kernel * own_kernel) + jnp.sum(own_bias * own_bias)
    grad_norm = jnp.sqrt(lax.psum(squares, ("dp", "mp")))
    factor = 1.0 / jnp.maximum(grad_norm, 1.0)
    kernel_w, kernel_m, kernel_v = adam_step(
        kernel, kernel_first, kernel_second, own_kernel * factor, 0.1
    )
    bias_w, bias_m, bias_v = adam_step(bias_rows, bias_first, bias_second, own_bias * factor, 0.0)
    kernel_mask = own_kernel_valid[:, None, None] > 0.5
    bias_mask = own_bias_valid[:, None] > 0.5
    return (
        result.astype(jnp.bfloat16),
        input_grads,
        jnp.where(kernel_mask, kernel_w, 0.0),
        jnp.where(kernel_mask, kernel_m, 0.0),
        jnp.where(kernel_mask, kernel_v, 0.0),
        jnp.where(bias_mask, bias_w, 0.0),
        jnp.where(bias_mask, bias_m, 0.0),
        jnp.where(bias_mask, bias_v, 0.0),
        grad_norm,
    )


MESH_ID = pl.DeviceIdType.MESH
LANES = 128
CHUNKS = 4
PIECES = 3
VMEM = 61 * 2**20


def place():
    dp, mp = lax.axis_index("dp"), lax.axis_index("mp")
    return dp // 2, lax.rem(dp, 2), mp // 2, lax.rem(mp, 2)


def partners(y, x, z, c):
    dp, mp = y * 2 + x, z * 2 + c
    return {
        "x": (y * 2 + 1 - x, mp),
        "y": ((1 - y) * 2 + x, mp),
        "xy": ((1 - y) * 2 + 1 - x, mp),
        "core": (dp, z * 2 + 1 - c),
        "up": (dp, mp + 2),
        "down": (dp, mp - 2),
    }


def greet(who, names, z, depth, more=0):
    barrier = pltpu.get_barrier_semaphore()
    for name in names:
        pl.semaphore_signal(barrier, inc=1, device_id=who[name], device_id_type=MESH_ID)

    @pl.when(z < depth - 1)
    def _():
        pl.semaphore_signal(barrier, inc=1, device_id=who["up"], device_id_type=MESH_ID)

    @pl.when(z > 0)
    def _():
        pl.semaphore_signal(barrier, inc=1, device_id=who["down"], device_id_type=MESH_ID)

    both = (z < depth - 1).astype(jnp.int32) + (z > 0).astype(jnp.int32)
    pl.semaphore_wait(barrier, len(names) + more + both)


class Sends:
    def __init__(self, sems):
        self.sems, self.number, self.made = sems, 0, []

    def start(self, src, dst, recv, device, when=None):
        slot = self.number
        self.number += 1

        def build():
            return pltpu.make_async_remote_copy(
                src_ref=src(),
                dst_ref=dst(),
                send_sem=self.sems.at[slot],
                recv_sem=recv,
                device_id=device,
                device_id_type=MESH_ID,
            )

        def go():
            build().start()

        if when is None:
            go()
        else:
            pl.when(when)(go)
        self.made.append((build, when))

    def finish(self):
        for build, when in self.made:
            if when is None:
                build().wait_send()
            else:
                pl.when(when)(lambda build=build: build().wait_send())


def landed(ref, sem, device):
    pltpu.make_async_remote_copy(
        src_ref=ref, dst_ref=ref, send_sem=sem, recv_sem=sem, device_id=device, device_id_type=MESH_ID
    ).wait_recv()


def gather_kernel(
    w_ref, x_ref, cot_ref, res_ref, bias_ref,
    wg, xg, cg, rg, bg,
    wf, wb, load_sem, own_sem, send_sem, w_sem, x_sem, c_sem, r_sem, b_sem,
):
    y, x, z, c = place()
    dp, mp = y * 2 + x, z * 2 + c
    who = partners(y, x, z, c)
    slots, width, _ = w_ref.shape
    half = width // 2
    depth = xg.shape[1] // width // 2
    rows = slots // CHUNKS

    def part(index):
        return pl.ds(pl.multiple_of(index * half, half), half)

    def rows_of(index):
        return pl.ds(pl.multiple_of(index * width, width), width)

    loads = [
        pltpu.make_async_copy(
            w_ref.at[pl.ds(i * rows, rows)], wf.at[pl.ds(i * rows, rows)], load_sem.at[i]
        )
        for i in range(CHUNKS)
    ]
    for load in loads:
        load.start()
    own = [
        pltpu.make_async_copy(x_ref, xg.at[x, rows_of(mp)], own_sem.at[0]),
        pltpu.make_async_copy(cot_ref.at[part(x)], cg.at[x], own_sem.at[1]),
        pltpu.make_async_copy(res_ref, rg.at[x], own_sem.at[2]),
        pltpu.make_async_copy(bias_ref, bg.at[dp], own_sem.at[3]),
    ]
    for copy in own:
        copy.start()
    greet(who, ("x", "y", "xy", "core"), z, depth)
    sends = Sends(send_sem)

    def spread(stream, place_z, src, up, down, core=True):
        number = place_z * 2 + c

        def dst():
            return xg.at[stream, rows_of(number)]

        recv = x_sem.at[stream, number]
        if up is not False:
            sends.start(src, dst, recv, who["up"], up)
        if down is not False:
            sends.start(src, dst, recv, who["down"], down)
        sends.start(src, dst, recv, who["core"], core)

    spread(x, z, lambda: x_ref, z < depth - 1, z > 0, None)
    sends.start(lambda: x_ref, lambda: xg.at[x, rows_of(mp)], x_sem.at[x, mp], who["x"])
    for name in ("x", "y", "xy"):
        sends.start(lambda: bias_ref, lambda: bg.at[dp], b_sem.at[dp], who[name])
    sends.start(lambda: res_ref, lambda: rg.at[x], r_sem, who["x"])
    for i in range(CHUNKS):
        loads[i].wait()

        def cast(r, _, i=i):
            wb[i * rows + r] = wf[i * rows + r].astype(jnp.bfloat16)
            return 0

        lax.fori_loop(0, rows, cast, 0)

        def dst(i=i):
            return wg.at[pl.ds(dp * slots + i * rows, rows)]

        sends.start(lambda i=i: wb.at[pl.ds(i * rows, rows), part(x)], dst, w_sem.at[dp, i], who["y"])
        sends.start(
            lambda i=i: wb.at[pl.ds(i * rows, rows), part(1 - x)], dst, w_sem.at[dp, i], who["x"]
        )
        copy = pltpu.make_async_copy(wb.at[pl.ds(i * rows, rows), part(x)], dst(), own_sem.at[4 + i])
        copy.start()
        own.append(copy)
    sends.start(lambda: cot_ref.at[part(1 - x)], lambda: cg.at[x], c_sem, who["x"])

    def along_z(stream, d):
        @pl.when(z >= d)
        def _():
            landed(xg.at[stream, rows_of((z - d) * 2 + c)], x_sem.at[stream, (z - d) * 2 + c], who["down"])

        src = lambda: xg.at[stream, rows_of((z - d) * 2 + c)]
        spread(stream, z - d, src, (z >= d) & (z < depth - 1), False, z >= d)

        @pl.when(z + d < depth)
        def _():
            landed(xg.at[stream, rows_of((z + d) * 2 + c)], x_sem.at[stream, (z + d) * 2 + c], who["up"])

        src = lambda: xg.at[stream, rows_of((z + d) * 2 + c)]
        spread(stream, z + d, src, False, (z + d < depth) & (z > 0), z + d < depth)

    def pass_on(i):
        def ref():
            return wg.at[pl.ds((y * 2 + 1 - x) * slots + i * rows, rows)]

        sem = w_sem.at[y * 2 + 1 - x, i]
        landed(ref(), sem, who["x"])
        sends.start(ref, ref, sem, who["y"])

    def other_stream():
        ref = lambda: xg.at[1 - x, rows_of(mp)]
        landed(ref(), x_sem.at[1 - x, mp], who["x"])
        spread(1 - x, z, ref, z < depth - 1, z > 0, None)

    steps = [lambda d=d: along_z(x, d) for d in range(1, depth)]
    steps += [lambda d=d: along_z(1 - x, d) for d in range(1, depth)]
    steps.insert(1, other_stream)
    after = [2, 4, 5, 7]
    for i in range(CHUNKS):
        steps.insert(min(after[i] + 1, len(steps)), lambda i=i: pass_on(i))
    for step in steps:
        step()
    for source in ((1 - y) * 2 + x, (1 - y) * 2 + 1 - x):
        for i in range(CHUNKS):
            landed(wg.at[pl.ds(source * slots + i * rows, rows)], w_sem.at[source, i], who["y"])
    for stream in (x, 1 - x):
        for k in range(depth):
            number = k * 2 + 1 - c
            landed(xg.at[stream, rows_of(number)], x_sem.at[stream, number], who["core"])
    landed(cg.at[1 - x], c_sem, who["x"])
    landed(rg.at[1 - x], r_sem, who["x"])
    for source in (y * 2 + 1 - x, (1 - y) * 2 + x, (1 - y) * 2 + 1 - x):
        landed(bg.at[source], b_sem.at[source], who["x"])
    for copy in own:
        copy.wait()
    sends.finish()


def slot_table(owners, slot, count, blocks, slots):
    for d in range(4):
        count[d] = 0

    def one(i, _):
        owner = owners[i]
        slot[i] = owner * slots + count[owner]
        count[owner] = count[owner] + 1
        return 0

    lax.fori_loop(0, blocks, one, 0)


def bias_rank(owners, blocks, g):
    owner = owners[blocks + g]
    rank = jnp.int32(0)
    for h in range(g):
        rank += (owners[blocks + h] == owner).astype(jnp.int32)
    return owner, rank


def scan_later(a, b, length):
    d = 1
    while d < length:
        b = b + a * pltpu.roll(b, d, 1)
        if 2 * d < length:
            a = a * pltpu.roll(a, d, 1)
        d *= 2
    return b


def scan_earlier(a, b, length):
    d = 1
    while d < length:
        b = b + a * pltpu.roll(b, length - d, 1)
        if 2 * d < length:
            a = a * pltpu.roll(a, length - d, 1)
        d *= 2
    return b


def layer_kernel(
    owners, wg, xg, cg, rg, bg,
    h_out, gs, j_out, w_out, bgrad,
    slot, count, wv, xv, p, joined, gb, bcol, w_sem, x_sem, o_sem,
):
    half, block_rows = wg.shape[1], wg.shape[2]
    slots = wg.shape[0] // 4
    streams, full, length = xg.shape
    per_half = full // block_rows
    blocks = 6 * per_half
    x = lax.rem(lax.axis_index("dp"), 2)
    x_loads = [pltpu.make_async_copy(xg.at[s], xv.at[s], x_sem.at[s]) for s in range(2)]
    slot_table(owners, slot, count, blocks, slots)
    for h in range(2):
        for g in range(3):

            def fetch(k, _, h=h, g=g):
                pltpu.make_async_copy(
                    wg.at[slot[g * 2 * per_half + h * per_half + k]],
                    wv.at[
                        pl.ds((h * 3 + g) * half, half),
                        pl.ds(pl.multiple_of(k * block_rows, block_rows), block_rows),
                    ],
                    w_sem,
                ).start()
                return 0

            lax.fori_loop(0, per_half, fetch, 0)
    for load in x_loads:
        load.start()
    lane_of = lax.broadcasted_iota(jnp.int32, (half, 2 * half), 1)
    row_of = lax.broadcasted_iota(jnp.int32, (half, 2 * half), 0)
    diagonal = lane_of == row_of + x * half
    for g in range(3):
        owner, rank = bias_rank(owners, blocks, g)
        held = bg[owner]
        line = jnp.zeros((1, 2 * half), jnp.float32)
        for r in range(3):
            line = jnp.where(rank == r, held[r : r + 1], line)
        line = line.astype(jnp.bfloat16).astype(jnp.float32)
        column = jnp.sum(jnp.where(diagonal, line, 0.0), axis=1, keepdims=True)
        bcol[pl.ds(g * half, half), :] = jnp.broadcast_to(column, (half, LANES))
    bgrad[...] = jnp.zeros_like(bgrad)
    pltpu.make_async_copy(wv, wv, w_sem).wait()
    w_back = pltpu.make_async_copy(wv, w_out, o_sem.at[0])
    w_back.start()
    tile = 16
    moment = lax.broadcasted_iota(jnp.int32, (tile, length), 1)
    lane = lax.broadcasted_iota(jnp.int32, (tile, LANES), 1)
    for s in range(2):
        x_loads[s].wait()

        def project(n, _, s=s):
            columns = pl.ds(pl.multiple_of(n * 256, 256), 256)
            p[:, columns] = jnp.dot(wv[...], xv[s, :, columns], preferred_element_type=jnp.float32)
            return 0

        lax.fori_loop(0, length // 256, project, 0)
        keep = 1.0 - jnp.broadcast_to(rg[s], (tile, length)).astype(jnp.float32)
        keep = jnp.where(moment == 0, 0.0, keep)

        def gates(i, _, s=s, keep=keep):
            base = pl.multiple_of(i * tile, tile)

            def pre(g):
                now = p[pl.ds(g * half + base, tile), :]
                before = pltpu.roll(p[pl.ds((3 + g) * half + base, tile), :], 1, 1)
                return (
                    now
                    + jnp.where(moment == 0, 0.0, before)
                    + bcol[pl.ds(g * half + base, tile), :][:, :1]
                )

            cand = jnp.tanh(pre(0))
            forget = jax.nn.sigmoid(pre(1))
            gate = jax.nn.sigmoid(pre(2))
            decay = forget * keep
            cells = scan_later(decay, (1.0 - forget) * cand, length)
            h_out[s, pl.ds(base, tile), :] = (gate * cells).astype(jnp.bfloat16)
            dh = cg[s, pl.ds(base, tile), :].astype(jnp.float32)
            dc = scan_earlier(pltpu.roll(decay, length - 1, 1), dh * gate, length)
            d_gate = dh * cells * gate * (1.0 - gate)
            d_cand = dc * (1.0 - forget) * (1.0 - cand * cand)
            d_forget = (
                dc * (keep * pltpu.roll(cells, 1, 1) - cand) * forget * (1.0 - forget)
            )
            total = bgrad[pl.ds(base, tile), :]
            for g, value in enumerate((d_cand, d_forget, d_gate)):
                value = value.astype(jnp.bfloat16)
                wide = value.astype(jnp.float32)
                joined[pl.ds(g * half + base, tile), pl.ds(s * length, length)] = value
                ahead = jnp.where(moment == length - 1, 0.0, pltpu.roll(wide, length - 1, 1))
                joined[pl.ds((3 + g) * half + base, tile), pl.ds(s * length, length)] = ahead.astype(
                    jnp.bfloat16
                )
                total += jnp.where(lane == g, jnp.sum(wide, axis=1, keepdims=True), 0.0)
            bgrad[pl.ds(base, tile), :] = total
            return 0

        lax.fori_loop(0, half // tile, gates, 0)
    j_back = pltpu.make_async_copy(joined, j_out, o_sem.at[1])
    j_back.start()

    def weight_grad(k, _):
        rows = pl.ds(pl.multiple_of(k * block_rows, block_rows), block_rows)
        both = (((1,), (1,)), ((), ()))
        total = lax.dot_general(
            joined[:, pl.ds(0, length)], xv[0, rows, :], both, preferred_element_type=jnp.float32
        )
        total += lax.dot_general(
            joined[:, pl.ds(length, length)], xv[1, rows, :], both, preferred_element_type=jnp.float32
        )
        gb[k] = total.astype(jnp.bfloat16)
        for h in range(2):
            for g in range(3):
                pltpu.make_async_copy(
                    gb.at[k, pl.ds((h * 3 + g) * half, half)],
                    gs.at[slot[g * 2 * per_half + h * per_half + k]],
                    w_sem,
                ).start()
        return 0

    lax.fori_loop(0, per_half, weight_grad, 0)
    pltpu.make_async_copy(gb, gb, w_sem).wait()
    w_back.wait()
    j_back.wait()


def reduce_kernel(
    owners, gs, w_hbm, j_hbm, h_in, bgrad,
    gt, h_out, ig_out, bt, norm,
    wv, jv, ig, up_got, down_got, core_got, x_got, y_got, y_own, b_got, squares, s_got,
    load_sem, own_sem, send_sem, y_sem, x_sem, core_sem, up_sem, down_sem, z_send, ix_sem, h_sem, b_sem, s_sem,
):
    y, x, z, c = place()
    who = partners(y, x, z, c)
    slots, width, block_rows = gt.shape
    half = width // 2
    length = h_out.shape[1]
    full = w_hbm.shape[1]
    depth = full // width // 2
    rows = slots // PIECES
    blocks = 6 * (full // block_rows)
    tile = 16
    streams = (1 - x, x)

    def part(index):
        return pl.ds(pl.multiple_of(index * half, half), half)

    def rows_of(place_z, core):
        return pl.ds(pl.multiple_of((place_z * 2 + core) * width, width), width)

    loads = [
        pltpu.make_async_copy(w_hbm, wv, load_sem.at[0]),
        pltpu.make_async_copy(j_hbm, jv, load_sem.at[1]),
    ]
    for load in loads:
        load.start()
    own_loads = []
    for q in range(2):
        copy = pltpu.make_async_copy(
            gs.at[pl.ds((y * 2 + streams[q]) * slots, slots)], y_own.at[q], load_sem.at[2 + q]
        )
        copy.start()
        own_loads.append(copy)
    h_own = pltpu.make_async_copy(h_in.at[x], h_out.at[part(x)], own_sem.at[0])
    h_own.start()
    near = (y * 2 + x, jnp.bitwise_xor(z, 1) * 2 + c)
    far_off = (y * 2 + x, jnp.bitwise_xor(z, 2) * 2 + c)
    barrier = pltpu.get_barrier_semaphore()
    for device in (near, far_off):
        pl.semaphore_signal(barrier, inc=1, device_id=device, device_id_type=MESH_ID)
    greet(who, ("x", "y", "core"), z, depth, 2)

    sends = Sends(send_sem)

    def y_send(t):
        q, i = t // PIECES, t % PIECES
        sends.start(
            lambda: gs.at[pl.ds(((1 - y) * 2 + streams[q]) * slots + i * rows, rows)],
            lambda: y_got.at[q, pl.ds(i * rows, rows)],
            y_sem.at[q, i],
            who["y"],
        )

    y_send(0)
    y_send(1)
    sends.start(lambda: bgrad, lambda: b_got.at[0], b_sem.at[0], who["y"])
    sends.start(lambda: h_in.at[1 - x], lambda: h_out.at[part(x)], h_sem, who["x"])
    for load in loads:
        load.wait()

    def input_grad(q):
        def one(k, _):
            columns = pl.ds(pl.multiple_of(k * 256, 256), 256)
            lanes = pl.ds(pl.multiple_of(streams[q] * length, length), length)
            ig[q, columns, :] = lax.dot_general(
                wv[:, columns],
                jv[:, lanes],
                (((0,), (0,)), ((), ())),
                preferred_element_type=jnp.float32,
            ).astype(jnp.bfloat16)
            return 0

        lax.fori_loop(0, full // 256, one, 0)
        for k in range(depth):
            sends.start(
                lambda k=k: ig.at[q, rows_of(k, 1 - c)],
                lambda k=k: core_got.at[q, k],
                core_sem.at[q, k],
                who["core"],
            )

    def add_tiles(refs):
        def one(i, _):
            at = pl.ds(pl.multiple_of(i * tile, tile), tile)
            total = refs[0][at, :].astype(jnp.float32)
            for ref in refs[1:]:
                total += ref[at, :].astype(jnp.float32)
            refs[0][at, :] = total.astype(jnp.bfloat16)
            return 0

        lax.fori_loop(0, width // tile, one, 0)

    def z_send_of(q, dest, got, recv, device, sem):
        return pltpu.make_async_remote_copy(
            src_ref=ig.at[q, rows_of(dest, c)],
            dst_ref=got.at[q, dest],
            send_sem=sem,
            recv_sem=recv.at[q, dest],
            device_id=device,
            device_id_type=MESH_ID,
        )

    def z_tick(t):
        hops = depth - 1
        for index, (after, got, recv, source, target) in enumerate(
            (
                (z, up_got, up_sem, who["down"], who["up"]),
                (depth - 1 - z, down_got, down_sem, who["up"], who["down"]),
            )
        ):
            item = t - after
            k = lax.rem(jnp.maximum(item, 0), hops)
            q = jnp.maximum(item, 0) // hops
            dest = depth - 1 - k if index == 0 else k
            on = (item >= 0) & (after < depth - 1 - k)

            @pl.when(on)
            def _(index=index, after=after, got=got, recv=recv, source=source, target=target, item=item, q=q, dest=dest):
                landed(core_got.at[q, dest], core_sem.at[q, dest], who["core"])
                mine = ig.at[q, rows_of(dest, c)]

                @pl.when(after == 0)
                def _():
                    add_tiles((mine, core_got.at[q, dest]))

                @pl.when(after > 0)
                def _():
                    landed(got.at[q, dest], recv.at[q, dest], source)
                    add_tiles((mine, core_got.at[q, dest], got.at[q, dest]))

                send = z_send_of(q, dest, got, recv, target, z_send.at[index])

                @pl.when(item > 0)
                def _():
                    send.wait_send()

                send.start()

    def z_last(q):
        landed(core_got.at[q, z], core_sem.at[q, z], who["core"])
        extra = (core_got.at[q, z],)
        if q == 1:
            landed(x_got, ix_sem, who["x"])
            extra += (x_got,)
        mine = ig.at[q, rows_of(z, c)]

        @pl.when(z > 0)
        def _():
            landed(up_got.at[q, z], up_sem.at[q, z], who["down"])

        @pl.when(z < depth - 1)
        def _():
            landed(down_got.at[q, z], down_sem.at[q, z], who["up"])

        @pl.when(z == 0)
        def _():
            add_tiles((mine, *extra, down_got.at[q, z]))

        @pl.when(z == depth - 1)
        def _():
            add_tiles((mine, *extra, up_got.at[q, z]))

        @pl.when((z > 0) & (z < depth - 1))
        def _():
            add_tiles((mine, *extra, up_got.at[q, z], down_got.at[q, z]))

        if q == 0:
            sends.start(lambda: mine, lambda: x_got, ix_sem, who["x"])
        else:
            copy = pltpu.make_async_copy(mine, ig_out, own_sem.at[1])
            copy.start()
            own_copies.append(copy)

    squares[...] = jnp.zeros_like(squares)
    owned = []
    for q in range(2):
        number = jnp.int32(0)
        for j in range(blocks):
            number += (owners[j] == y * 2 + streams[q]).astype(jnp.int32)
        owned.append(number)
    own_copies = [h_own]

    def own_chunk(t):
        q, i = t // PIECES, t % PIECES
        if i == 0:
            own_loads[q].wait()
        landed(y_got.at[q, pl.ds(i * rows, rows)], y_sem.at[q, i], who["y"])
        if t + 2 < 2 * PIECES:
            y_send(t + 2)

        def one(r, _):
            valid = jnp.broadcast_to(i * rows + r < owned[q], (half, block_rows))
            total = y_own[q, i * rows + r].astype(jnp.float32) + y_got[q, i * rows + r].astype(
                jnp.float32
            )
            total = jnp.where(valid, total, 0.0)
            y_own[q, i * rows + r] = total.astype(jnp.bfloat16)
            squares[...] += jnp.sum((total * total).reshape(half // 8, 8, block_rows), axis=0)
            return 0

        lax.fori_loop(0, rows, one, 0)
        src = lambda: y_own.at[q, pl.ds(i * rows, rows)]
        dst = lambda: gt.at[pl.ds(i * rows, rows), part(x)]
        if q == 0:
            sends.start(src, dst, x_sem.at[i], who["x"])
        else:
            copy = pltpu.make_async_copy(src(), dst(), own_sem.at[2 + i])
            copy.start()
            own_copies.append(copy)

    def bias_sum():
        landed(b_got.at[0], b_sem.at[0], who["y"])
        total = bgrad[...] + b_got[0]
        b_got[1] = total
        bt[x] = total
        sends.start(lambda: b_got.at[1], lambda: bt.at[x], b_sem.at[1], who["x"])
        counted = jnp.broadcast_to(y == 0, (half, LANES))
        each = jnp.where(counted, total * total, 0.0)
        squares[:, pl.ds(0, LANES)] += jnp.sum(each.reshape(half // 8, 8, LANES), axis=0)

    input_grad(0)
    ticks = 2 * (depth - 1)
    z_tick(0)
    input_grad(1)
    chunks = 2 * PIECES
    done = 0
    for t in range(1, ticks + 1):
        upto = chunks * t // ticks
        if t == ticks:
            upto = chunks - 1
        for i in range(done, upto):
            own_chunk(i)
        done = upto
        if t == 1:
            bias_sum()
        if t < ticks:
            z_tick(t)
        if t == depth - 1:
            z_last(0)
    own_chunk(chunks - 1)
    total = squares[:, pl.ds(0, LANES)] + squares[:, pl.ds(LANES, LANES)]
    for step, device in enumerate((who["core"], near, far_off, who["x"], who["y"])):
        s_got[0, step] = total
        sends.start(
            lambda step=step: s_got.at[0, step],
            lambda step=step: s_got.at[1, step],
            s_sem.at[step],
            device,
        )
        landed(s_got.at[1, step], s_sem.at[step], device)
        total = total + s_got[1, step]
    norm[...] = jnp.broadcast_to(jnp.sqrt(jnp.sum(total, keepdims=True)), norm.shape)
    z_last(1)
    for i in range(PIECES):
        landed(gt.at[pl.ds(i * rows, rows), part(1 - x)], x_sem.at[i], who["x"])
    landed(h_out.at[part(1 - x)], h_sem, who["x"])
    landed(bt.at[1 - x], b_sem.at[1], who["x"])

    @pl.when(z < depth - 1)
    def _():
        z_send_of(0, z + 1, up_got, up_sem, who["up"], z_send.at[0]).wait_send()

    @pl.when(z > 0)
    def _():
        z_send_of(0, z - 1, down_got, down_sem, who["down"], z_send.at[1]).wait_send()

    for copy in own_copies:
        copy.wait()
    sends.finish()


def adam_kernel(
    owners, norm, bt, bw, bm, bv, g, w, m, v,
    w_new, m_new, v_new, bw_new, bm_new, bv_new,
):
    step = pl.program_id(0)
    per_step, width, block_rows = w.shape
    half = width // 2
    blocks = owners.shape[0] - 3
    me = lax.axis_index("dp")
    number = jnp.int32(0)
    for j in range(blocks):
        number += (owners[j] == me).astype(jnp.int32)
    factor = 1.0 / jnp.maximum(norm[:1, :1], 1.0)
    for r in range(per_step):
        grad = g[r].astype(jnp.float32) * factor
        valid = jnp.broadcast_to(step * per_step + r < number, (width, block_rows))
        news = adam_step(w[r], m[r], v[r], grad, 0.1)
        for ref, new in zip((w_new, m_new, v_new), news):
            ref[r] = jnp.where(valid, new, 0.0)

    @pl.when(step == 0)
    def _():
        lane_of = lax.broadcasted_iota(jnp.int32, (half, width), 1)
        row_of = lax.broadcasted_iota(jnp.int32, (half, width), 0)
        row = lax.broadcasted_iota(jnp.int32, (3, width), 0)
        grads = jnp.zeros((3, width), jnp.float32)
        valid = jnp.zeros((3, width), jnp.int32)
        for gate in range(3):
            owner, rank = bias_rank(owners, blocks, gate)
            line = jnp.zeros((1, width), jnp.float32)
            for h in range(2):
                column = bt[h][:, gate : gate + 1]
                line += jnp.sum(
                    jnp.where(lane_of == row_of + h * half, column, 0.0), axis=0, keepdims=True
                )
            here = (row == rank) & jnp.broadcast_to(owner == me, (3, width))
            grads = jnp.where(here, line, grads)
            valid = jnp.where(here, 1, valid)
        news = adam_step(bw[...], bm[...], bv[...], grads * factor, 0.0)
        for ref, new in zip((bw_new, bm_new, bv_new), news):
            ref[...] = jnp.where(valid > 0, new, 0.0)


def paired(
    inputs, resets, owners, kernel, kernel_first, kernel_second, bias_rows, bias_first, bias_second, cotangent
):
    _, width, length = inputs.shape
    slots, _, block_rows = kernel.shape
    blocks = owners.shape[0] - 3
    full = width * lax.axis_size("mp")
    depth = lax.axis_size("mp") // 2
    half = width // 2
    bf16, f32 = jnp.bfloat16, jnp.float32
    shape = jax.ShapeDtypeStruct
    hbm = pl.BlockSpec(memory_space=pltpu.MemorySpace.HBM)
    vmem = pl.BlockSpec(memory_space=pltpu.VMEM)
    smem = pl.BlockSpec(memory_space=pltpu.SMEM)
    dma = pltpu.SemaphoreType.DMA
    wg, xg, cg, rg, bg = pl.pallas_call(
        gather_kernel,
        out_shape=(
            shape((4 * slots, half, block_rows), bf16),
            shape((2, full, length), bf16),
            shape((2, half, length), bf16),
            shape((2, 1, length), jnp.int32),
            shape((4, 3, width), f32),
        ),
        in_specs=[hbm] * 5,
        out_specs=[hbm] * 5,
        scratch_shapes=[
            pltpu.VMEM((slots, width, block_rows), f32),
            pltpu.VMEM((slots, width, block_rows), bf16),
            dma((CHUNKS,)),
            dma((4 + CHUNKS,)),
            dma((64,)),
            dma((4, CHUNKS)),
            dma((2, 2 * depth)),
            dma,
            dma,
            dma((4,)),
        ],
        compiler_params=pltpu.CompilerParams(
            collective_id=0, has_side_effects=True, vmem_limit_bytes=VMEM
        ),
        name="gather",
    )(
        kernel,
        inputs.reshape(width, length),
        cotangent.reshape(width, length),
        resets,
        bias_rows,
    )
    h, gs, joined, wv, bgrad = pl.pallas_call(
        layer_kernel,
        out_shape=(
            shape((2, half, length), bf16),
            shape((4 * slots, half, block_rows), bf16),
            shape((6 * half, 2 * length), bf16),
            shape((6 * half, full), bf16),
            shape((half, LANES), f32),
        ),
        in_specs=[smem, hbm, hbm, vmem, vmem, vmem],
        out_specs=[vmem, hbm, hbm, hbm, vmem],
        scratch_shapes=[
            pltpu.SMEM((blocks,), jnp.int32),
            pltpu.SMEM((4,), jnp.int32),
            pltpu.VMEM((6 * half, full), bf16),
            pltpu.VMEM((2, full, length), bf16),
            pltpu.VMEM((6 * half, length), f32),
            pltpu.VMEM((6 * half, 2 * length), bf16),
            pltpu.VMEM((full // block_rows, 6 * half, block_rows), bf16),
            pltpu.VMEM((3 * half, LANES), f32),
            dma,
            dma((2,)),
            dma((2,)),
        ],
        compiler_params=pltpu.CompilerParams(vmem_limit_bytes=VMEM),
        name="layer",
    )(owners, wg, xg, cg, rg, bg)
    gt, h_new, ig, bt, norm = pl.pallas_call(
        reduce_kernel,
        out_shape=(
            shape((slots, width, block_rows), bf16),
            shape((width, length), bf16),
            shape((width, length), bf16),
            shape((2, half, LANES), f32),
            shape((8, LANES), f32),
        ),
        in_specs=[smem, hbm, hbm, hbm, hbm, vmem],
        out_specs=[hbm, hbm, hbm, vmem, vmem],
        scratch_shapes=[
            pltpu.VMEM((6 * half, full), bf16),
            pltpu.VMEM((6 * half, 2 * length), bf16),
            pltpu.VMEM((2, full, length), bf16),
            pltpu.VMEM((2, depth, width, length), bf16),
            pltpu.VMEM((2, depth, width, length), bf16),
            pltpu.VMEM((2, depth, width, length), bf16),
            pltpu.VMEM((width, length), bf16),
            pltpu.VMEM((2, slots, half, block_rows), bf16),
            pltpu.VMEM((2, slots, half, block_rows), bf16),
            pltpu.VMEM((2, half, LANES), f32),
            pltpu.VMEM((8, block_rows), f32),
            pltpu.VMEM((2, 5, 8, LANES), f32),
            dma((4,)),
            dma((2 + PIECES,)),
            dma((64,)),
            dma((2, PIECES)),
            dma((PIECES,)),
            dma((2, depth)),
            dma((2, depth)),
            dma((2, depth)),
            dma((2,)),
            dma,
            dma,
            dma((2,)),
            dma((5,)),
        ],
        compiler_params=pltpu.CompilerParams(
            collective_id=1, has_side_effects=True, vmem_limit_bytes=VMEM
        ),
        name="reduce",
    )(owners, gs, wv, joined, h, bgrad)
    per_step = 2
    block = pl.BlockSpec((per_step, width, block_rows), lambda i: (i, 0, 0))
    whole = lambda *dims: pl.BlockSpec(dims, lambda i: (0,) * len(dims))
    news = pl.pallas_call(
        adam_kernel,
        grid=(slots // per_step,),
        out_shape=(shape(kernel.shape, f32),) * 3 + (shape(bias_rows.shape, f32),) * 3,
        in_specs=[smem, whole(8, LANES), whole(2, half, LANES)]
        + [whole(*bias_rows.shape)] * 3
        + [block] * 4,
        out_specs=[block] * 3 + [whole(*bias_rows.shape)] * 3,
        compiler_params=pltpu.CompilerParams(vmem_limit_bytes=VMEM),
        name="adam",
    )(owners, norm, bt, bias_rows, bias_first, bias_second, gt, kernel, kernel_first, kernel_second)
    kernel_w, kernel_m, kernel_v, bias_w, bias_m, bias_v = news
    return (h_new[None], ig[None], kernel_w, kernel_m, kernel_v, bias_w, bias_m, bias_v, norm[0, 0])


def solution(mesh):
    placed = (
        P("dp", "mp", None),
        P("dp", None),
        P(),
        P("dp", "mp", None),
        P("dp", "mp", None),
        P("dp", "mp", None),
        P("dp", "mp"),
        P("dp", "mp"),
        P("dp", "mp"),
        P("dp", "mp", None),
    )
    fits = mesh.shape["dp"] == 4 and mesh.shape["mp"] == 8
    return jax.shard_map(
        paired if fits else shards,
        mesh=mesh,
        in_specs=placed,
        out_specs=(
            P("dp", "mp", None),
            P("dp", "mp", None),
            P("dp", "mp", None),
            P("dp", "mp", None),
            P("dp", "mp", None),
            P("dp", "mp"),
            P("dp", "mp"),
            P("dp", "mp"),
            P(),
        ),
        check_vma=False,
    )
```

```python
import jax
import jax.numpy as jnp
from jax import lax
from jax.experimental import pallas as pl
from jax.experimental.pallas import tpu as pltpu
from jax.sharding import PartitionSpec as P

D = 2304
STEP = 10


def earlier_count(owned):
    number = owned.shape[0]
    places = jnp.arange(number, dtype=jnp.int32)
    earlier = (owned[:, None] == owned[None, :]) & (places[None, :] < places[:, None])
    return jnp.sum(earlier.astype(jnp.int32), axis=1)


def slot_sources(slot, count):
    places = jnp.arange(slot.shape[0], dtype=jnp.int32)
    hits = slot[None, :] == jnp.arange(count, dtype=jnp.int32)[:, None]
    source = jnp.sum(jnp.where(hits, places[None, :], 0), axis=1)
    return (source, jnp.any(hits, axis=1).astype(jnp.float32))


def shift_later(values):
    return jnp.pad(values, ((0, 0), (0, 0), (1, 0)))[:, :, :-1]


def shift_earlier(values):
    return jnp.pad(values, ((0, 0), (0, 0), (0, 1)))[:, :, 1:]


def combine(earlier, later):
    return (earlier[0] * later[0], later[0] * earlier[1] + later[1])


def pooled(preact, keeping):
    channels = preact.shape[1] // 3
    candidate = jnp.tanh(preact[:, :channels])
    forget = jax.nn.sigmoid(preact[:, channels : 2 * channels])
    output_gate = jax.nn.sigmoid(preact[:, 2 * channels :])
    decay = forget * keeping[:, None, :]
    _, cells = lax.associative_scan(combine, (decay, (1.0 - forget) * candidate), axis=2)
    return output_gate * cells


def adam_step(weights, first, second, grad, decay_rate):
    rate = (2.0 * D) ** (-0.5)
    first_new = 0.9 * first + 0.1 * grad
    second_new = 0.999 * second + 0.001 * grad * grad
    first_hat = first_new / (1.0 - 0.9**STEP)
    second_hat = second_new / (1.0 - 0.999**STEP)
    weights_new = weights - rate * (
        first_hat / (jnp.sqrt(second_hat) + 1e-08) + decay_rate * weights
    )
    return (weights_new, first_new, second_new)


def shards(
    inputs,
    resets,
    owners,
    kernel,
    kernel_first,
    kernel_second,
    bias_rows,
    bias_first,
    bias_second,
    cotangent,
):
    streams, local_width, length = inputs.shape
    slots_own, _, block_rows = kernel.shape
    block_count = owners.shape[0] - 3
    dp_size = lax.axis_size("dp")
    dp_index = lax.axis_index("dp")
    kernel_owner = owners[:block_count]
    bias_owner = owners[block_count:]
    kernel_slot = kernel_owner * slots_own + earlier_count(kernel_owner)
    bias_slot = bias_owner * 3 + earlier_count(bias_owner)
    all_kernel, all_bias = (
        lax.all_gather(kernel.astype(jnp.bfloat16), "dp", axis=0, tiled=True),
        lax.all_gather(bias_rows.astype(jnp.bfloat16), "dp", axis=0, tiled=True),
    )
    per_gate = block_count // 3
    double_width = per_gate * block_rows
    full_width = double_width // 2
    gate_cols = 3 * local_width
    arranged = (
        all_kernel[kernel_slot]
        .reshape(3, per_gate, local_width, block_rows)
        .transpose(0, 2, 1, 3)
        .reshape(gate_cols, double_width)
    )
    paired_t = jnp.concatenate([arranged[:, :full_width], arranged[:, full_width:]], axis=0)
    bias_vec = all_bias[bias_slot].astype(jnp.float32).reshape(gate_cols)
    rows = paired_t
    projected = jnp.einsum(
        "ok,skl->sol",
        rows,
        lax.all_gather(inputs, "mp", axis=1, tiled=True),
        preferred_element_type=jnp.float32,
    )
    preact = (
        projected[:, :gate_cols] + shift_later(projected[:, gate_cols:]) + bias_vec[None, :, None]
    )
    keeping = (1 - resets).astype(jnp.float32)
    result, pullback = jax.vjp(lambda values: pooled(values, keeping), preact)
    pre_grad = pullback(cotangent.astype(jnp.float32))[0].astype(jnp.bfloat16)
    joined = jnp.concatenate([pre_grad, shift_earlier(pre_grad)], axis=1)
    bias_grad = jnp.sum(pre_grad.astype(jnp.float32), axis=(0, 2)).reshape(3, local_width)
    pair_grad = jnp.einsum(
        "sol,skl->ok",
        joined,
        lax.all_gather(inputs, "mp", axis=1, tiled=True),
        preferred_element_type=jnp.float32,
    )
    rows = paired_t
    term_rows = lax.psum_scatter(
        jnp.einsum("ok,sol->ksl", rows, joined, preferred_element_type=jnp.float32),
        "mp",
        scatter_dimension=0,
        tiled=True,
    )
    input_grads = jnp.transpose(term_rows.astype(jnp.bfloat16), (1, 0, 2))
    block_grad = pair_grad.reshape(2, 3, local_width, full_width).transpose(1, 2, 0, 3)
    block_grad = (
        block_grad.reshape(3, local_width, per_gate, block_rows)
        .transpose(0, 2, 1, 3)
        .reshape(block_count, local_width, block_rows)
    )
    kernel_source, kernel_valid = slot_sources(kernel_slot, dp_size * slots_own)
    bias_source, bias_valid = slot_sources(bias_slot, dp_size * 3)
    own_kernel_valid = lax.dynamic_slice_in_dim(kernel_valid, dp_index * slots_own, slots_own)
    own_bias_valid = lax.dynamic_slice_in_dim(bias_valid, dp_index * 3, 3)
    total_kernel, total_bias = lax.psum((block_grad, bias_grad), "dp")
    own_kernel_source = lax.dynamic_slice_in_dim(kernel_source, dp_index * slots_own, slots_own)
    own_bias_source = lax.dynamic_slice_in_dim(bias_source, dp_index * 3, 3)
    own_kernel = total_kernel[own_kernel_source] * own_kernel_valid[:, None, None]
    own_bias = total_bias[own_bias_source] * own_bias_valid[:, None]
    squares = jnp.sum(own_kernel * own_kernel) + jnp.sum(own_bias * own_bias)
    grad_norm = jnp.sqrt(lax.psum(squares, ("dp", "mp")))
    factor = 1.0 / jnp.maximum(grad_norm, 1.0)
    kernel_w, kernel_m, kernel_v = adam_step(
        kernel, kernel_first, kernel_second, own_kernel * factor, 0.1
    )
    bias_w, bias_m, bias_v = adam_step(bias_rows, bias_first, bias_second, own_bias * factor, 0.0)
    kernel_mask = own_kernel_valid[:, None, None] > 0.5
    bias_mask = own_bias_valid[:, None] > 0.5
    return (
        result.astype(jnp.bfloat16),
        input_grads,
        jnp.where(kernel_mask, kernel_w, 0.0),
        jnp.where(kernel_mask, kernel_m, 0.0),
        jnp.where(kernel_mask, kernel_v, 0.0),
        jnp.where(bias_mask, bias_w, 0.0),
        jnp.where(bias_mask, bias_m, 0.0),
        jnp.where(bias_mask, bias_v, 0.0),
        grad_norm,
    )


MESH_ID = pl.DeviceIdType.MESH
LANES = 128
CHUNKS = 4
BANDS = 3
VMEM = 61 * 2**20


def place():
    dp, mp = lax.axis_index("dp"), lax.axis_index("mp")
    return dp // 2, lax.rem(dp, 2), mp // 2, lax.rem(mp, 2)


def partners(y, x, z, c):
    dp, mp = y * 2 + x, z * 2 + c
    return {
        "x": (y * 2 + 1 - x, mp),
        "y": ((1 - y) * 2 + x, mp),
        "xy": ((1 - y) * 2 + 1 - x, mp),
        "core": (dp, z * 2 + 1 - c),
        "up": (dp, mp + 2),
        "down": (dp, mp - 2),
    }


def greet(who, names, z, depth, more=0):
    barrier = pltpu.get_barrier_semaphore()
    for name in names:
        pl.semaphore_signal(barrier, inc=1, device_id=who[name], device_id_type=MESH_ID)

    @pl.when(z < depth - 1)
    def _():
        pl.semaphore_signal(barrier, inc=1, device_id=who["up"], device_id_type=MESH_ID)

    @pl.when(z > 0)
    def _():
        pl.semaphore_signal(barrier, inc=1, device_id=who["down"], device_id_type=MESH_ID)

    both = (z < depth - 1).astype(jnp.int32) + (z > 0).astype(jnp.int32)
    pl.semaphore_wait(barrier, len(names) + more + both)


class Sends:
    def __init__(self, sems):
        self.sems, self.number, self.made = sems, 0, []

    def start(self, src, dst, recv, device, when=None):
        slot = self.number
        self.number += 1

        def build():
            return pltpu.make_async_remote_copy(
                src_ref=src(),
                dst_ref=dst(),
                send_sem=self.sems.at[slot],
                recv_sem=recv,
                device_id=device,
                device_id_type=MESH_ID,
            )

        def go():
            build().start()

        if when is None:
            go()
        else:
            pl.when(when)(go)
        self.made.append((build, when))

    def finish(self):
        for build, when in self.made:
            if when is None:
                build().wait_send()
            else:
                pl.when(when)(lambda build=build: build().wait_send())


def landed(ref, sem, device):
    pltpu.make_async_remote_copy(
        src_ref=ref, dst_ref=ref, send_sem=sem, recv_sem=sem, device_id=device, device_id_type=MESH_ID
    ).wait_recv()


def fill_order(perm):
    length = perm.shape[0]
    tile = 16
    column = lax.broadcasted_iota(jnp.int32, (tile, length), 1)
    wanted = lax.rem(column, LANES) * (length // LANES) + column // LANES
    wanted = wanted - lax.broadcasted_iota(jnp.int32, (tile, length), 0)

    def one(i, _):
        at = pl.ds(pl.multiple_of(i * tile, tile), tile)
        perm[at, :] = jnp.where(wanted == i * tile, 1.0, 0.0).astype(jnp.bfloat16)
        return 0

    lax.fori_loop(0, length // tile, one, 0)


def reorder(ref, perm):
    tile = 96 if ref.shape[0] % 96 == 0 else 16

    def one(i, _):
        at = pl.ds(pl.multiple_of(i * tile, tile), tile)
        moved = jnp.dot(ref[at, :], perm[...], preferred_element_type=jnp.float32)
        ref[at, :] = moved.astype(ref.dtype)
        return 0

    lax.fori_loop(0, ref.shape[0] // tile, one, 0)


def restore(src, dst, perm):
    tile = 96 if src.shape[0] % 96 == 0 else 16

    def one(i, _):
        at = pl.ds(pl.multiple_of(i * tile, tile), tile)
        moved = lax.dot_general(
            src[at, :], perm[...], (((1,), (1,)), ((), ())), preferred_element_type=jnp.float32
        )
        dst[at, :] = moved.astype(dst.dtype)
        return 0

    lax.fori_loop(0, src.shape[0] // tile, one, 0)


def gather_kernel(
    w_ref, x_ref, cot_ref, res_ref, bias_ref,
    wg, xg, cg, rg, bg,
    wf, wb, perm, xs, cs, rs, load_sem, own_sem, send_sem, w_sem, x_sem, c_sem, r_sem, b_sem,
):
    y, x, z, c = place()
    dp, mp = y * 2 + x, z * 2 + c
    who = partners(y, x, z, c)
    slots, width, _ = w_ref.shape
    length = xg.shape[2]
    half = width // 2
    depth = xg.shape[1] // width // 2
    rows = slots // CHUNKS

    def part(index):
        return pl.ds(pl.multiple_of(index * half, half), half)

    def rows_of(index):
        return pl.ds(pl.multiple_of(index * width, width), width)

    loads = [
        pltpu.make_async_copy(
            w_ref.at[pl.ds(i * rows, rows)], wf.at[pl.ds(i * rows, rows)], load_sem.at[i]
        )
        for i in range(CHUNKS)
    ]
    takes = [
        pltpu.make_async_copy(x_ref, xs, load_sem.at[CHUNKS]),
        pltpu.make_async_copy(cot_ref, cs, load_sem.at[CHUNKS + 1]),
    ]
    for load in takes + loads:
        load.start()
    greet(who, ("x", "y", "xy", "core"), z, depth)
    fill_order(perm)
    takes[0].wait()
    reorder(xs, perm)
    sends = Sends(send_sem)

    def spread(stream, place_z, src, up, down, core=True):
        number = place_z * 2 + c

        def dst():
            return xg.at[stream, rows_of(number)]

        recv = x_sem.at[stream, number]
        if up is not False:
            sends.start(src, dst, recv, who["up"], up)
        if down is not False:
            sends.start(src, dst, recv, who["down"], down)
        sends.start(src, dst, recv, who["core"], core)

    spread(x, z, lambda: xs, z < depth - 1, z > 0, None)
    sends.start(lambda: xs, lambda: xg.at[x, rows_of(mp)], x_sem.at[x, mp], who["x"])
    takes[1].wait()
    reorder(cs, perm)
    keep = 1.0 - jnp.broadcast_to(res_ref[...], (16, length)).astype(jnp.float32)
    rs[...] = jnp.dot(keep.astype(jnp.bfloat16), perm[...], preferred_element_type=jnp.float32)[:1]
    own = [
        pltpu.make_async_copy(xs, xg.at[x, rows_of(mp)], own_sem.at[0]),
        pltpu.make_async_copy(cs.at[part(x)], cg.at[x], own_sem.at[1]),
        pltpu.make_async_copy(rs, rg.at[x], own_sem.at[2]),
        pltpu.make_async_copy(bias_ref, bg.at[dp], own_sem.at[3]),
    ]
    for copy in own:
        copy.start()
    for name in ("x", "y", "xy"):
        sends.start(lambda: bias_ref, lambda: bg.at[dp], b_sem.at[dp], who[name])
    sends.start(lambda: rs, lambda: rg.at[x], r_sem, who["x"])
    for i in range(CHUNKS):
        loads[i].wait()

        def cast(r, _, i=i):
            wb[i * rows + r] = wf[i * rows + r].astype(jnp.bfloat16)
            return 0

        lax.fori_loop(0, rows, cast, 0)

        def dst(i=i):
            return wg.at[pl.ds(dp * slots + i * rows, rows)]

        sends.start(lambda i=i: wb.at[pl.ds(i * rows, rows), part(x)], dst, w_sem.at[dp, i], who["y"])
        sends.start(
            lambda i=i: wb.at[pl.ds(i * rows, rows), part(1 - x)], dst, w_sem.at[dp, i], who["x"]
        )
        copy = pltpu.make_async_copy(wb.at[pl.ds(i * rows, rows), part(x)], dst(), own_sem.at[4 + i])
        copy.start()
        own.append(copy)
    sends.start(lambda: cs.at[part(1 - x)], lambda: cg.at[x], c_sem, who["x"])

    def along_z(stream, d):
        @pl.when(z >= d)
        def _():
            landed(xg.at[stream, rows_of((z - d) * 2 + c)], x_sem.at[stream, (z - d) * 2 + c], who["down"])

        src = lambda: xg.at[stream, rows_of((z - d) * 2 + c)]
        spread(stream, z - d, src, (z >= d) & (z < depth - 1), False, z >= d)

        @pl.when(z + d < depth)
        def _():
            landed(xg.at[stream, rows_of((z + d) * 2 + c)], x_sem.at[stream, (z + d) * 2 + c], who["up"])

        src = lambda: xg.at[stream, rows_of((z + d) * 2 + c)]
        spread(stream, z + d, src, False, (z + d < depth) & (z > 0), z + d < depth)

    def pass_on(i):
        def ref():
            return wg.at[pl.ds((y * 2 + 1 - x) * slots + i * rows, rows)]

        sem = w_sem.at[y * 2 + 1 - x, i]
        landed(ref(), sem, who["x"])
        sends.start(ref, ref, sem, who["y"])

    def other_stream():
        ref = lambda: xg.at[1 - x, rows_of(mp)]
        landed(ref(), x_sem.at[1 - x, mp], who["x"])
        spread(1 - x, z, ref, z < depth - 1, z > 0, None)

    steps = [lambda d=d: along_z(x, d) for d in range(1, depth)]
    steps += [lambda d=d: along_z(1 - x, d) for d in range(1, depth)]
    steps.insert(1, other_stream)
    after = [2, 4, 5, 7]
    for i in range(CHUNKS):
        steps.insert(min(after[i] + 1, len(steps)), lambda i=i: pass_on(i))
    for step in steps:
        step()
    for source in ((1 - y) * 2 + x, (1 - y) * 2 + 1 - x):
        for i in range(CHUNKS):
            landed(wg.at[pl.ds(source * slots + i * rows, rows)], w_sem.at[source, i], who["y"])
    for stream in (x, 1 - x):
        for k in range(depth):
            number = k * 2 + 1 - c
            landed(xg.at[stream, rows_of(number)], x_sem.at[stream, number], who["core"])
    landed(cg.at[1 - x], c_sem, who["x"])
    landed(rg.at[1 - x], r_sem, who["x"])
    for source in (y * 2 + 1 - x, (1 - y) * 2 + x, (1 - y) * 2 + 1 - x):
        landed(bg.at[source], b_sem.at[source], who["x"])
    for copy in own:
        copy.wait()
    sends.finish()


def bias_rank(owners, blocks, g):
    owner = owners[blocks + g]
    rank = jnp.int32(0)
    for h in range(g):
        rank += (owners[blocks + h] == owner).astype(jnp.int32)
    return owner, rank


def later(values):
    return [pltpu.roll(values[-1], 1, 1)] + values[:-1]


def scan_both(decay, fresh, source):
    groups = len(decay)
    held, gain = [fresh[0]], [decay[0]]
    for v in range(1, groups):
        held.append(fresh[v] + decay[v] * held[-1])
        gain.append(decay[v] * gain[-1])
    back, fall = [source[-1]], [None]
    for v in range(groups - 2, -1, -1):
        back.insert(0, source[v] + decay[v + 1] * back[0])
        fall.insert(0, decay[v + 1] if fall[0] is None else decay[v + 1] * fall[0])
    ahead = pltpu.roll(decay[0], LANES - 1, 1)
    level, factor = held[-1], gain[-1]
    behind, drop = back[0], fall[0] * ahead
    d = 1
    while d < LANES:
        level = level + factor * pltpu.roll(level, d, 1)
        behind = behind + drop * pltpu.roll(behind, LANES - d, 1)
        if 2 * d < LANES:
            factor = factor * pltpu.roll(factor, d, 1)
            drop = drop * pltpu.roll(drop, LANES - d, 1)
        d *= 2
    carry = pltpu.roll(level, 1, 1)
    cells = [held[v] + gain[v] * carry for v in range(groups)]
    carry = ahead * pltpu.roll(behind, LANES - 1, 1)
    dc = [back[v] + fall[v] * carry for v in range(groups - 1)] + [back[-1] + carry]
    return cells, dc


def gate_tile(p, pre_at, bias_at, keep, dh_at, h_at, joined_at, add_bias):
    groups = len(keep)
    lane = lax.broadcasted_iota(jnp.int32, keep[0].shape, 1)

    def pre(g):
        now = [pre_at(0, g, v) for v in range(groups)]
        before = later([pre_at(1, g, v) for v in range(groups)])
        before[0] = jnp.where(lane == 0, 0.0, before[0])
        bias = bias_at(g)
        return [n + b + bias for n, b in zip(now, before)]

    cand = [jnp.tanh(v) for v in pre(0)]
    forget = [jax.nn.sigmoid(v) for v in pre(1)]
    gate = [jax.nn.sigmoid(v) for v in pre(2)]
    decay = [f * k for f, k in zip(forget, keep)]
    dh = [dh_at(v) for v in range(groups)]
    cells, dc = scan_both(
        decay,
        [(1.0 - f) * z for f, z in zip(forget, cand)],
        [d * o for d, o in zip(dh, gate)],
    )
    for v in range(groups):
        h_at(v, gate[v] * cells[v])
    past = later(cells)
    grads = (
        [dc[v] * (1.0 - forget[v]) * (1.0 - cand[v] * cand[v]) for v in range(groups)],
        [
            dc[v] * (keep[v] * past[v] - cand[v]) * (forget[v] * (1.0 - forget[v]))
            for v in range(groups)
        ],
        [dh[v] * cells[v] * (gate[v] * (1.0 - gate[v])) for v in range(groups)],
    )
    for g in range(3):
        narrow = [value.astype(jnp.bfloat16) for value in grads[g]]
        wide = [value.astype(jnp.float32) for value in narrow]
        first = jnp.where(lane == LANES - 1, 0.0, pltpu.roll(wide[0], LANES - 1, 1))
        ahead = wide[1:] + [first]
        total = wide[0]
        for v in range(groups):
            joined_at(0, g, v, narrow[v])
            joined_at(1, g, v, ahead[v].astype(jnp.bfloat16))
            if v:
                total = total + wide[v]
        add_bias(jnp.where(lane == g, jnp.sum(total, axis=1, keepdims=True), 0.0))


def work_kernel(
    owners, slot, source, count, wg_in, xg_in, cg_in, rg, bg,
    gt, h_out, ig_out, bt, norm,
    wg, wv, xv, cg, hv, p, jv, gb, bcol, bgrad, perm, ig, up_got, down_got, core_got, x_got, b_got, squares, s_got,
    load_sem, own_sem, send_sem, y_sem, x_sem, core_sem, up_sem, down_sem, z_send, ix_sem, h_sem, b_sem, s_sem,
    free_sem,
):
    y, x, z, c = place()
    who = partners(y, x, z, c)
    slots, width, block_rows = gt.shape
    half = width // 2
    length = h_out.shape[1]
    full = xv.shape[1]
    depth = full // width // 2
    per_half = full // block_rows
    blocks = 6 * per_half
    tile = 16
    groups = length // LANES
    band = wg.shape[1]
    bands = half // band
    got, give = 0, wg.shape[0] // 2
    streams = (1 - x, x)

    def part(index):
        return pl.ds(pl.multiple_of(index * half, half), half)

    def rows_of(place_z, core):
        return pl.ds(pl.multiple_of((place_z * 2 + core) * width, width), width)

    x_loads = [
        pltpu.make_async_copy(xg_in.at[streams[q]], xv.at[q], load_sem.at[q]) for q in range(2)
    ]
    w_load = pltpu.make_async_copy(wg_in, wg, load_sem.at[2])
    c_load = pltpu.make_async_copy(cg_in, cg, load_sem.at[3])
    for load in (w_load, x_loads[0], c_load, x_loads[1]):
        load.start()
    near = (y * 2 + x, jnp.bitwise_xor(z, 1) * 2 + c)
    far_off = (y * 2 + x, jnp.bitwise_xor(z, 2) * 2 + c)
    barrier = pltpu.get_barrier_semaphore()
    for device in (near, far_off):
        pl.semaphore_signal(barrier, inc=1, device_id=device, device_id_type=MESH_ID)
    greet(who, ("x", "y", "core"), z, depth, 2)

    sends = Sends(send_sem)

    fill_order(perm)
    lane_of = lax.broadcasted_iota(jnp.int32, (half, width), 1)
    row_of = lax.broadcasted_iota(jnp.int32, (half, width), 0)
    diagonal = lane_of == row_of + x * half
    for g in range(3):
        owner, rank = bias_rank(owners, blocks, g)
        held = bg[owner]
        line = jnp.zeros((1, width), jnp.float32)
        for r in range(3):
            line = jnp.where(rank == r, held[r : r + 1], line)
        line = line.astype(jnp.bfloat16).astype(jnp.float32)
        column = jnp.sum(jnp.where(diagonal, line, 0.0), axis=1, keepdims=True)
        bcol[pl.ds(g * half, half), :] = jnp.broadcast_to(column, (half, LANES))
    bgrad[...] = jnp.zeros_like(bgrad)
    w_load.wait()
    for h in range(2):
        for g in range(3):

            def arrange(k, _, h=h, g=g):
                first = slot[g * 2 * per_half + h * per_half + k] * bands
                columns = pl.ds(pl.multiple_of(k * block_rows, block_rows), block_rows)
                for n in range(bands):
                    wv[pl.ds((n * 6 + h * 3 + g) * band, band), columns] = wg[first + n]
                return 0

            lax.fori_loop(0, per_half, arrange, 0)
    pl.semaphore_signal(free_sem, inc=1, device_id=who["y"], device_id_type=MESH_ID)

    def project(q, first, number):
        def one(n, _):
            columns = pl.ds(pl.multiple_of(n * 256, 256), 256)
            at = pl.ds(first * 6 * band, number * 6 * band)
            p[at, columns] = jnp.dot(wv[at, :], xv[q, :, columns], preferred_element_type=jnp.float32)
            return 0

        lax.fori_loop(0, length // 256, one, 0)

    def gates(q, n):
        lane = lax.broadcasted_iota(jnp.int32, (tile, LANES), 1)
        keep = [
            jnp.broadcast_to(rg[streams[q], :, pl.ds(v * LANES, LANES)], (tile, LANES))
            for v in range(groups)
        ]
        keep[0] = jnp.where(lane == 0, 0.0, keep[0])

        def one(i, _):
            off = pl.multiple_of(i * tile, tile)
            at = pl.ds(n * band + off, tile)

            def row(h, g):
                return pl.ds((n * 6 + h * 3 + g) * band + off, tile)

            def h_at(v, value):
                hv[at, pl.ds(v * LANES, LANES)] = value.astype(jnp.bfloat16)

            def joined_at(h, g, v, value):
                jv[row(h, g), pl.ds(q * length + v * LANES, LANES)] = value

            def add_bias(value):
                bgrad[at, :] += value

            gate_tile(
                p,
                lambda h, g, v: p[row(h, g), pl.ds(v * LANES, LANES)],
                lambda g: bcol[pl.ds(g * half + n * band + off, tile), :],
                keep,
                lambda v: cg[streams[q], at, pl.ds(v * LANES, LANES)].astype(jnp.float32),
                h_at,
                joined_at,
                add_bias,
            )
            return 0

        lax.fori_loop(0, band // tile, one, 0)

    def weight_grad(n):
        at = pl.ds(n * 6 * band, 6 * band)
        both = (((1,), (1,)), ((), ()))

        def one(k, _):
            rows = pl.ds(pl.multiple_of(k * block_rows, block_rows), block_rows)
            total = lax.dot_general(
                jv[at, pl.ds(0, length)], xv[0, rows, :], both, preferred_element_type=jnp.float32
            )
            total += lax.dot_general(
                jv[at, pl.ds(length, length)], xv[1, rows, :], both, preferred_element_type=jnp.float32
            )
            total = total.astype(jnp.bfloat16)
            for i in range(6):
                gb[n, k * 6 + i] = total[i * band : (i + 1) * band]
            return 0

        lax.fori_loop(0, per_half, one, 0)

        for q in range(2):

            def pack(r, _, q=q):
                wg[give + (n * 2 + q) * slots + r] = gb[n, source[((1 - y) * 2 + streams[q]) * slots + r]]
                return 0

            lax.fori_loop(0, slots, pack, 0)

    def y_send(t):
        sends.start(
            lambda: wg.at[pl.ds(give + t * slots, slots)],
            lambda: wg.at[pl.ds(got + t * slots, slots)],
            y_sem.at[t],
            who["y"],
        )

    def input_grad(q):
        def one(k, _):
            columns = pl.ds(pl.multiple_of(k * 256, 256), 256)
            ig[q, columns, :] = lax.dot_general(
                wv[:, columns],
                jv[:, pl.ds(q * length, length)],
                (((0,), (0,)), ((), ())),
                preferred_element_type=jnp.float32,
            ).astype(jnp.bfloat16)
            return 0

        lax.fori_loop(0, full // 256, one, 0)
        for k in range(depth):
            sends.start(
                lambda k=k: ig.at[q, rows_of(k, 1 - c)],
                lambda k=k: core_got.at[q, k],
                core_sem.at[q, k],
                who["core"],
            )

    def add_tiles(refs):
        def one(i, _):
            at = pl.ds(pl.multiple_of(i * tile, tile), tile)
            total = refs[0][at, :].astype(jnp.float32)
            for ref in refs[1:]:
                total += ref[at, :].astype(jnp.float32)
            refs[0][at, :] = total.astype(jnp.bfloat16)
            return 0

        lax.fori_loop(0, width // tile, one, 0)

    def z_send_of(q, dest, got, recv, device, sem):
        return pltpu.make_async_remote_copy(
            src_ref=ig.at[q, rows_of(dest, c)],
            dst_ref=got.at[q, dest],
            send_sem=sem,
            recv_sem=recv.at[q, dest],
            device_id=device,
            device_id_type=MESH_ID,
        )

    def z_tick(t):
        hops = depth - 1
        for index, (after, got, recv, source, target) in enumerate(
            (
                (z, up_got, up_sem, who["down"], who["up"]),
                (depth - 1 - z, down_got, down_sem, who["up"], who["down"]),
            )
        ):
            item = t - after
            k = lax.rem(jnp.maximum(item, 0), hops)
            q = jnp.maximum(item, 0) // hops
            dest = depth - 1 - k if index == 0 else k
            on = (item >= 0) & (after < depth - 1 - k)

            @pl.when(on)
            def _(index=index, after=after, got=got, recv=recv, source=source, target=target, item=item, q=q, dest=dest):
                landed(core_got.at[q, dest], core_sem.at[q, dest], who["core"])
                mine = ig.at[q, rows_of(dest, c)]

                @pl.when(after == 0)
                def _():
                    add_tiles((mine, core_got.at[q, dest]))

                @pl.when(after > 0)
                def _():
                    landed(got.at[q, dest], recv.at[q, dest], source)
                    add_tiles((mine, core_got.at[q, dest], got.at[q, dest]))

                send = z_send_of(q, dest, got, recv, target, z_send.at[index])

                @pl.when(item > 0)
                def _():
                    send.wait_send()

                send.start()

    def z_last(q):
        landed(core_got.at[q, z], core_sem.at[q, z], who["core"])
        extra = (core_got.at[q, z],)
        if q == 1:
            landed(x_got, ix_sem, who["x"])
            extra += (x_got,)
        mine = ig.at[q, rows_of(z, c)]

        @pl.when(z > 0)
        def _():
            landed(up_got.at[q, z], up_sem.at[q, z], who["down"])

        @pl.when(z < depth - 1)
        def _():
            landed(down_got.at[q, z], down_sem.at[q, z], who["up"])

        @pl.when(z == 0)
        def _():
            add_tiles((mine, *extra, down_got.at[q, z]))

        @pl.when(z == depth - 1)
        def _():
            add_tiles((mine, *extra, up_got.at[q, z]))

        @pl.when((z > 0) & (z < depth - 1))
        def _():
            add_tiles((mine, *extra, up_got.at[q, z], down_got.at[q, z]))

        if q == 0:
            sends.start(lambda: mine, lambda: x_got, ix_sem, who["x"])
        else:
            restore(mine, x_got, perm)
            copy = pltpu.make_async_copy(x_got, ig_out, own_sem.at[1])
            copy.start()
            own_copies.append(copy)

    squares[...] = jnp.zeros_like(squares)
    own_copies = []

    def own_chunk(t):
        n, q = t // 2, t % 2
        landed(wg.at[pl.ds(got + t * slots, slots)], y_sem.at[t], who["y"])
        if t + 2 < 2 * bands:
            y_send(t + 2)
        mine = y * 2 + streams[q]

        def one(r, _):
            valid = jnp.broadcast_to(r < count[mine], (band, block_rows))
            total = gb[n, source[mine * slots + r]].astype(jnp.float32) + wg[
                got + t * slots + r
            ].astype(jnp.float32)
            total = jnp.where(valid, total, 0.0)
            wg[got + t * slots + r] = total.astype(jnp.bfloat16)
            squares[...] += jnp.sum((total * total).reshape(band // 8, 8, block_rows), axis=0)
            return 0

        lax.fori_loop(0, slots, one, 0)
        src = lambda: wg.at[pl.ds(got + t * slots, slots)]
        dst = lambda: gt.at[:, pl.ds(pl.multiple_of(x * half + n * band, 16), band)]
        if q == 0:
            sends.start(src, dst, x_sem.at[n], who["x"])
        else:
            copy = pltpu.make_async_copy(src(), dst(), own_sem.at[2 + n])
            copy.start()
            own_copies.append(copy)

    def bias_sum():
        landed(b_got.at[0], b_sem.at[0], who["y"])
        total = bgrad[...] + b_got[0]
        b_got[1] = total
        bt[x] = total
        sends.start(lambda: b_got.at[1], lambda: bt.at[x], b_sem.at[1], who["x"])
        counted = jnp.broadcast_to(y == 0, (half, LANES))
        each = jnp.where(counted, total * total, 0.0)
        squares[:, pl.ds(0, LANES)] += jnp.sum(each.reshape(half // 8, 8, LANES), axis=0)

    x_loads[0].wait()
    c_load.wait()
    project(0, 0, bands)
    for n in range(bands):
        gates(0, n)
    input_grad(0)
    restore(hv, cg.at[streams[0]], perm)
    sends.start(lambda: cg.at[1 - x], lambda: h_out.at[part(x)], h_sem, who["x"])
    x_loads[1].wait()
    ticks = 2 * (depth - 1)
    chunks = 2 * bands
    for n in range(bands):
        project(1, n, 1)
        if n == 0:
            z_tick(0)
        gates(1, n)
        weight_grad(n)
        if n == 0:
            pl.semaphore_wait(free_sem, 1)
            y_send(0)
            y_send(1)
    sends.start(lambda: bgrad, lambda: b_got.at[0], b_sem.at[0], who["y"])
    z_tick(1)
    input_grad(1)
    restore(hv, cg.at[streams[1]], perm)
    h_own = pltpu.make_async_copy(cg.at[x], h_out.at[part(x)], own_sem.at[0])
    h_own.start()
    own_copies.append(h_own)
    own_chunk(0)
    z_tick(2)
    bias_sum()
    done = 1
    for t in range(depth - 1, ticks + 1):
        if t < ticks:
            z_tick(t)
        if t == depth - 1:
            z_last(0)
        upto = min(chunks, max(done, 1 + (chunks - 1) * (t - depth + 2) // (ticks - depth + 2)))
        for i in range(done, upto):
            own_chunk(i)
        done = upto
    total = squares[:, pl.ds(0, LANES)] + squares[:, pl.ds(LANES, LANES)]
    for step, device in enumerate((who["core"], near, far_off, who["x"], who["y"])):
        s_got[0, step] = total
        sends.start(
            lambda step=step: s_got.at[0, step],
            lambda step=step: s_got.at[1, step],
            s_sem.at[step],
            device,
        )
        landed(s_got.at[1, step], s_sem.at[step], device)
        total = total + s_got[1, step]
    norm[...] = jnp.broadcast_to(jnp.sqrt(jnp.sum(total, keepdims=True)), norm.shape)
    z_last(1)
    for n in range(bands):
        landed(gt.at[:, pl.ds(pl.multiple_of((1 - x) * half + n * band, 16), band)], x_sem.at[n], who["x"])
    landed(h_out.at[part(1 - x)], h_sem, who["x"])
    landed(bt.at[1 - x], b_sem.at[1], who["x"])

    @pl.when(z < depth - 1)
    def _():
        z_send_of(0, z + 1, up_got, up_sem, who["up"], z_send.at[0]).wait_send()

    @pl.when(z > 0)
    def _():
        z_send_of(0, z - 1, down_got, down_sem, who["down"], z_send.at[1]).wait_send()

    for copy in own_copies:
        copy.wait()
    sends.finish()


def adam_kernel(
    owners, norm, bt, bw, bm, bv, g, w, m, v,
    w_new, m_new, v_new, bw_new, bm_new, bv_new,
):
    step = pl.program_id(0)
    per_step, width, block_rows = w.shape
    half = width // 2
    blocks = owners.shape[0] - 3
    me = lax.axis_index("dp")
    number = jnp.int32(0)
    for j in range(blocks):
        number += (owners[j] == me).astype(jnp.int32)
    factor = 1.0 / jnp.maximum(norm[:1, :1], 1.0)
    for r in range(per_step):
        grad = g[r].astype(jnp.float32) * factor
        valid = jnp.broadcast_to(step * per_step + r < number, (width, block_rows))
        news = adam_step(w[r], m[r], v[r], grad, 0.1)
        for ref, new in zip((w_new, m_new, v_new), news):
            ref[r] = jnp.where(valid, new, 0.0)

    @pl.when(step == 0)
    def _():
        lane_of = lax.broadcasted_iota(jnp.int32, (half, width), 1)
        row_of = lax.broadcasted_iota(jnp.int32, (half, width), 0)
        row = lax.broadcasted_iota(jnp.int32, (3, width), 0)
        grads = jnp.zeros((3, width), jnp.float32)
        valid = jnp.zeros((3, width), jnp.int32)
        for gate in range(3):
            owner, rank = bias_rank(owners, blocks, gate)
            line = jnp.zeros((1, width), jnp.float32)
            for h in range(2):
                column = bt[h][:, gate : gate + 1]
                line += jnp.sum(
                    jnp.where(lane_of == row_of + h * half, column, 0.0), axis=0, keepdims=True
                )
            here = (row == rank) & jnp.broadcast_to(owner == me, (3, width))
            grads = jnp.where(here, line, grads)
            valid = jnp.where(here, 1, valid)
        news = adam_step(bw[...], bm[...], bv[...], grads * factor, 0.0)
        for ref, new in zip((bw_new, bm_new, bv_new), news):
            ref[...] = jnp.where(valid > 0, new, 0.0)


def tables(owned, slots):
    blocks = owned.shape[0]
    per_half = blocks // 6
    slot = owned * slots + earlier_count(owned)
    number = jnp.arange(blocks, dtype=jnp.int32)
    stands = lax.rem(number, per_half) * 6 + lax.rem(number // per_half, 2) * 3 + number // (2 * per_half)
    hits = slot[None, :] == jnp.arange(4 * slots, dtype=jnp.int32)[:, None]
    source = jnp.sum(jnp.where(hits, stands[None, :], 0), axis=1)
    count = jnp.sum((owned[None, :] == jnp.arange(4, dtype=jnp.int32)[:, None]).astype(jnp.int32), axis=1)
    return slot, source, count


def paired(
    inputs, resets, owners, kernel, kernel_first, kernel_second, bias_rows, bias_first, bias_second, cotangent
):
    _, width, length = inputs.shape
    slots, _, block_rows = kernel.shape
    blocks = owners.shape[0] - 3
    full = width * lax.axis_size("mp")
    depth = lax.axis_size("mp") // 2
    half = width // 2
    bf16, f32 = jnp.bfloat16, jnp.float32
    shape = jax.ShapeDtypeStruct
    hbm = pl.BlockSpec(memory_space=pltpu.MemorySpace.HBM)
    vmem = pl.BlockSpec(memory_space=pltpu.VMEM)
    smem = pl.BlockSpec(memory_space=pltpu.SMEM)
    dma = pltpu.SemaphoreType.DMA
    wg, xg, cg, rg, bg = pl.pallas_call(
        gather_kernel,
        out_shape=(
            shape((4 * slots, half, block_rows), bf16),
            shape((2, full, length), bf16),
            shape((2, half, length), bf16),
            shape((2, 1, length), f32),
            shape((4, 3, width), f32),
        ),
        in_specs=[hbm] * 3 + [vmem, hbm],
        out_specs=[hbm] * 5,
        scratch_shapes=[
            pltpu.VMEM((slots, width, block_rows), f32),
            pltpu.VMEM((slots, width, block_rows), bf16),
            pltpu.VMEM((length, length), bf16),
            pltpu.VMEM((width, length), bf16),
            pltpu.VMEM((width, length), bf16),
            pltpu.VMEM((1, length), f32),
            dma((CHUNKS + 2,)),
            dma((4 + CHUNKS,)),
            dma((64,)),
            dma((4, CHUNKS)),
            dma((2, 2 * depth)),
            dma,
            dma,
            dma((4,)),
        ],
        compiler_params=pltpu.CompilerParams(
            collective_id=0, has_side_effects=True, vmem_limit_bytes=VMEM
        ),
        name="gather",
    )(
        kernel,
        inputs.reshape(width, length),
        cotangent.reshape(width, length),
        resets,
        bias_rows,
    )
    band = half // BANDS
    slot, source, count = tables(owners[:blocks], slots)
    gt, h_new, ig, bt, norm = pl.pallas_call(
        work_kernel,
        out_shape=(
            shape((slots, width, block_rows), bf16),
            shape((width, length), bf16),
            shape((width, length), bf16),
            shape((2, half, LANES), f32),
            shape((8, LANES), f32),
        ),
        in_specs=[smem] * 4 + [hbm] * 3 + [vmem] * 2,
        out_specs=[hbm, hbm, hbm, vmem, vmem],
        scratch_shapes=[
            pltpu.VMEM((4 * slots * BANDS, band, block_rows), bf16),
            pltpu.VMEM((6 * half, full), bf16),
            pltpu.VMEM((2, full, length), bf16),
            pltpu.VMEM((2, half, length), bf16),
            pltpu.VMEM((half, length), bf16),
            pltpu.VMEM((6 * half, length), f32),
            pltpu.VMEM((6 * half, 2 * length), bf16),
            pltpu.VMEM((BANDS, blocks, band, block_rows), bf16),
            pltpu.VMEM((3 * half, LANES), f32),
            pltpu.VMEM((half, LANES), f32),
            pltpu.VMEM((length, length), bf16),
            pltpu.VMEM((2, full, length), bf16),
            pltpu.VMEM((2, depth, width, length), bf16),
            pltpu.VMEM((2, depth, width, length), bf16),
            pltpu.VMEM((2, depth, width, length), bf16),
            pltpu.VMEM((width, length), bf16),
            pltpu.VMEM((2, half, LANES), f32),
            pltpu.VMEM((8, block_rows), f32),
            pltpu.VMEM((2, 5, 8, LANES), f32),
            dma((4,)),
            dma((2 + BANDS,)),
            dma((64,)),
            dma((2 * BANDS,)),
            dma((BANDS,)),
            dma((2, depth)),
            dma((2, depth)),
            dma((2, depth)),
            dma((2,)),
            dma,
            dma,
            dma((2,)),
            dma((5,)),
            pltpu.SemaphoreType.REGULAR,
        ],
        compiler_params=pltpu.CompilerParams(
            collective_id=1, has_side_effects=True, vmem_limit_bytes=VMEM
        ),
        name="work",
    )(
        owners, slot, source, count, wg.reshape(4 * slots * BANDS, band, block_rows), xg, cg, rg, bg
    )
    per_step = 2
    block = pl.BlockSpec((per_step, width, block_rows), lambda i: (i, 0, 0))
    whole = lambda *dims: pl.BlockSpec(dims, lambda i: (0,) * len(dims))
    news = pl.pallas_call(
        adam_kernel,
        grid=(slots // per_step,),
        out_shape=(shape(kernel.shape, f32),) * 3 + (shape(bias_rows.shape, f32),) * 3,
        in_specs=[smem, whole(8, LANES), whole(2, half, LANES)]
        + [whole(*bias_rows.shape)] * 3
        + [block] * 4,
        out_specs=[block] * 3 + [whole(*bias_rows.shape)] * 3,
        compiler_params=pltpu.CompilerParams(vmem_limit_bytes=VMEM),
        name="adam",
    )(owners, norm, bt, bias_rows, bias_first, bias_second, gt, kernel, kernel_first, kernel_second)
    kernel_w, kernel_m, kernel_v, bias_w, bias_m, bias_v = news
    return (h_new[None], ig[None], kernel_w, kernel_m, kernel_v, bias_w, bias_m, bias_v, norm[0, 0])


def solution(mesh):
    placed = (
        P("dp", "mp", None),
        P("dp", None),
        P(),
        P("dp", "mp", None),
        P("dp", "mp", None),
        P("dp", "mp", None),
        P("dp", "mp"),
        P("dp", "mp"),
        P("dp", "mp"),
        P("dp", "mp", None),
    )
    fits = mesh.shape["dp"] == 4 and mesh.shape["mp"] == 8
    return jax.shard_map(
        paired if fits else shards,
        mesh=mesh,
        in_specs=placed,
        out_specs=(
            P("dp", "mp", None),
            P("dp", "mp", None),
            P("dp", "mp", None),
            P("dp", "mp", None),
            P("dp", "mp", None),
            P("dp", "mp"),
            P("dp", "mp"),
            P("dp", "mp"),
            P(),
        ),
        check_vma=False,
    )
```

```python
import jax
import jax.numpy as jnp
from jax import lax
from jax.experimental import pallas as pl
from jax.experimental.pallas import tpu as pltpu
from jax.sharding import PartitionSpec as P

D = 2304
STEP = 10


def earlier_count(owned):
    number = owned.shape[0]
    places = jnp.arange(number, dtype=jnp.int32)
    earlier = (owned[:, None] == owned[None, :]) & (places[None, :] < places[:, None])
    return jnp.sum(earlier.astype(jnp.int32), axis=1)


def slot_sources(slot, count):
    places = jnp.arange(slot.shape[0], dtype=jnp.int32)
    hits = slot[None, :] == jnp.arange(count, dtype=jnp.int32)[:, None]
    source = jnp.sum(jnp.where(hits, places[None, :], 0), axis=1)
    return (source, jnp.any(hits, axis=1).astype(jnp.float32))


def shift_later(values):
    return jnp.pad(values, ((0, 0), (0, 0), (1, 0)))[:, :, :-1]


def shift_earlier(values):
    return jnp.pad(values, ((0, 0), (0, 0), (0, 1)))[:, :, 1:]


def combine(earlier, later):
    return (earlier[0] * later[0], later[0] * earlier[1] + later[1])


def pooled(preact, keeping):
    channels = preact.shape[1] // 3
    candidate = jnp.tanh(preact[:, :channels])
    forget = jax.nn.sigmoid(preact[:, channels : 2 * channels])
    output_gate = jax.nn.sigmoid(preact[:, 2 * channels :])
    decay = forget * keeping[:, None, :]
    _, cells = lax.associative_scan(combine, (decay, (1.0 - forget) * candidate), axis=2)
    return output_gate * cells


def adam_step(weights, first, second, grad, decay_rate):
    rate = (2.0 * D) ** (-0.5)
    first_new = 0.9 * first + 0.1 * grad
    second_new = 0.999 * second + 0.001 * grad * grad
    first_hat = first_new / (1.0 - 0.9**STEP)
    second_hat = second_new / (1.0 - 0.999**STEP)
    weights_new = weights - rate * (
        first_hat / (jnp.sqrt(second_hat) + 1e-08) + decay_rate * weights
    )
    return (weights_new, first_new, second_new)


def shards(
    inputs,
    resets,
    owners,
    kernel,
    kernel_first,
    kernel_second,
    bias_rows,
    bias_first,
    bias_second,
    cotangent,
):
    streams, local_width, length = inputs.shape
    slots_own, _, block_rows = kernel.shape
    block_count = owners.shape[0] - 3
    dp_size = lax.axis_size("dp")
    dp_index = lax.axis_index("dp")
    kernel_owner = owners[:block_count]
    bias_owner = owners[block_count:]
    kernel_slot = kernel_owner * slots_own + earlier_count(kernel_owner)
    bias_slot = bias_owner * 3 + earlier_count(bias_owner)
    all_kernel, all_bias = (
        lax.all_gather(kernel.astype(jnp.bfloat16), "dp", axis=0, tiled=True),
        lax.all_gather(bias_rows.astype(jnp.bfloat16), "dp", axis=0, tiled=True),
    )
    per_gate = block_count // 3
    double_width = per_gate * block_rows
    full_width = double_width // 2
    gate_cols = 3 * local_width
    arranged = (
        all_kernel[kernel_slot]
        .reshape(3, per_gate, local_width, block_rows)
        .transpose(0, 2, 1, 3)
        .reshape(gate_cols, double_width)
    )
    paired_t = jnp.concatenate([arranged[:, :full_width], arranged[:, full_width:]], axis=0)
    bias_vec = all_bias[bias_slot].astype(jnp.float32).reshape(gate_cols)
    rows = paired_t
    projected = jnp.einsum(
        "ok,skl->sol",
        rows,
        lax.all_gather(inputs, "mp", axis=1, tiled=True),
        preferred_element_type=jnp.float32,
    )
    preact = (
        projected[:, :gate_cols] + shift_later(projected[:, gate_cols:]) + bias_vec[None, :, None]
    )
    keeping = (1 - resets).astype(jnp.float32)
    result, pullback = jax.vjp(lambda values: pooled(values, keeping), preact)
    pre_grad = pullback(cotangent.astype(jnp.float32))[0].astype(jnp.bfloat16)
    joined = jnp.concatenate([pre_grad, shift_earlier(pre_grad)], axis=1)
    bias_grad = jnp.sum(pre_grad.astype(jnp.float32), axis=(0, 2)).reshape(3, local_width)
    pair_grad = jnp.einsum(
        "sol,skl->ok",
        joined,
        lax.all_gather(inputs, "mp", axis=1, tiled=True),
        preferred_element_type=jnp.float32,
    )
    rows = paired_t
    term_rows = lax.psum_scatter(
        jnp.einsum("ok,sol->ksl", rows, joined, preferred_element_type=jnp.float32),
        "mp",
        scatter_dimension=0,
        tiled=True,
    )
    input_grads = jnp.transpose(term_rows.astype(jnp.bfloat16), (1, 0, 2))
    block_grad = pair_grad.reshape(2, 3, local_width, full_width).transpose(1, 2, 0, 3)
    block_grad = (
        block_grad.reshape(3, local_width, per_gate, block_rows)
        .transpose(0, 2, 1, 3)
        .reshape(block_count, local_width, block_rows)
    )
    kernel_source, kernel_valid = slot_sources(kernel_slot, dp_size * slots_own)
    bias_source, bias_valid = slot_sources(bias_slot, dp_size * 3)
    own_kernel_valid = lax.dynamic_slice_in_dim(kernel_valid, dp_index * slots_own, slots_own)
    own_bias_valid = lax.dynamic_slice_in_dim(bias_valid, dp_index * 3, 3)
    total_kernel, total_bias = lax.psum((block_grad, bias_grad), "dp")
    own_kernel_source = lax.dynamic_slice_in_dim(kernel_source, dp_index * slots_own, slots_own)
    own_bias_source = lax.dynamic_slice_in_dim(bias_source, dp_index * 3, 3)
    own_kernel = total_kernel[own_kernel_source] * own_kernel_valid[:, None, None]
    own_bias = total_bias[own_bias_source] * own_bias_valid[:, None]
    squares = jnp.sum(own_kernel * own_kernel) + jnp.sum(own_bias * own_bias)
    grad_norm = jnp.sqrt(lax.psum(squares, ("dp", "mp")))
    factor = 1.0 / jnp.maximum(grad_norm, 1.0)
    kernel_w, kernel_m, kernel_v = adam_step(
        kernel, kernel_first, kernel_second, own_kernel * factor, 0.1
    )
    bias_w, bias_m, bias_v = adam_step(bias_rows, bias_first, bias_second, own_bias * factor, 0.0)
    kernel_mask = own_kernel_valid[:, None, None] > 0.5
    bias_mask = own_bias_valid[:, None] > 0.5
    return (
        result.astype(jnp.bfloat16),
        input_grads,
        jnp.where(kernel_mask, kernel_w, 0.0),
        jnp.where(kernel_mask, kernel_m, 0.0),
        jnp.where(kernel_mask, kernel_v, 0.0),
        jnp.where(bias_mask, bias_w, 0.0),
        jnp.where(bias_mask, bias_m, 0.0),
        jnp.where(bias_mask, bias_v, 0.0),
        grad_norm,
    )


MESH_ID = pl.DeviceIdType.MESH
LANES = 128
BANDS = 3
DEEP = 8
STAGES = 4
VMEM = 61 * 2**20


def place():
    dp, mp = lax.axis_index("dp"), lax.axis_index("mp")
    return dp // 2, lax.rem(dp, 2), mp // 2, lax.rem(mp, 2)


def partners(y, x, z, c):
    dp, mp = y * 2 + x, z * 2 + c
    return {
        "x": (y * 2 + 1 - x, mp),
        "y": ((1 - y) * 2 + x, mp),
        "xy": ((1 - y) * 2 + 1 - x, mp),
        "core": (dp, z * 2 + 1 - c),
        "up": (dp, mp + 2),
        "down": (dp, mp - 2),
    }


def greet(devices):
    barrier = pltpu.get_barrier_semaphore()
    for device in devices:
        pl.semaphore_signal(barrier, inc=1, device_id=device, device_id_type=MESH_ID)
    pl.semaphore_wait(barrier, len(devices))


class Sends:
    def __init__(self, sems):
        self.sems, self.number, self.made = sems, 0, {}

    def start(self, src, dst, recv, device, when=None):
        slot = self.number
        self.number += 1

        def build():
            return pltpu.make_async_remote_copy(
                src_ref=src(),
                dst_ref=dst(),
                send_sem=self.sems.at[slot],
                recv_sem=recv,
                device_id=device,
                device_id_type=MESH_ID,
            )

        if when is None:
            build().start()
        else:
            pl.when(when)(lambda: build().start())
        self.made[slot] = (build, when)
        return slot

    def wait(self, slots):
        for slot in slots:
            build, when = self.made.pop(slot)
            if when is None:
                build().wait_send()
            else:
                pl.when(when)(lambda build=build: build().wait_send())

    def finish(self):
        self.wait(list(self.made))


def landed(ref, sem, device):
    pltpu.make_async_remote_copy(
        src_ref=ref, dst_ref=ref, send_sem=sem, recv_sem=sem, device_id=device, device_id_type=MESH_ID
    ).wait_recv()


def fill_order(perm):
    length = perm.shape[0]
    tile = 16
    column = lax.broadcasted_iota(jnp.int32, (tile, length), 1)
    wanted = lax.rem(column, LANES) * (length // LANES) + column // LANES
    wanted = wanted - lax.broadcasted_iota(jnp.int32, (tile, length), 0)

    def one(i, _):
        at = pl.ds(pl.multiple_of(i * tile, tile), tile)
        perm[at, :] = jnp.where(wanted == i * tile, 1.0, 0.0).astype(jnp.bfloat16)
        return 0

    lax.fori_loop(0, length // tile, one, 0)


def reorder(src, dst, perm):
    def one(i, _):
        at = pl.ds(pl.multiple_of(i * 256, 256), 256)
        moved = jnp.dot(src[...], perm[:, at], preferred_element_type=jnp.float32)
        dst[:, at] = moved.astype(dst.dtype)
        return 0

    lax.fori_loop(0, perm.shape[1] // 256, one, 0)


def restore(src, dst, perm):
    def one(i, _):
        at = pl.ds(pl.multiple_of(i * 256, 256), 256)
        moved = lax.dot_general(
            src[...], perm[at, :], (((1,), (1,)), ((), ())), preferred_element_type=jnp.float32
        )
        dst[:, at] = moved.astype(dst.dtype)
        return 0

    lax.fori_loop(0, perm.shape[0] // 256, one, 0)


def bias_rank(owners, blocks, g):
    owner = owners[blocks + g]
    rank = jnp.int32(0)
    for h in range(g):
        rank += (owners[blocks + h] == owner).astype(jnp.int32)
    return owner, rank


def sigmoid(v):
    return 0.5 * jnp.tanh(0.5 * v) + 0.5


def later(values):
    return [pltpu.roll(values[-1], 1, 1)] + values[:-1]


def scan_both(decay, fresh, source):
    groups = len(decay)
    held, gain = [fresh[0]], [decay[0]]
    for v in range(1, groups):
        held.append(fresh[v] + decay[v] * held[-1])
        gain.append(decay[v] * gain[-1])
    back, fall = [source[-1]], [None]
    for v in range(groups - 2, -1, -1):
        back.insert(0, source[v] + decay[v + 1] * back[0])
        fall.insert(0, decay[v + 1] if fall[0] is None else decay[v + 1] * fall[0])
    ahead = pltpu.roll(decay[0], LANES - 1, 1)
    level, factor = held[-1], gain[-1]
    behind, drop = back[0], fall[0] * ahead
    d = 1
    while d < LANES:
        level = level + factor * pltpu.roll(level, d, 1)
        behind = behind + drop * pltpu.roll(behind, LANES - d, 1)
        if 2 * d < LANES:
            factor = factor * pltpu.roll(factor, d, 1)
            drop = drop * pltpu.roll(drop, LANES - d, 1)
        d *= 2
    carry = pltpu.roll(level, 1, 1)
    cells = [held[v] + gain[v] * carry for v in range(groups)]
    carry = ahead * pltpu.roll(behind, LANES - 1, 1)
    dc = [back[v] + fall[v] * carry for v in range(groups - 1)] + [back[-1] + carry]
    return cells, dc


def gate_tile(p, pre_at, bias_at, keep, dh_at, h_at, joined_at, add_bias):
    groups = len(keep)
    lane = lax.broadcasted_iota(jnp.int32, keep[0].shape, 1)

    def pre(g):
        now = [pre_at(0, g, v) for v in range(groups)]
        before = later([pre_at(1, g, v) for v in range(groups)])
        before[0] = jnp.where(lane == 0, 0.0, before[0])
        bias = bias_at(g)
        return [n + b + bias for n, b in zip(now, before)]

    cand = [jnp.tanh(v) for v in pre(0)]
    forget = [sigmoid(v) for v in pre(1)]
    gate = [sigmoid(v) for v in pre(2)]
    decay = [f * k for f, k in zip(forget, keep)]
    dh = [dh_at(v) for v in range(groups)]
    cells, dc = scan_both(
        decay,
        [(1.0 - f) * z for f, z in zip(forget, cand)],
        [d * o for d, o in zip(dh, gate)],
    )
    for v in range(groups):
        h_at(v, gate[v] * cells[v])
    past = later(cells)
    grads = (
        [dc[v] * (1.0 - forget[v]) * (1.0 - cand[v] * cand[v]) for v in range(groups)],
        [
            dc[v] * (keep[v] * past[v] - cand[v]) * (forget[v] * (1.0 - forget[v]))
            for v in range(groups)
        ],
        [dh[v] * cells[v] * (gate[v] * (1.0 - gate[v])) for v in range(groups)],
    )
    for g in range(3):
        narrow = [value.astype(jnp.bfloat16) for value in grads[g]]
        wide = [value.astype(jnp.float32) for value in narrow]
        first = jnp.where(lane == LANES - 1, 0.0, pltpu.roll(wide[0], LANES - 1, 1))
        ahead = wide[1:] + [first]
        total = wide[0]
        for v in range(groups):
            joined_at(0, g, v, narrow[v])
            joined_at(1, g, v, ahead[v].astype(jnp.bfloat16))
            if v:
                total = total + wide[v]
        add_bias(jnp.where(lane == g, jnp.sum(total, axis=1, keepdims=True), 0.0))


def fill_tables(owners, table, table_v, sem, blocks, slots):
    per_half = blocks // 6
    down = lax.broadcasted_iota(jnp.int32, (64, LANES), 0)
    along = lax.broadcasted_iota(jnp.int32, (64, LANES), 1)

    def spell(j, both):
        owner = owners[j]
        return jnp.where(down == j, owner, both[0]), jnp.where(along == j, owner, both[1])

    start = (jnp.full((64, LANES), -1, jnp.int32), jnp.full((64, LANES), -2, jnp.int32))
    rows, columns = lax.fori_loop(0, blocks, spell, start)
    rank = jnp.sum(jnp.where((rows == columns) & (down < along), 1, 0), axis=0, keepdims=True)
    table_v[pl.ds(0, 1), :] = columns[:1] * slots + rank
    table_v[pl.ds(1, 1), :] = jnp.sum(jnp.where(rows == along, 1, 0), axis=0, keepdims=True)
    first = pltpu.make_async_copy(table_v.at[pl.ds(0, 8)], table.at[pl.ds(0, 8)], sem.at[0])
    first.start()
    first.wait()

    def place_of(j, held):
        stands = lax.rem(j, per_half) * 6 + lax.rem(j // per_half, 2) * 3 + j // (2 * per_half)
        return jnp.where(along[:1] == table[0, j], stands, held)

    table_v[pl.ds(8, 1), :] = lax.fori_loop(0, blocks, place_of, jnp.zeros((1, LANES), jnp.int32))
    second = pltpu.make_async_copy(table_v.at[pl.ds(8, 8)], table.at[pl.ds(8, 8)], sem.at[1])
    second.start()
    second.wait()


def layer_kernel(
    owners, w_ref, x_ref, cot_ref, res_ref, bias_ref,
    gt, h_out, ig_out, bt, norm,
    table, table_v, wf, wg0, wg1, wg2, wv, xv, cg, rg, bg, hv, p, jv, gb, bcol, bgrad, perm,
    ig, up_got, down_got, core_got, x_got, b_got, squares, s_got, t_got,
    load_sem, table_sem, own_sem, send_sem, w_sem, xg_sem, c_sem, r_sem, bg_sem,
    y_sem, x_sem, core_sem, up_sem, down_sem, z_send, ix_sem, h_sem, b_sem, s_sem, t_sem, free_sem,
):
    y, x, z, c = place()
    dp, mp = y * 2 + x, z * 2 + c
    who = partners(y, x, z, c)
    slots, width, block_rows = gt.shape
    half = width // 2
    length = h_out.shape[1]
    full = xv.shape[1]
    depth = full // width // 2
    per_half = full // block_rows
    blocks = 6 * per_half
    tile = 16
    groups = length // LANES
    wg = (wg0, wg1, wg2)
    band = wg0.shape[1]
    bands = half // band
    owner_x = (1 - x, x)
    mp_peers = [(dp, lax.rem(mp + r, 2 * depth)) for r in range(1, 2 * depth)]
    dp_peers = [who["x"], who["y"], who["xy"]]

    def part(index):
        return pl.ds(pl.multiple_of(index * half, half), half)

    def rows_of(place_z, core):
        return pl.ds(pl.multiple_of((place_z * 2 + core) * width, width), width)

    def piece(n, owner):
        return wg[n].at[pl.ds(owner * slots, slots)]

    def reused(t, give):
        row = (t + (2 * bands if give else 0)) * slots
        return wg[row // (4 * slots)], row % (4 * slots)

    def reused_at(t, give):
        ref, row = reused(t, give)
        return ref.at[pl.ds(row, slots)]

    mine = xv.at[1, rows_of(z, c)]
    x_held = jv.at[pl.ds(0, width), pl.ds(0, length)]
    c_held = [jv.at[pl.ds(width + i * half, half), pl.ds(0, length)] for i in range(2)]
    x_load = pltpu.make_async_copy(x_ref, x_held, load_sem.at[0])
    c_loads = [
        pltpu.make_async_copy(cot_ref.at[part(x)], c_held[0], load_sem.at[1]),
        pltpu.make_async_copy(cot_ref.at[part(1 - x)], c_held[1], load_sem.at[2]),
    ]

    def w_load(i):
        at = pl.multiple_of((x if i % 2 == 0 else 1 - x) * half + (i // 2) * band, 16)
        return pltpu.make_async_copy(
            w_ref.at[:, pl.ds(at, band)], wf.at[i % 2], load_sem.at[3 + i % 2]
        )

    x_load.start()
    w_load(0).start()
    w_load(1).start()
    for load in c_loads:
        load.start()
    greet(mp_peers + dp_peers)
    sends = Sends(send_sem)
    fill_order(perm)
    x_load.wait()
    reorder(x_held, mine, perm)

    def slice_of(q, place_z, core):
        return xv.at[q, rows_of(place_z, core)]

    def spread(q, place_z, up, down, core):
        ref = lambda: slice_of(q, place_z, c)
        recv = xg_sem.at[q, place_z * 2 + c]
        for name, when in (("up", up), ("down", down), ("core", core)):
            if when is not False:
                sends.start(ref, ref, recv, who[name], when)

    spread(1, z, z < depth - 1, z > 0, None)
    sends.start(lambda: mine, lambda: xv.at[0, rows_of(z, c)], xg_sem.at[0, mp], who["x"])
    y_pieces, x_pieces = [], []

    def y_piece(n):
        ref = lambda: piece(n, dp)
        y_pieces.append(sends.start(ref, ref, w_sem.at[n, dp], who["y"]))

    def x_piece(n):
        x_pieces.append(
            sends.start(
                lambda: gb.at[n, pl.ds(0, slots)],
                lambda: piece(n, dp),
                w_sem.at[n, dp],
                who["x"],
            )
        )

    for i in range(2 * bands):
        n = i // 2
        w_load(i).wait()

        def cast(r, _, i=i, n=n):
            value = wf[i % 2, r].astype(jnp.bfloat16)
            if i % 2 == 0:
                wg[n][dp * slots + r] = value
            else:
                gb[n, r] = value
            return 0

        lax.fori_loop(0, slots, cast, 0)
        if i + 2 < 2 * bands:
            w_load(i + 2).start()
        if i == 0:
            y_piece(0)
    for name in ("x", "y", "xy"):
        sends.start(lambda: bias_ref, lambda: bg.at[dp], bg_sem.at[dp], who[name])
    bg[dp] = bias_ref[...]
    for load in c_loads:
        load.wait()
    reorder(c_held[0], cg.at[1], perm)
    reorder(c_held[1], hv.at[0], perm)
    keep_row = 1.0 - jnp.broadcast_to(res_ref[...], (16, length)).astype(jnp.float32)
    rg[1] = jnp.dot(keep_row.astype(jnp.bfloat16), perm[...], preferred_element_type=jnp.float32)[:1]
    sends.start(lambda: rg.at[1], lambda: rg.at[0], r_sem, who["x"])
    fill_tables(owners, table, table_v, table_sem, blocks, slots)
    for owner in (y * 2 + 1 - x, (1 - y) * 2 + x, (1 - y) * 2 + 1 - x):
        landed(bg.at[owner], bg_sem.at[owner], who["x"])
    lane_of = lax.broadcasted_iota(jnp.int32, (half, width), 1)
    row_of = lax.broadcasted_iota(jnp.int32, (half, width), 0)
    diagonal = lane_of == row_of + x * half
    for g in range(3):
        owner, rank = bias_rank(owners, blocks, g)
        held = bg[owner]
        line = jnp.zeros((1, width), jnp.float32)
        for r in range(3):
            line = jnp.where(rank == r, held[r : r + 1], line)
        line = line.astype(jnp.bfloat16).astype(jnp.float32)
        column = jnp.sum(jnp.where(diagonal, line, 0.0), axis=1, keepdims=True)
        bcol[pl.ds(g * half, half), :] = jnp.broadcast_to(column, (half, LANES))
    bgrad[...] = jnp.zeros_like(bgrad)
    squares[...] = jnp.zeros_like(squares)

    def along_z(q, d):
        for at, on, on_z, device, up in (
            (z - d, z >= d, z < depth - 1, who["down"], True),
            (z + d, z + d < depth, z > 0, who["up"], False),
        ):

            @pl.when(on)
            def _(at=at, device=device):
                landed(slice_of(q, at, c), xg_sem.at[q, at * 2 + c], device)

            further = on & on_z
            spread(q, at, further if up else False, False if up else further, on)

    def pass_on(n):
        owner = y * 2 + 1 - x
        ref = lambda: piece(n, owner)
        landed(ref(), w_sem.at[n, owner], who["x"])
        if n + 1 < bands:
            x_piece(n + 1)
        y_pieces.append(sends.start(ref, ref, w_sem.at[n, owner], who["y"]))

    def arrange(n):
        for owner in ((1 - y) * 2 + x, (1 - y) * 2 + 1 - x):
            landed(piece(n, owner), w_sem.at[n, owner], who["y"])
        for h in range(2):
            for g in range(3):

                def one(k, _, h=h, g=g):
                    columns = pl.ds(pl.multiple_of(k * block_rows, block_rows), block_rows)
                    first = table[0, g * 2 * per_half + h * per_half + k]
                    wv[pl.ds((n * 6 + h * 3 + g) * band, band), columns] = wg[n][first]
                    return 0

                lax.fori_loop(0, per_half, one, 0)

    def from_core(q):
        for k in range(depth):
            landed(slice_of(q, k, 1 - c), xg_sem.at[q, k * 2 + 1 - c], who["core"])

    def project(q, first, number):
        def one(n, _):
            columns = pl.ds(pl.multiple_of(n * 256, 256), 256)
            at = pl.ds(first * 6 * band, number * 6 * band)
            p[at, columns] = jnp.dot(wv[at, :], xv[q, :, columns], preferred_element_type=jnp.float32)
            return 0

        lax.fori_loop(0, length // 256, one, 0)

    def gates(q, n):
        lane = lax.broadcasted_iota(jnp.int32, (tile, LANES), 1)
        keep = [
            jnp.broadcast_to(rg[q, :, pl.ds(v * LANES, LANES)], (tile, LANES))
            for v in range(groups)
        ]
        keep[0] = jnp.where(lane == 0, 0.0, keep[0])

        def one(i, _):
            off = pl.multiple_of(i * tile, tile)
            at = pl.ds(n * band + off, tile)

            def row(h, g):
                return pl.ds((n * 6 + h * 3 + g) * band + off, tile)

            def h_at(v, value):
                hv[q, at, pl.ds(v * LANES, LANES)] = value.astype(jnp.bfloat16)

            def joined_at(h, g, v, value):
                jv[row(h, g), pl.ds(q * length + v * LANES, LANES)] = value

            def add_bias(value):
                bgrad[at, :] += value

            gate_tile(
                p,
                lambda h, g, v: p[row(h, g), pl.ds(v * LANES, LANES)],
                lambda g: bcol[pl.ds(g * half + n * band + off, tile), :],
                keep,
                lambda v: cg[q, at, pl.ds(v * LANES, LANES)].astype(jnp.float32),
                h_at,
                joined_at,
                add_bias,
            )
            return 0

        lax.fori_loop(0, band // tile, one, 0)

    def weight_grad(n):
        at = pl.ds(n * 6 * band, 6 * band)
        both = (((1,), (1,)), ((), ()))

        def one(k, _):
            rows = pl.ds(pl.multiple_of(k * block_rows, block_rows), block_rows)
            total = lax.dot_general(
                jv[at, pl.ds(0, length)], xv[0, rows, :], both, preferred_element_type=jnp.float32
            )
            total += lax.dot_general(
                jv[at, pl.ds(length, length)], xv[1, rows, :], both, preferred_element_type=jnp.float32
            )
            total = total.astype(jnp.bfloat16)
            for i in range(6):
                gb[n, k * 6 + i] = total[i * band : (i + 1) * band]
            return 0

        lax.fori_loop(0, per_half, one, 0)

        for q in range(2):

            def pack(r, _, q=q):
                ref, row = reused(n * 2 + q, True)
                ref[row + r] = gb[n, table[8, ((1 - y) * 2 + owner_x[q]) * slots + r]]
                return 0

            lax.fori_loop(0, slots, pack, 0)

    def y_send(t):
        sends.start(
            lambda: reused_at(t, True),
            lambda: reused_at(t, False),
            y_sem.at[t],
            who["y"],
        )

    def input_grad(q):
        def one(k, _):
            columns = pl.ds(pl.multiple_of(k * 256, 256), 256)
            ig[q, columns, :] = lax.dot_general(
                wv[:, columns],
                jv[:, pl.ds(q * length, length)],
                (((0,), (0,)), ((), ())),
                preferred_element_type=jnp.float32,
            ).astype(jnp.bfloat16)
            return 0

        lax.fori_loop(0, full // 256, one, 0)
        for k in range(depth):
            sends.start(
                lambda k=k: ig.at[q, rows_of(k, 1 - c)],
                lambda k=k: core_got.at[q, k],
                core_sem.at[q, k],
                who["core"],
            )

    def add_tiles(refs):
        def one(i, _):
            at = pl.ds(pl.multiple_of(i * tile, tile), tile)
            total = refs[0][at, :].astype(jnp.float32)
            for ref in refs[1:]:
                total += ref[at, :].astype(jnp.float32)
            refs[0][at, :] = total.astype(jnp.bfloat16)
            return 0

        lax.fori_loop(0, width // tile, one, 0)

    def z_send_of(q, dest, got, recv, device, sem):
        return pltpu.make_async_remote_copy(
            src_ref=ig.at[q, rows_of(dest, c)],
            dst_ref=got.at[q, dest],
            send_sem=sem,
            recv_sem=recv.at[q, dest],
            device_id=device,
            device_id_type=MESH_ID,
        )

    mid = depth // 2 - 1
    up_items = [(0, d) for d in range(depth - 1, 0, -1) if d != mid]
    up_items += [(1, d) for d in range(depth - 1, 0, -1)]
    down_items = [(0, d) for d in range(depth - 1) if d != mid]
    down_items += [(1, d) for d in range(depth - 1)]

    def z_tick(t):
        for index, (items, after, got, recv, source, target) in enumerate(
            (
                (up_items, z, up_got, up_sem, who["down"], who["up"]),
                (down_items, depth - 1 - z, down_got, down_sem, who["up"], who["down"]),
            )
        ):
            item = t - after
            q = jnp.int32(0)
            dest = jnp.int32(0)
            earlier = jnp.int32(0)
            on = item < 0
            for i, (q_of, dest_of) in enumerate(items):
                goes = z < dest_of if index == 0 else z > dest_of
                q = jnp.where(item == i, q_of, q)
                dest = jnp.where(item == i, dest_of, dest)
                earlier += (goes & (item > i)).astype(jnp.int32)
                on = (on & (item != i)) | (goes & (item == i))
            on = on & (item >= 0) & (item < len(items))

            @pl.when(on)
            def _(index=index, after=after, got=got, recv=recv, source=source, target=target, q=q, dest=dest, earlier=earlier):
                landed(core_got.at[q, dest], core_sem.at[q, dest], who["core"])
                mine = ig.at[q, rows_of(dest, c)]

                @pl.when(after == 0)
                def _():
                    add_tiles((mine, core_got.at[q, dest]))

                @pl.when(after > 0)
                def _():
                    landed(got.at[q, dest], recv.at[q, dest], source)
                    add_tiles((mine, core_got.at[q, dest], got.at[q, dest]))

                send = z_send_of(q, dest, got, recv, target, z_send.at[index, lax.rem(earlier, 2)])

                @pl.when(earlier > 1)
                def _():
                    send.wait_send()

                send.start()

    def x_first():
        mine = ig.at[0, rows_of(mid, c)]
        landed(core_got.at[0, mid], core_sem.at[0, mid], who["core"])
        add_tiles((mine, core_got.at[0, mid]))
        sends.start(lambda: mine, lambda: up_got.at[0, mid], up_sem.at[0, mid], who["x"])

    def x_first_got():
        landed(up_got.at[0, mid], up_sem.at[0, mid], who["x"])
        add_tiles((ig.at[1, rows_of(mid, c)], up_got.at[0, mid]))

    def z_last(q):
        mine = ig.at[q, rows_of(z, c)]
        core = core_got.at[q, z]

        def joint(when, extra, above, below):
            @pl.when(when)
            def _():
                landed(core, core_sem.at[q, z], who["core"])
                refs = (mine, core)
                if extra:
                    landed(x_got, ix_sem, who["x"])
                    refs += (x_got,)
                if below:
                    landed(up_got.at[q, z], up_sem.at[q, z], who["down"])
                    refs += (up_got.at[q, z],)
                if above:
                    landed(down_got.at[q, z], down_sem.at[q, z], who["up"])
                    refs += (down_got.at[q, z],)
                add_tiles(refs)

        extra = q == 1
        joint(z == 0, extra, True, False)
        joint(z == depth - 1, extra, False, True)
        joint((z > 0) & (z < depth - 1) & (z != mid), extra, True, True)
        if q == 1:
            joint(z == mid, False, True, True)
            restore(mine, x_got, perm)
            copy = pltpu.make_async_copy(x_got, ig_out, own_sem.at[1])
            copy.start()
            own_copies.append(copy)
        else:
            sends.start(lambda: mine, lambda: x_got, ix_sem, who["x"], z != mid)

    own_copies = []

    def own_chunk(t):
        n, q = t // 2, t % 2
        landed(reused_at(t, False), y_sem.at[t], who["y"])
        ref, row = reused(t, False)
        if t + 2 < 2 * bands:
            y_send(t + 2)
        owner = y * 2 + owner_x[q]

        def one(r, _):
            valid = jnp.broadcast_to(r < table[1, owner], (band, block_rows))
            total = gb[n, table[8, owner * slots + r]].astype(jnp.float32)
            total += ref[row + r].astype(jnp.float32)
            total = jnp.where(valid, total, 0.0)
            ref[row + r] = total.astype(jnp.bfloat16)
            squares[...] += jnp.sum((total * total).reshape(band // 8, 8, block_rows), axis=0)
            return 0

        lax.fori_loop(0, slots, one, 0)
        src = lambda: reused_at(t, False)
        dst = lambda: gt.at[:, pl.ds(pl.multiple_of(x * half + n * band, 16), band)]
        if q == 0:
            sends.start(src, dst, x_sem.at[n], who["x"])
        else:
            copy = pltpu.make_async_copy(src(), dst(), own_sem.at[2 + n])
            copy.start()
            own_copies.append(copy)

    def bias_sum():
        landed(b_got.at[0], b_sem.at[0], who["y"])
        total = bgrad[...] + b_got[0]
        b_got[1] = total
        bt[x] = total
        sends.start(lambda: b_got.at[1], lambda: bt.at[x], b_sem.at[1], who["x"])
        counted = jnp.broadcast_to(y == 0, (half, LANES))
        each = jnp.where(counted, total * total, 0.0)
        squares[:, pl.ds(0, LANES)] += jnp.sum(each.reshape(half // 8, 8, LANES), axis=0)

    landed(xv.at[0, rows_of(z, c)], xg_sem.at[0, mp], who["x"])
    spread(0, z, z < depth - 1, z > 0, None)
    cot_sent = sends.start(lambda: hv.at[0], lambda: cg.at[0], c_sem, who["x"])
    x_piece(0)
    y_piece(1)
    for d in range(1, depth):
        along_z(0, d)
        if d == 1:
            y_piece(2)
        if d <= 2:
            pass_on(d - 1)
    along_z(1, 1)
    landed(cg.at[0], c_sem, who["x"])
    landed(rg.at[0], r_sem, who["x"])
    sends.wait([cot_sent])
    from_core(0)
    def layer_part(q, n):
        project(q, n, 1)
        gates(q, n)

    def give_part(n):
        weight_grad(n)
        if n == 0:
            pl.semaphore_wait(free_sem, 1)
            y_send(0)
            y_send(1)

    chunks = 2 * bands
    ticks = 2 * depth - 3
    arrange(0)
    layer_part(0, 0)
    pass_on(2)
    along_z(1, 2)
    arrange(1)
    layer_part(0, 1)
    along_z(1, 3)
    arrange(2)
    sends.wait(y_pieces + x_pieces)
    pl.semaphore_signal(free_sem, inc=1, device_id=who["y"], device_id_type=MESH_ID)
    from_core(1)
    layer_part(1, 0)
    give_part(0)
    layer_part(0, 2)
    input_grad(0)
    project(1, 1, 1)
    x_first()
    z_tick(0)
    gates(1, 1)
    give_part(1)
    z_tick(1)
    layer_part(1, 2)
    give_part(2)
    sends.start(lambda: bgrad, lambda: b_got.at[0], b_sem.at[0], who["y"])
    own_chunk(0)
    input_grad(1)
    x_first_got()
    z_tick(2)
    for q in (0, 1):
        restore(hv.at[q], cg.at[q], perm)
    sends.start(lambda: cg.at[0], lambda: h_out.at[part(x)], h_sem, who["x"])
    h_own = pltpu.make_async_copy(cg.at[1], h_out.at[part(x)], own_sem.at[0])
    h_own.start()
    own_copies.append(h_own)
    bias_sum()
    own_chunk(1)
    own_chunk(2)
    z_last(0)
    for t in range(depth - 1, ticks):
        z_tick(t)
        own_chunk(t)
    for t in range(ticks, chunks):
        own_chunk(t)
    total = squares[:, pl.ds(0, LANES)] + squares[:, pl.ds(LANES, LANES)]
    s_got[mp] = total
    for device in mp_peers:
        sends.start(lambda: s_got.at[mp], lambda: s_got.at[mp], s_sem.at[mp], device)
    for device in mp_peers:
        landed(s_got.at[device[1]], s_sem.at[device[1]], device)
    total = s_got[0]
    for k in range(1, 2 * depth):
        total = total + s_got[k]
    t_got[dp] = total
    for device in dp_peers:
        sends.start(lambda: t_got.at[dp], lambda: t_got.at[dp], t_sem.at[dp], device)
    z_last(1)
    for device in dp_peers:
        landed(t_got.at[device[0]], t_sem.at[device[0]], device)
    total = t_got[0]
    for k in range(1, 4):
        total = total + t_got[k]
    norm[...] = jnp.broadcast_to(jnp.sqrt(jnp.sum(total, keepdims=True)), norm.shape)
    for n in range(bands):
        landed(gt.at[:, pl.ds(pl.multiple_of((1 - x) * half + n * band, 16), band)], x_sem.at[n], who["x"])
    landed(h_out.at[part(1 - x)], h_sem, who["x"])
    landed(bt.at[1 - x], b_sem.at[1], who["x"])

    @pl.when(z < depth - 1)
    def _():
        for k in range(2):
            z_send_of(1, z + 1, up_got, up_sem, who["up"], z_send.at[0, k]).wait_send()

    @pl.when(z > 0)
    def _():
        for k in range(2):
            z_send_of(1, z - 1, down_got, down_sem, who["down"], z_send.at[1, k]).wait_send()

    for copy in own_copies:
        copy.wait()
    sends.finish()


def adam_turn(weights, first, second, grad, decay_rate):
    rate = (2.0 * D) ** (-0.5)
    first_new = 0.9 * first + 0.1 * grad
    second_new = 0.999 * second + (0.001 * grad) * grad
    second_hat = second_new * (1.0 / (1.0 - 0.999**STEP))
    root = second_hat * lax.rsqrt(jnp.maximum(second_hat, 1e-37)) + 1e-08
    turn = pl.reciprocal(root, approx=True)
    turn = turn * (2.0 - root * turn)
    step = (first_new * (rate / (1.0 - 0.9**STEP))) * turn
    return (weights * (1.0 - rate * decay_rate) - step, first_new, second_new)


def adam_kernel(
    owners, norm, bt, bw, bm, bv, g, w, m, v,
    w_new, m_new, v_new, bw_new, bm_new, bv_new,
    g_held, held, made, in_sem, out_sem,
):
    deep, rows, width, block_rows = g_held.shape
    stages = made.shape[1]
    turns = g.shape[0] // rows
    half = width // 2
    blocks = owners.shape[0] - 3
    me = lax.axis_index("dp")

    def taken(i):
        slot = lax.rem(i, deep)
        at = pl.ds(i * rows, rows)
        copies = [pltpu.make_async_copy(g.at[at], g_held.at[slot], in_sem.at[slot, 3])]
        for k, ref in enumerate((w, m, v)):
            copies.append(pltpu.make_async_copy(ref.at[at], held.at[k, slot], in_sem.at[slot, k]))
        return copies

    def given(i):
        slot = lax.rem(i, stages)
        at = pl.ds(i * rows, rows)
        return [
            pltpu.make_async_copy(made.at[k, slot], ref.at[at], out_sem.at[slot, k])
            for k, ref in enumerate((w_new, m_new, v_new))
        ]

    for i in range(min(deep, turns)):
        for copy in taken(jnp.int32(i)):
            copy.start()
    number = jnp.int32(0)
    for j in range(blocks):
        number += (owners[j] == me).astype(jnp.int32)
    factor = 1.0 / jnp.maximum(norm[:1, :1], 1.0)
    lane_of = lax.broadcasted_iota(jnp.int32, (half, width), 1)
    row_of = lax.broadcasted_iota(jnp.int32, (half, width), 0)
    row = lax.broadcasted_iota(jnp.int32, (3, width), 0)
    grads = jnp.zeros((3, width), jnp.float32)
    filled = jnp.zeros((3, width), jnp.int32)
    for gate in range(3):
        owner, rank = bias_rank(owners, blocks, gate)
        line = jnp.zeros((1, width), jnp.float32)
        for h in range(2):
            column = bt[h][:, gate : gate + 1]
            line += jnp.sum(
                jnp.where(lane_of == row_of + h * half, column, 0.0), axis=0, keepdims=True
            )
        here = (row == rank) & jnp.broadcast_to(owner == me, (3, width))
        grads = jnp.where(here, line, grads)
        filled = jnp.where(here, 1, filled)
    news = adam_step(bw[...], bm[...], bv[...], grads * factor, 0.0)
    for ref, new in zip((bw_new, bm_new, bv_new), news):
        ref[...] = jnp.where(filled > 0, new, 0.0)

    def turn(i, _):
        slot, stage = lax.rem(i, deep), lax.rem(i, stages)
        for copy in taken(i):
            copy.wait()

        @pl.when(i >= stages)
        def _():
            for copy in given(i - stages):
                copy.wait()

        for r in range(rows):
            grad = g_held[slot, r].astype(jnp.float32) * factor
            valid = jnp.broadcast_to(i * rows + r < number, (width, block_rows))
            news = adam_turn(held[0, slot, r], held[1, slot, r], held[2, slot, r], grad, 0.1)
            for k, new in enumerate(news):
                made[k, stage, r] = jnp.where(valid, new, 0.0)
        for copy in given(i):
            copy.start()

        @pl.when(i + deep < turns)
        def _():
            for copy in taken(i + deep):
                copy.start()

        return 0

    lax.fori_loop(0, turns, turn, 0)
    for i in range(max(0, turns - stages), turns):
        for copy in given(jnp.int32(i)):
            copy.wait()


def paired(
    inputs, resets, owners, kernel, kernel_first, kernel_second, bias_rows, bias_first, bias_second, cotangent
):
    _, width, length = inputs.shape
    slots, _, block_rows = kernel.shape
    blocks = owners.shape[0] - 3
    full = width * lax.axis_size("mp")
    depth = lax.axis_size("mp") // 2
    half = width // 2
    bf16, f32 = jnp.bfloat16, jnp.float32
    shape = jax.ShapeDtypeStruct
    hbm = pl.BlockSpec(memory_space=pltpu.MemorySpace.HBM)
    vmem = pl.BlockSpec(memory_space=pltpu.VMEM)
    smem = pl.BlockSpec(memory_space=pltpu.SMEM)
    dma = pltpu.SemaphoreType.DMA
    band = half // BANDS
    gt, h_new, ig, bt, norm = pl.pallas_call(
        layer_kernel,
        out_shape=(
            shape((slots, width, block_rows), bf16),
            shape((width, length), bf16),
            shape((width, length), bf16),
            shape((2, half, LANES), f32),
            shape((8, LANES), f32),
        ),
        in_specs=[smem] + [hbm] * 3 + [vmem] * 2,
        out_specs=[hbm, hbm, hbm, vmem, vmem],
        scratch_shapes=[
            pltpu.SMEM((16, LANES), jnp.int32),
            pltpu.VMEM((16, LANES), jnp.int32),
            pltpu.VMEM((2, slots, band, block_rows), f32),
            pltpu.VMEM((4 * slots, band, block_rows), bf16),
            pltpu.VMEM((4 * slots, band, block_rows), bf16),
            pltpu.VMEM((4 * slots, band, block_rows), bf16),
            pltpu.VMEM((6 * half, full), bf16),
            pltpu.VMEM((2, full, length), bf16),
            pltpu.VMEM((2, half, length), bf16),
            pltpu.VMEM((2, 1, length), f32),
            pltpu.VMEM((4, 3, width), f32),
            pltpu.VMEM((2, half, length), bf16),
            pltpu.VMEM((6 * half, length), f32),
            pltpu.VMEM((6 * half, 2 * length), bf16),
            pltpu.VMEM((BANDS, blocks, band, block_rows), bf16),
            pltpu.VMEM((3 * half, LANES), f32),
            pltpu.VMEM((half, LANES), f32),
            pltpu.VMEM((length, length), bf16),
            pltpu.VMEM((2, full, length), bf16),
            pltpu.VMEM((2, depth, width, length), bf16),
            pltpu.VMEM((2, depth, width, length), bf16),
            pltpu.VMEM((2, depth, width, length), bf16),
            pltpu.VMEM((width, length), bf16),
            pltpu.VMEM((2, half, LANES), f32),
            pltpu.VMEM((8, block_rows), f32),
            pltpu.VMEM((2 * depth, 8, LANES), f32),
            pltpu.VMEM((4, 8, LANES), f32),
            dma((5,)),
            dma((2,)),
            dma((2 + BANDS,)),
            dma((96,)),
            dma((BANDS, 4)),
            dma((2, 2 * depth)),
            dma,
            dma,
            dma((4,)),
            dma((2 * BANDS,)),
            dma((BANDS,)),
            dma((2, depth)),
            dma((2, depth)),
            dma((2, depth)),
            dma((2, 2)),
            dma,
            dma,
            dma((2,)),
            dma((2 * depth,)),
            dma((4,)),
            pltpu.SemaphoreType.REGULAR,
        ],
        compiler_params=pltpu.CompilerParams(
            collective_id=0, has_side_effects=True, vmem_limit_bytes=VMEM
        ),
        name="layer",
    )(
        owners,
        kernel,
        inputs.reshape(width, length),
        cotangent.reshape(width, length),
        resets,
        bias_rows,
    )
    rows = 1
    news = pl.pallas_call(
        adam_kernel,
        out_shape=(shape(kernel.shape, f32),) * 3 + (shape(bias_rows.shape, f32),) * 3,
        in_specs=[smem] + [vmem] * 5 + [hbm] * 4,
        out_specs=[hbm] * 3 + [vmem] * 3,
        scratch_shapes=[
            pltpu.VMEM((DEEP, rows, width, block_rows), bf16),
            pltpu.VMEM((3, DEEP, rows, width, block_rows), f32),
            pltpu.VMEM((3, STAGES, rows, width, block_rows), f32),
            dma((DEEP, 4)),
            dma((STAGES, 3)),
        ],
        compiler_params=pltpu.CompilerParams(vmem_limit_bytes=VMEM),
        name="adam",
    )(owners, norm, bt, bias_rows, bias_first, bias_second, gt, kernel, kernel_first, kernel_second)
    kernel_w, kernel_m, kernel_v, bias_w, bias_m, bias_v = news
    return (h_new[None], ig[None], kernel_w, kernel_m, kernel_v, bias_w, bias_m, bias_v, norm[0, 0])


def solution(mesh):
    placed = (
        P("dp", "mp", None),
        P("dp", None),
        P(),
        P("dp", "mp", None),
        P("dp", "mp", None),
        P("dp", "mp", None),
        P("dp", "mp"),
        P("dp", "mp"),
        P("dp", "mp"),
        P("dp", "mp", None),
    )
    fits = mesh.shape["dp"] == 4 and mesh.shape["mp"] == 8
    return jax.shard_map(
        paired if fits else shards,
        mesh=mesh,
        in_specs=placed,
        out_specs=(
            P("dp", "mp", None),
            P("dp", "mp", None),
            P("dp", "mp", None),
            P("dp", "mp", None),
            P("dp", "mp", None),
            P("dp", "mp"),
            P("dp", "mp"),
            P("dp", "mp"),
            P(),
        ),
        check_vma=False,
    )
```

```python
import jax
import jax.numpy as jnp
from jax import lax
from jax.experimental import pallas as pl
from jax.experimental.pallas import tpu as pltpu
from jax.sharding import PartitionSpec as P

D = 2304
STEP = 10


def earlier_count(owned):
    number = owned.shape[0]
    places = jnp.arange(number, dtype=jnp.int32)
    earlier = (owned[:, None] == owned[None, :]) & (places[None, :] < places[:, None])
    return jnp.sum(earlier.astype(jnp.int32), axis=1)


def slot_sources(slot, count):
    places = jnp.arange(slot.shape[0], dtype=jnp.int32)
    hits = slot[None, :] == jnp.arange(count, dtype=jnp.int32)[:, None]
    source = jnp.sum(jnp.where(hits, places[None, :], 0), axis=1)
    return (source, jnp.any(hits, axis=1).astype(jnp.float32))


def shift_later(values):
    return jnp.pad(values, ((0, 0), (0, 0), (1, 0)))[:, :, :-1]


def shift_earlier(values):
    return jnp.pad(values, ((0, 0), (0, 0), (0, 1)))[:, :, 1:]


def combine(earlier, later):
    return (earlier[0] * later[0], later[0] * earlier[1] + later[1])


def pooled(preact, keeping):
    channels = preact.shape[1] // 3
    candidate = jnp.tanh(preact[:, :channels])
    forget = jax.nn.sigmoid(preact[:, channels : 2 * channels])
    output_gate = jax.nn.sigmoid(preact[:, 2 * channels :])
    decay = forget * keeping[:, None, :]
    _, cells = lax.associative_scan(combine, (decay, (1.0 - forget) * candidate), axis=2)
    return output_gate * cells


def adam_step(weights, first, second, grad, decay_rate):
    rate = (2.0 * D) ** (-0.5)
    first_new = 0.9 * first + 0.1 * grad
    second_new = 0.999 * second + 0.001 * grad * grad
    first_hat = first_new / (1.0 - 0.9**STEP)
    second_hat = second_new / (1.0 - 0.999**STEP)
    weights_new = weights - rate * (
        first_hat / (jnp.sqrt(second_hat) + 1e-08) + decay_rate * weights
    )
    return (weights_new, first_new, second_new)


def shards(
    inputs,
    resets,
    owners,
    kernel,
    kernel_first,
    kernel_second,
    bias_rows,
    bias_first,
    bias_second,
    cotangent,
):
    streams, local_width, length = inputs.shape
    slots_own, _, block_rows = kernel.shape
    block_count = owners.shape[0] - 3
    dp_size = lax.axis_size("dp")
    dp_index = lax.axis_index("dp")
    kernel_owner = owners[:block_count]
    bias_owner = owners[block_count:]
    kernel_slot = kernel_owner * slots_own + earlier_count(kernel_owner)
    bias_slot = bias_owner * 3 + earlier_count(bias_owner)
    all_kernel, all_bias = (
        lax.all_gather(kernel.astype(jnp.bfloat16), "dp", axis=0, tiled=True),
        lax.all_gather(bias_rows.astype(jnp.bfloat16), "dp", axis=0, tiled=True),
    )
    per_gate = block_count // 3
    double_width = per_gate * block_rows
    full_width = double_width // 2
    gate_cols = 3 * local_width
    arranged = (
        all_kernel[kernel_slot]
        .reshape(3, per_gate, local_width, block_rows)
        .transpose(0, 2, 1, 3)
        .reshape(gate_cols, double_width)
    )
    paired_t = jnp.concatenate([arranged[:, :full_width], arranged[:, full_width:]], axis=0)
    bias_vec = all_bias[bias_slot].astype(jnp.float32).reshape(gate_cols)
    rows = paired_t
    projected = jnp.einsum(
        "ok,skl->sol",
        rows,
        lax.all_gather(inputs, "mp", axis=1, tiled=True),
        preferred_element_type=jnp.float32,
    )
    preact = (
        projected[:, :gate_cols] + shift_later(projected[:, gate_cols:]) + bias_vec[None, :, None]
    )
    keeping = (1 - resets).astype(jnp.float32)
    result, pullback = jax.vjp(lambda values: pooled(values, keeping), preact)
    pre_grad = pullback(cotangent.astype(jnp.float32))[0].astype(jnp.bfloat16)
    joined = jnp.concatenate([pre_grad, shift_earlier(pre_grad)], axis=1)
    bias_grad = jnp.sum(pre_grad.astype(jnp.float32), axis=(0, 2)).reshape(3, local_width)
    pair_grad = jnp.einsum(
        "sol,skl->ok",
        joined,
        lax.all_gather(inputs, "mp", axis=1, tiled=True),
        preferred_element_type=jnp.float32,
    )
    rows = paired_t
    term_rows = lax.psum_scatter(
        jnp.einsum("ok,sol->ksl", rows, joined, preferred_element_type=jnp.float32),
        "mp",
        scatter_dimension=0,
        tiled=True,
    )
    input_grads = jnp.transpose(term_rows.astype(jnp.bfloat16), (1, 0, 2))
    block_grad = pair_grad.reshape(2, 3, local_width, full_width).transpose(1, 2, 0, 3)
    block_grad = (
        block_grad.reshape(3, local_width, per_gate, block_rows)
        .transpose(0, 2, 1, 3)
        .reshape(block_count, local_width, block_rows)
    )
    kernel_source, kernel_valid = slot_sources(kernel_slot, dp_size * slots_own)
    bias_source, bias_valid = slot_sources(bias_slot, dp_size * 3)
    own_kernel_valid = lax.dynamic_slice_in_dim(kernel_valid, dp_index * slots_own, slots_own)
    own_bias_valid = lax.dynamic_slice_in_dim(bias_valid, dp_index * 3, 3)
    total_kernel, total_bias = lax.psum((block_grad, bias_grad), "dp")
    own_kernel_source = lax.dynamic_slice_in_dim(kernel_source, dp_index * slots_own, slots_own)
    own_bias_source = lax.dynamic_slice_in_dim(bias_source, dp_index * 3, 3)
    own_kernel = total_kernel[own_kernel_source] * own_kernel_valid[:, None, None]
    own_bias = total_bias[own_bias_source] * own_bias_valid[:, None]
    squares = jnp.sum(own_kernel * own_kernel) + jnp.sum(own_bias * own_bias)
    grad_norm = jnp.sqrt(lax.psum(squares, ("dp", "mp")))
    factor = 1.0 / jnp.maximum(grad_norm, 1.0)
    kernel_w, kernel_m, kernel_v = adam_step(
        kernel, kernel_first, kernel_second, own_kernel * factor, 0.1
    )
    bias_w, bias_m, bias_v = adam_step(bias_rows, bias_first, bias_second, own_bias * factor, 0.0)
    kernel_mask = own_kernel_valid[:, None, None] > 0.5
    bias_mask = own_bias_valid[:, None] > 0.5
    return (
        result.astype(jnp.bfloat16),
        input_grads,
        jnp.where(kernel_mask, kernel_w, 0.0),
        jnp.where(kernel_mask, kernel_m, 0.0),
        jnp.where(kernel_mask, kernel_v, 0.0),
        jnp.where(bias_mask, bias_w, 0.0),
        jnp.where(bias_mask, bias_m, 0.0),
        jnp.where(bias_mask, bias_v, 0.0),
        grad_norm,
    )


MESH_ID = pl.DeviceIdType.MESH
LANES = 128
BANDS = 3
IM = 768
IN = 512
DEEP = 8
STAGES = 4
VMEM = 61 * 2**20


def place():
    dp, mp = lax.axis_index("dp"), lax.axis_index("mp")
    return dp // 2, lax.rem(dp, 2), mp // 2, lax.rem(mp, 2)


def partners(y, x, z, c):
    dp, mp = y * 2 + x, z * 2 + c
    return {
        "x": (y * 2 + 1 - x, mp),
        "y": ((1 - y) * 2 + x, mp),
        "xy": ((1 - y) * 2 + 1 - x, mp),
        "core": (dp, z * 2 + 1 - c),
        "up": (dp, mp + 2),
        "down": (dp, mp - 2),
    }


def greet(devices):
    barrier = pltpu.get_barrier_semaphore()
    for device in devices:
        pl.semaphore_signal(barrier, inc=1, device_id=device, device_id_type=MESH_ID)
    pl.semaphore_wait(barrier, len(devices))


class Sends:
    def __init__(self, sems):
        self.sems, self.number, self.made = sems, 0, {}

    def start(self, src, dst, recv, device, when=None):
        slot = self.number
        self.number += 1

        def build():
            return pltpu.make_async_remote_copy(
                src_ref=src(),
                dst_ref=dst(),
                send_sem=self.sems.at[slot],
                recv_sem=recv,
                device_id=device,
                device_id_type=MESH_ID,
            )

        if when is None:
            build().start()
        else:
            pl.when(when)(lambda: build().start())
        self.made[slot] = (build, when)
        return slot

    def wait(self, slots):
        for slot in slots:
            build, when = self.made.pop(slot)
            if when is None:
                build().wait_send()
            else:
                pl.when(when)(lambda build=build: build().wait_send())

    def finish(self):
        self.wait(list(self.made))


def landed(ref, sem, device):
    pltpu.make_async_remote_copy(
        src_ref=ref, dst_ref=ref, send_sem=sem, recv_sem=sem, device_id=device, device_id_type=MESH_ID
    ).wait_recv()


def fill_order(perm):
    length = perm.shape[0]
    tile = 16
    column = lax.broadcasted_iota(jnp.int32, (tile, length), 1)
    wanted = lax.rem(column, LANES) * (length // LANES) + column // LANES
    wanted = wanted - lax.broadcasted_iota(jnp.int32, (tile, length), 0)

    def one(i, _):
        at = pl.ds(pl.multiple_of(i * tile, tile), tile)
        perm[at, :] = jnp.where(wanted == i * tile, 1.0, 0.0).astype(jnp.bfloat16)
        return 0

    lax.fori_loop(0, length // tile, one, 0)


def reorder(src, dst, perm):
    def one(i, _):
        at = pl.ds(pl.multiple_of(i * 256, 256), 256)
        moved = jnp.dot(src[...], perm[:, at], preferred_element_type=jnp.float32)
        dst[:, at] = moved.astype(dst.dtype)
        return 0

    lax.fori_loop(0, perm.shape[1] // 256, one, 0)


def restore(src, dst, perm):
    def one(i, _):
        at = pl.ds(pl.multiple_of(i * 256, 256), 256)
        moved = lax.dot_general(
            src[...], perm[at, :], (((1,), (1,)), ((), ())), preferred_element_type=jnp.float32
        )
        dst[:, at] = moved.astype(dst.dtype)
        return 0

    lax.fori_loop(0, perm.shape[0] // 256, one, 0)


def bias_rank(owners, blocks, g):
    owner = owners[blocks + g]
    rank = jnp.int32(0)
    for h in range(g):
        rank += (owners[blocks + h] == owner).astype(jnp.int32)
    return owner, rank


def sigmoid(v):
    return 0.5 * jnp.tanh(0.5 * v) + 0.5


def later(values):
    return [pltpu.roll(values[-1], 1, 1)] + values[:-1]


def scan_both(decay, fresh, source):
    groups = len(decay)
    held, gain = [fresh[0]], [decay[0]]
    for v in range(1, groups):
        held.append(fresh[v] + decay[v] * held[-1])
        gain.append(decay[v] * gain[-1])
    back, fall = [source[-1]], [None]
    for v in range(groups - 2, -1, -1):
        back.insert(0, source[v] + decay[v + 1] * back[0])
        fall.insert(0, decay[v + 1] if fall[0] is None else decay[v + 1] * fall[0])
    ahead = pltpu.roll(decay[0], LANES - 1, 1)
    level, factor = held[-1], gain[-1]
    behind, drop = back[0], fall[0] * ahead
    d = 1
    while d < LANES:
        level = level + factor * pltpu.roll(level, d, 1)
        behind = behind + drop * pltpu.roll(behind, LANES - d, 1)
        if 2 * d < LANES:
            factor = factor * pltpu.roll(factor, d, 1)
            drop = drop * pltpu.roll(drop, LANES - d, 1)
        d *= 2
    carry = pltpu.roll(level, 1, 1)
    cells = [held[v] + gain[v] * carry for v in range(groups)]
    carry = ahead * pltpu.roll(behind, LANES - 1, 1)
    dc = [back[v] + fall[v] * carry for v in range(groups - 1)] + [back[-1] + carry]
    return cells, dc


def gate_tile(pre_at, bias_at, keep, dh_at, h_at, joined_at, add_bias):
    groups = len(keep)
    lane = lax.broadcasted_iota(jnp.int32, keep[0].shape, 1)

    def pre(g):
        now = [pre_at(0, g, v) for v in range(groups)]
        before = later([pre_at(1, g, v) for v in range(groups)])
        before[0] = jnp.where(lane == 0, 0.0, before[0])
        bias = bias_at(g)
        return [n + b + bias for n, b in zip(now, before)]

    cand = [jnp.tanh(v) for v in pre(0)]
    forget = [sigmoid(v) for v in pre(1)]
    gate = [sigmoid(v) for v in pre(2)]
    decay = [f * k for f, k in zip(forget, keep)]
    dh = [dh_at(v) for v in range(groups)]
    cells, dc = scan_both(
        decay,
        [(1.0 - f) * z for f, z in zip(forget, cand)],
        [d * o for d, o in zip(dh, gate)],
    )
    for v in range(groups):
        h_at(v, gate[v] * cells[v])
    past = later(cells)
    grads = (
        [dc[v] * (1.0 - forget[v]) * (1.0 - cand[v] * cand[v]) for v in range(groups)],
        [
            dc[v] * (keep[v] * past[v] - cand[v]) * (forget[v] * (1.0 - forget[v]))
            for v in range(groups)
        ],
        [dh[v] * cells[v] * (gate[v] * (1.0 - gate[v])) for v in range(groups)],
    )
    for g in range(3):
        narrow = [value.astype(jnp.bfloat16) for value in grads[g]]
        wide = [value.astype(jnp.float32) for value in narrow]
        first = jnp.where(lane == LANES - 1, 0.0, pltpu.roll(wide[0], LANES - 1, 1))
        ahead = wide[1:] + [first]
        total = wide[0]
        for v in range(groups):
            joined_at(0, g, v, narrow[v])
            joined_at(1, g, v, ahead[v].astype(jnp.bfloat16))
            if v:
                total = total + wide[v]
        add_bias(jnp.where(lane == g, jnp.sum(total, axis=1, keepdims=True), 0.0))


def fill_tables(owners, table, table_v, sem, blocks, slots):
    per_half = blocks // 6
    down = lax.broadcasted_iota(jnp.int32, (64, LANES), 0)
    along = lax.broadcasted_iota(jnp.int32, (64, LANES), 1)

    def spell(j, both):
        owner = owners[j]
        return jnp.where(down == j, owner, both[0]), jnp.where(along == j, owner, both[1])

    start = (jnp.full((64, LANES), -1, jnp.int32), jnp.full((64, LANES), -2, jnp.int32))
    rows, columns = lax.fori_loop(0, blocks, spell, start)
    rank = jnp.sum(jnp.where((rows == columns) & (down < along), 1, 0), axis=0, keepdims=True)
    table_v[pl.ds(0, 1), :] = columns[:1] * slots + rank
    table_v[pl.ds(1, 1), :] = jnp.sum(jnp.where(rows == along, 1, 0), axis=0, keepdims=True)
    first = pltpu.make_async_copy(table_v.at[pl.ds(0, 8)], table.at[pl.ds(0, 8)], sem.at[0])
    first.start()
    first.wait()

    def place_of(j, held):
        stands = lax.rem(j, per_half) * 6 + lax.rem(j // per_half, 2) * 3 + j // (2 * per_half)
        return jnp.where(along[:1] == table[0, j], stands, held)

    table_v[pl.ds(8, 1), :] = lax.fori_loop(0, blocks, place_of, jnp.zeros((1, LANES), jnp.int32))
    second = pltpu.make_async_copy(table_v.at[pl.ds(8, 8)], table.at[pl.ds(8, 8)], sem.at[1])
    second.start()
    second.wait()


def layer_kernel(
    owners, w_ref, x_ref, cot_ref, res_ref, bias_ref,
    gt, h_out, ig_out, bt, norm,
    table, table_v, wf, wg0, wg1, wg2, wv, xv, cg, rg, bg, hv, p, jv, gb, bcol, bgrad, perm,
    ig, up_got, down_got, core_got, x_got, b_got, squares, s_got, t_got,
    load_sem, table_sem, own_sem, send_sem, w_sem, xg_sem, c_sem, r_sem, bg_sem,
    y_sem, x_sem, core_sem, up_sem, down_sem, z_send, ix_sem, h_sem, b_sem, s_sem, t_sem, free_sem,
):
    y, x, z, c = place()
    dp, mp = y * 2 + x, z * 2 + c
    who = partners(y, x, z, c)
    slots, width, block_rows = gt.shape
    half = width // 2
    length = h_out.shape[1]
    full = xv.shape[1]
    depth = full // width // 2
    per_half = full // block_rows
    blocks = 6 * per_half
    tile = 16
    groups = length // LANES
    wg = (wg0, wg1, wg2)
    band = wg0.shape[1]
    bands = half // band
    owner_x = (1 - x, x)
    mp_peers = [(dp, lax.rem(mp + r, 2 * depth)) for r in range(1, 2 * depth)]
    dp_peers = [who["x"], who["y"], who["xy"]]

    def part(index):
        return pl.ds(pl.multiple_of(index * half, half), half)

    def rows_of(place_z, core):
        return pl.ds(pl.multiple_of((place_z * 2 + core) * width, width), width)

    def piece(n, owner):
        return wg[n].at[pl.ds(owner * slots, slots)]

    def reused(t, give):
        row = (t + (2 * bands if give else 0)) * slots
        return wg[row // (4 * slots)], row % (4 * slots)

    def reused_at(t, give):
        ref, row = reused(t, give)
        return ref.at[pl.ds(row, slots)]

    mine = xv.at[1, rows_of(z, c)]
    x_held = jv.at[pl.ds(0, width), pl.ds(0, length)]
    c_held = [jv.at[pl.ds(width + i * half, half), pl.ds(0, length)] for i in range(2)]
    x_load = pltpu.make_async_copy(x_ref, x_held, load_sem.at[0])
    c_loads = [
        pltpu.make_async_copy(cot_ref.at[part(x)], c_held[0], load_sem.at[1]),
        pltpu.make_async_copy(cot_ref.at[part(1 - x)], c_held[1], load_sem.at[2]),
    ]

    def w_load(i):
        at = pl.multiple_of((x if i % 2 == 0 else 1 - x) * half + (i // 2) * band, 16)
        return pltpu.make_async_copy(
            w_ref.at[:, pl.ds(at, band)], wf.at[i % 2], load_sem.at[3 + i % 2]
        )

    x_load.start()
    w_load(0).start()
    w_load(1).start()
    for load in c_loads:
        load.start()
    greet(mp_peers + dp_peers)
    sends = Sends(send_sem)
    fill_order(perm)
    x_load.wait()
    reorder(x_held, mine, perm)

    def slice_of(q, place_z, core):
        return xv.at[q, rows_of(place_z, core)]

    def spread(q, place_z, up, down, core):
        ref = lambda: slice_of(q, place_z, c)
        recv = xg_sem.at[q, place_z * 2 + c]
        for name, when in (("up", up), ("down", down), ("core", core)):
            if when is not False:
                sends.start(ref, ref, recv, who[name], when)

    spread(1, z, z < depth - 1, z > 0, None)
    sends.start(lambda: mine, lambda: xv.at[0, rows_of(z, c)], xg_sem.at[0, mp], who["x"])
    y_pieces, x_pieces = [], []

    def y_piece(n):
        ref = lambda: piece(n, dp)
        y_pieces.append(sends.start(ref, ref, w_sem.at[n, dp], who["y"]))

    def x_piece(n):
        x_pieces.append(
            sends.start(
                lambda: gb.at[n, pl.ds(0, slots)],
                lambda: piece(n, dp),
                w_sem.at[n, dp],
                who["x"],
            )
        )

    for i in range(2 * bands):
        n = i // 2
        w_load(i).wait()

        def cast(r, _, i=i, n=n):
            value = wf[i % 2, r].astype(jnp.bfloat16)
            if i % 2 == 0:
                wg[n][dp * slots + r] = value
            else:
                gb[n, r] = value
            return 0

        lax.fori_loop(0, slots, cast, 0)
        if i + 2 < 2 * bands:
            w_load(i + 2).start()
        if i == 0:
            y_piece(0)
    for name in ("x", "y", "xy"):
        sends.start(lambda: bias_ref, lambda: bg.at[dp], bg_sem.at[dp], who[name])
    bg[dp] = bias_ref[...]
    for load in c_loads:
        load.wait()
    reorder(c_held[0], cg.at[1], perm)
    reorder(c_held[1], hv.at[0], perm)
    keep_row = 1.0 - jnp.broadcast_to(res_ref[...], (16, length)).astype(jnp.float32)
    rg[1] = jnp.dot(keep_row.astype(jnp.bfloat16), perm[...], preferred_element_type=jnp.float32)[:1]
    sends.start(lambda: rg.at[1], lambda: rg.at[0], r_sem, who["x"])
    fill_tables(owners, table, table_v, table_sem, blocks, slots)
    for owner in (y * 2 + 1 - x, (1 - y) * 2 + x, (1 - y) * 2 + 1 - x):
        landed(bg.at[owner], bg_sem.at[owner], who["x"])
    lane_of = lax.broadcasted_iota(jnp.int32, (half, width), 1)
    row_of = lax.broadcasted_iota(jnp.int32, (half, width), 0)
    diagonal = lane_of == row_of + x * half
    for g in range(3):
        owner, rank = bias_rank(owners, blocks, g)
        held = bg[owner]
        line = jnp.zeros((1, width), jnp.float32)
        for r in range(3):
            line = jnp.where(rank == r, held[r : r + 1], line)
        line = line.astype(jnp.bfloat16).astype(jnp.float32)
        column = jnp.sum(jnp.where(diagonal, line, 0.0), axis=1, keepdims=True)
        bcol[pl.ds(g * half, half), :] = jnp.broadcast_to(column, (half, LANES))
    bgrad[...] = jnp.zeros_like(bgrad)
    squares[...] = jnp.zeros_like(squares)

    def along_z(q, d):
        for at, on, on_z, device, up in (
            (z - d, z >= d, z < depth - 1, who["down"], True),
            (z + d, z + d < depth, z > 0, who["up"], False),
        ):

            @pl.when(on)
            def _(at=at, device=device):
                landed(slice_of(q, at, c), xg_sem.at[q, at * 2 + c], device)

            further = on & on_z
            spread(q, at, further if up else False, False if up else further, on)

    def pass_on(n):
        owner = y * 2 + 1 - x
        ref = lambda: piece(n, owner)
        landed(ref(), w_sem.at[n, owner], who["x"])
        if n + 1 < bands:
            x_piece(n + 1)
        y_pieces.append(sends.start(ref, ref, w_sem.at[n, owner], who["y"]))

    def arrange(n):
        for owner in ((1 - y) * 2 + x, (1 - y) * 2 + 1 - x):
            landed(piece(n, owner), w_sem.at[n, owner], who["y"])
        for h in range(2):
            for g in range(3):

                def one(k, _, h=h, g=g):
                    columns = pl.ds(pl.multiple_of(k * block_rows, block_rows), block_rows)
                    first = table[0, g * 2 * per_half + h * per_half + k]
                    wv[pl.ds((n * 6 + h * 3 + g) * band, band), columns] = wg[n][first]
                    return 0

                lax.fori_loop(0, per_half, one, 0)

    def from_core(q):
        for k in range(depth):
            landed(slice_of(q, k, 1 - c), xg_sem.at[q, k * 2 + 1 - c], who["core"])

    def project(q, n):
        rows = pl.ds(n * 6 * band, 6 * band)

        def one(i, _):
            columns = pl.ds(pl.multiple_of(i * 256, 256), 256)
            p[:, columns] = jnp.dot(wv[rows, :], xv[q, :, columns], preferred_element_type=jnp.float32)
            return 0

        lax.fori_loop(0, length // 256, one, 0)

    def gates(q, n):
        lane = lax.broadcasted_iota(jnp.int32, (band, LANES), 1)
        keep = [
            jnp.broadcast_to(rg[q, :, pl.ds(v * LANES, LANES)], (band, LANES))
            for v in range(groups)
        ]
        keep[0] = jnp.where(lane == 0, 0.0, keep[0])

        at = pl.ds(n * band, band)

        def row(h, g):
            return pl.ds((n * 6 + h * 3 + g) * band, band)

        def h_at(v, value):
            hv[q, at, pl.ds(v * LANES, LANES)] = value.astype(jnp.bfloat16)

        def joined_at(h, g, v, value):
            jv[row(h, g), pl.ds(q * length + v * LANES, LANES)] = value

        def add_bias(value):
            bgrad[at, :] += value

        gate_tile(
            lambda h, g, v: p[pl.ds((h * 3 + g) * band, band), pl.ds(v * LANES, LANES)],
            lambda g: bcol[pl.ds(g * half + n * band, band), :],
            keep,
            lambda v: cg[q, at, pl.ds(v * LANES, LANES)].astype(jnp.float32),
            h_at,
            joined_at,
            add_bias,
        )

    def weight_grad(n):
        at = pl.ds(n * 6 * band, 6 * band)
        both = (((1,), (1,)), ((), ()))

        def one(k, _):
            rows = pl.ds(pl.multiple_of(k * block_rows, block_rows), block_rows)
            total = lax.dot_general(
                jv[at, pl.ds(0, length)], xv[0, rows, :], both, preferred_element_type=jnp.float32
            )
            total += lax.dot_general(
                jv[at, pl.ds(length, length)], xv[1, rows, :], both, preferred_element_type=jnp.float32
            )
            total = total.astype(jnp.bfloat16)
            for i in range(6):
                gb[n, k * 6 + i] = total[i * band : (i + 1) * band]
            return 0

        lax.fori_loop(0, per_half, one, 0)

        for q in range(2):

            def pack(r, _, q=q):
                ref, row = reused(n * 2 + q, True)
                ref[row + r] = gb[n, table[8, ((1 - y) * 2 + owner_x[q]) * slots + r]]
                return 0

            lax.fori_loop(0, slots, pack, 0)

    def y_send(t):
        sends.start(
            lambda: reused_at(t, True),
            lambda: reused_at(t, False),
            y_sem.at[t],
            who["y"],
        )

    def input_grad(q):
        def one(i, _):
            columns = pl.ds(pl.multiple_of(i // (length // IN) * IM, IM), IM)
            lanes = pl.multiple_of(lax.rem(i, length // IN) * IN, IN)
            ig[q, columns, pl.ds(lanes, IN)] = lax.dot_general(
                wv[:, columns],
                jv[:, pl.ds(q * length + lanes, IN)],
                (((0,), (0,)), ((), ())),
                preferred_element_type=jnp.float32,
            ).astype(jnp.bfloat16)
            return 0

        lax.fori_loop(0, (full // IM) * (length // IN), one, 0)
        for k in range(depth):
            sends.start(
                lambda k=k: ig.at[q, rows_of(k, 1 - c)],
                lambda k=k: core_got.at[q, k],
                core_sem.at[q, k],
                who["core"],
            )

    def add_tiles(refs):
        def one(i, _):
            at = pl.ds(pl.multiple_of(i * tile, tile), tile)
            total = refs[0][at, :].astype(jnp.float32)
            for ref in refs[1:]:
                total += ref[at, :].astype(jnp.float32)
            refs[0][at, :] = total.astype(jnp.bfloat16)
            return 0

        lax.fori_loop(0, width // tile, one, 0)

    def z_send_of(q, dest, got, recv, device, sem):
        return pltpu.make_async_remote_copy(
            src_ref=ig.at[q, rows_of(dest, c)],
            dst_ref=got.at[q, dest],
            send_sem=sem,
            recv_sem=recv.at[q, dest],
            device_id=device,
            device_id_type=MESH_ID,
        )

    mid = depth // 2 - 1
    up_items = [(0, d) for d in range(depth - 1, 0, -1) if d != mid]
    up_items += [(1, d) for d in range(depth - 1, 0, -1)]
    down_items = [(0, d) for d in range(depth - 1) if d != mid]
    down_items += [(1, d) for d in range(depth - 1)]

    def z_tick(t, first=True, rest=True):
        for index, (items, after, got, recv, source, target) in enumerate(
            (
                (up_items, z, up_got, up_sem, who["down"], who["up"]),
                (down_items, depth - 1 - z, down_got, down_sem, who["up"], who["down"]),
            )
        ):
            item = t - after
            q = jnp.int32(0)
            dest = jnp.int32(0)
            earlier = jnp.int32(0)
            on = item < 0
            for i, (q_of, dest_of) in enumerate(items):
                goes = z < dest_of if index == 0 else z > dest_of
                q = jnp.where(item == i, q_of, q)
                dest = jnp.where(item == i, dest_of, dest)
                earlier += (goes & (item > i)).astype(jnp.int32)
                on = (on & (item != i)) | (goes & (item == i))
            on = on & (item >= 0) & (item < len(items))
            if not (first and rest):
                on = on & ((after == 0) if first else (after > 0))

            @pl.when(on)
            def _(index=index, after=after, got=got, recv=recv, source=source, target=target, q=q, dest=dest, earlier=earlier):
                landed(core_got.at[q, dest], core_sem.at[q, dest], who["core"])
                mine = ig.at[q, rows_of(dest, c)]

                @pl.when(after == 0)
                def _():
                    add_tiles((mine, core_got.at[q, dest]))

                @pl.when(after > 0)
                def _():
                    landed(got.at[q, dest], recv.at[q, dest], source)
                    add_tiles((mine, core_got.at[q, dest], got.at[q, dest]))

                send = z_send_of(q, dest, got, recv, target, z_send.at[index, lax.rem(earlier, 2)])

                @pl.when(earlier > 1)
                def _():
                    send.wait_send()

                send.start()

    def x_first():
        mine = ig.at[0, rows_of(mid, c)]
        landed(core_got.at[0, mid], core_sem.at[0, mid], who["core"])
        add_tiles((mine, core_got.at[0, mid]))
        sends.start(lambda: mine, lambda: up_got.at[0, mid], up_sem.at[0, mid], who["x"])

    def x_first_got():
        landed(up_got.at[0, mid], up_sem.at[0, mid], who["x"])
        add_tiles((ig.at[1, rows_of(mid, c)], up_got.at[0, mid]))

    def z_last(q):
        mine = ig.at[q, rows_of(z, c)]
        core = core_got.at[q, z]

        def joint(when, extra, above, below):
            @pl.when(when)
            def _():
                landed(core, core_sem.at[q, z], who["core"])
                refs = (mine, core)
                if extra:
                    landed(x_got, ix_sem, who["x"])
                    refs += (x_got,)
                if below:
                    landed(up_got.at[q, z], up_sem.at[q, z], who["down"])
                    refs += (up_got.at[q, z],)
                if above:
                    landed(down_got.at[q, z], down_sem.at[q, z], who["up"])
                    refs += (down_got.at[q, z],)
                add_tiles(refs)

        extra = q == 1
        joint(z == 0, extra, True, False)
        joint(z == depth - 1, extra, False, True)
        joint((z > 0) & (z < depth - 1) & (z != mid), extra, True, True)
        if q == 1:
            joint(z == mid, False, True, True)
            restore(mine, x_got, perm)
            copy = pltpu.make_async_copy(x_got, ig_out, own_sem.at[1])
            copy.start()
            own_copies.append(copy)
        else:
            sends.start(lambda: mine, lambda: x_got, ix_sem, who["x"], z != mid)

    own_copies = []

    def own_chunk(t):
        n, q = t // 2, t % 2
        landed(reused_at(t, False), y_sem.at[t], who["y"])
        ref, row = reused(t, False)
        if t + 3 < 2 * bands and t != 1:
            y_send(t + 3)
        owner = y * 2 + owner_x[q]

        def one(r, _):
            valid = jnp.broadcast_to(r < table[1, owner], (band, block_rows))
            total = gb[n, table[8, owner * slots + r]].astype(jnp.float32)
            total += ref[row + r].astype(jnp.float32)
            total = jnp.where(valid, total, 0.0)
            ref[row + r] = total.astype(jnp.bfloat16)
            squares[...] += jnp.sum((total * total).reshape(band // 8, 8, block_rows), axis=0)
            return 0

        lax.fori_loop(0, slots, one, 0)
        src = lambda: reused_at(t, False)
        dst = lambda: gt.at[:, pl.ds(pl.multiple_of(x * half + n * band, 16), band)]
        if q == 0:
            sends.start(src, dst, x_sem.at[n], who["x"])
        else:
            copy = pltpu.make_async_copy(src(), dst(), own_sem.at[2 + n])
            copy.start()
            own_copies.append(copy)

    def bias_sum():
        landed(b_got.at[0], b_sem.at[0], who["y"])
        total = bgrad[...] + b_got[0]
        b_got[1] = total
        bt[x] = total
        sends.start(lambda: b_got.at[1], lambda: bt.at[x], b_sem.at[1], who["x"])
        counted = jnp.broadcast_to(y == 0, (half, LANES))
        each = jnp.where(counted, total * total, 0.0)
        squares[:, pl.ds(0, LANES)] += jnp.sum(each.reshape(half // 8, 8, LANES), axis=0)

    landed(xv.at[0, rows_of(z, c)], xg_sem.at[0, mp], who["x"])
    spread(0, z, z < depth - 1, z > 0, None)
    cot_sent = sends.start(lambda: hv.at[0], lambda: cg.at[0], c_sem, who["x"])
    x_piece(0)
    y_piece(1)
    for d in range(1, depth):
        along_z(0, d)
        if d == 1:
            y_piece(2)
        if d <= 2:
            pass_on(d - 1)
    along_z(1, 1)
    landed(cg.at[0], c_sem, who["x"])
    landed(rg.at[0], r_sem, who["x"])
    sends.wait([cot_sent])
    from_core(0)
    def layer_part(q, n):
        project(q, n)
        gates(q, n)

    def give_part(n):
        weight_grad(n)
        if n == 0:
            pl.semaphore_wait(free_sem, 1)
            y_send(0)
            y_send(1)

    chunks = 2 * bands
    ticks = 2 * depth - 3
    arrange(0)
    layer_part(0, 0)
    pass_on(2)
    along_z(1, 2)
    arrange(1)
    layer_part(0, 1)
    along_z(1, 3)
    arrange(2)
    sends.wait(y_pieces + x_pieces)
    pl.semaphore_signal(free_sem, inc=1, device_id=who["y"], device_id_type=MESH_ID)
    from_core(1)
    layer_part(1, 0)
    give_part(0)
    layer_part(0, 2)
    input_grad(0)
    project(1, 1)
    x_first()
    z_tick(0)
    gates(1, 1)
    give_part(1)
    y_send(2)
    z_tick(1, rest=False)
    layer_part(1, 2)
    sends.start(lambda: bgrad, lambda: b_got.at[0], b_sem.at[0], who["y"])
    z_tick(1, first=False)
    input_grad(1)
    own_chunk(0)
    give_part(2)
    y_send(4)
    x_first_got()
    z_tick(2)
    own_chunk(1)
    for q in (0, 1):
        restore(hv.at[q], cg.at[q], perm)
    sends.start(lambda: cg.at[0], lambda: h_out.at[part(x)], h_sem, who["x"])
    h_own = pltpu.make_async_copy(cg.at[1], h_out.at[part(x)], own_sem.at[0])
    h_own.start()
    own_copies.append(h_own)
    bias_sum()
    own_chunk(2)
    z_last(0)
    for t in range(depth - 1, ticks):
        z_tick(t)
        own_chunk(t)
    for t in range(ticks, chunks):
        own_chunk(t)
    total = squares[:, pl.ds(0, LANES)] + squares[:, pl.ds(LANES, LANES)]
    s_got[mp] = total
    for device in mp_peers:
        sends.start(lambda: s_got.at[mp], lambda: s_got.at[mp], s_sem.at[mp], device)
    for device in mp_peers:
        landed(s_got.at[device[1]], s_sem.at[device[1]], device)
    total = s_got[0]
    for k in range(1, 2 * depth):
        total = total + s_got[k]
    t_got[dp] = total
    for device in dp_peers:
        sends.start(lambda: t_got.at[dp], lambda: t_got.at[dp], t_sem.at[dp], device)
    z_last(1)
    for device in dp_peers:
        landed(t_got.at[device[0]], t_sem.at[device[0]], device)
    total = t_got[0]
    for k in range(1, 4):
        total = total + t_got[k]
    norm[...] = jnp.broadcast_to(jnp.sqrt(jnp.sum(total, keepdims=True)), norm.shape)
    for n in range(bands):
        landed(gt.at[:, pl.ds(pl.multiple_of((1 - x) * half + n * band, 16), band)], x_sem.at[n], who["x"])
    landed(h_out.at[part(1 - x)], h_sem, who["x"])
    landed(bt.at[1 - x], b_sem.at[1], who["x"])

    @pl.when(z < depth - 1)
    def _():
        for k in range(2):
            z_send_of(1, z + 1, up_got, up_sem, who["up"], z_send.at[0, k]).wait_send()

    @pl.when(z > 0)
    def _():
        for k in range(2):
            z_send_of(1, z - 1, down_got, down_sem, who["down"], z_send.at[1, k]).wait_send()

    for copy in own_copies:
        copy.wait()
    sends.finish()


def adam_turn(weights, first, second, grad, decay_rate):
    rate = (2.0 * D) ** (-0.5)
    first_new = 0.9 * first + 0.1 * grad
    second_new = 0.999 * second + (0.001 * grad) * grad
    second_hat = second_new * (1.0 / (1.0 - 0.999**STEP))
    root = second_hat * lax.rsqrt(jnp.maximum(second_hat, 1e-37)) + 1e-08
    turn = pl.reciprocal(root, approx=True)
    turn = turn * (2.0 - root * turn)
    step = (first_new * (rate / (1.0 - 0.9**STEP))) * turn
    return (weights * (1.0 - rate * decay_rate) - step, first_new, second_new)


def adam_kernel(
    owners, norm, bt, bw, bm, bv, g, w, m, v,
    w_new, m_new, v_new, bw_new, bm_new, bv_new,
    g_held, held, made, in_sem, out_sem,
):
    deep, rows, width, block_rows = g_held.shape
    stages = made.shape[1]
    turns = g.shape[0] // rows
    half = width // 2
    blocks = owners.shape[0] - 3
    me = lax.axis_index("dp")

    def taken(i):
        slot = lax.rem(i, deep)
        at = pl.ds(i * rows, rows)
        copies = [pltpu.make_async_copy(g.at[at], g_held.at[slot], in_sem.at[slot, 3])]
        for k, ref in enumerate((w, m, v)):
            copies.append(pltpu.make_async_copy(ref.at[at], held.at[k, slot], in_sem.at[slot, k]))
        return copies

    def given(i):
        slot = lax.rem(i, stages)
        at = pl.ds(i * rows, rows)
        return [
            pltpu.make_async_copy(made.at[k, slot], ref.at[at], out_sem.at[slot, k])
            for k, ref in enumerate((w_new, m_new, v_new))
        ]

    for i in range(min(deep, turns)):
        for copy in taken(jnp.int32(i)):
            copy.start()
    number = jnp.int32(0)
    for j in range(blocks):
        number += (owners[j] == me).astype(jnp.int32)
    factor = 1.0 / jnp.maximum(norm[:1, :1], 1.0)
    lane_of = lax.broadcasted_iota(jnp.int32, (half, width), 1)
    row_of = lax.broadcasted_iota(jnp.int32, (half, width), 0)
    row = lax.broadcasted_iota(jnp.int32, (3, width), 0)
    grads = jnp.zeros((3, width), jnp.float32)
    filled = jnp.zeros((3, width), jnp.int32)
    for gate in range(3):
        owner, rank = bias_rank(owners, blocks, gate)
        line = jnp.zeros((1, width), jnp.float32)
        for h in range(2):
            column = bt[h][:, gate : gate + 1]
            line += jnp.sum(
                jnp.where(lane_of == row_of + h * half, column, 0.0), axis=0, keepdims=True
            )
        here = (row == rank) & jnp.broadcast_to(owner == me, (3, width))
        grads = jnp.where(here, line, grads)
        filled = jnp.where(here, 1, filled)
    news = adam_step(bw[...], bm[...], bv[...], grads * factor, 0.0)
    for ref, new in zip((bw_new, bm_new, bv_new), news):
        ref[...] = jnp.where(filled > 0, new, 0.0)

    def turn(i, _):
        slot, stage = lax.rem(i, deep), lax.rem(i, stages)
        for copy in taken(i):
            copy.wait()

        @pl.when(i >= stages)
        def _():
            for copy in given(i - stages):
                copy.wait()

        for r in range(rows):
            grad = g_held[slot, r].astype(jnp.float32) * factor
            valid = jnp.broadcast_to(i * rows + r < number, (width, block_rows))
            news = adam_turn(held[0, slot, r], held[1, slot, r], held[2, slot, r], grad, 0.1)
            for k, new in enumerate(news):
                made[k, stage, r] = jnp.where(valid, new, 0.0)
        for copy in given(i):
            copy.start()

        @pl.when(i + deep < turns)
        def _():
            for copy in taken(i + deep):
                copy.start()

        return 0

    lax.fori_loop(0, turns, turn, 0)
    for i in range(max(0, turns - stages), turns):
        for copy in given(jnp.int32(i)):
            copy.wait()


def paired(
    inputs, resets, owners, kernel, kernel_first, kernel_second, bias_rows, bias_first, bias_second, cotangent
):
    _, width, length = inputs.shape
    slots, _, block_rows = kernel.shape
    blocks = owners.shape[0] - 3
    full = width * lax.axis_size("mp")
    depth = lax.axis_size("mp") // 2
    half = width // 2
    bf16, f32 = jnp.bfloat16, jnp.float32
    shape = jax.ShapeDtypeStruct
    hbm = pl.BlockSpec(memory_space=pltpu.MemorySpace.HBM)
    vmem = pl.BlockSpec(memory_space=pltpu.VMEM)
    smem = pl.BlockSpec(memory_space=pltpu.SMEM)
    dma = pltpu.SemaphoreType.DMA
    band = half // BANDS
    gt, h_new, ig, bt, norm = pl.pallas_call(
        layer_kernel,
        out_shape=(
            shape((slots, width, block_rows), bf16),
            shape((width, length), bf16),
            shape((width, length), bf16),
            shape((2, half, LANES), f32),
            shape((8, LANES), f32),
        ),
        in_specs=[smem] + [hbm] * 3 + [vmem] * 2,
        out_specs=[hbm, hbm, hbm, vmem, vmem],
        scratch_shapes=[
            pltpu.SMEM((16, LANES), jnp.int32),
            pltpu.VMEM((16, LANES), jnp.int32),
            pltpu.VMEM((2, slots, band, block_rows), f32),
            pltpu.VMEM((4 * slots, band, block_rows), bf16),
            pltpu.VMEM((4 * slots, band, block_rows), bf16),
            pltpu.VMEM((4 * slots, band, block_rows), bf16),
            pltpu.VMEM((6 * half, full), bf16),
            pltpu.VMEM((2, full, length), bf16),
            pltpu.VMEM((2, half, length), bf16),
            pltpu.VMEM((2, 1, length), f32),
            pltpu.VMEM((4, 3, width), f32),
            pltpu.VMEM((2, half, length), bf16),
            pltpu.VMEM((6 * band, length), f32),
            pltpu.VMEM((6 * half, 2 * length), bf16),
            pltpu.VMEM((BANDS, blocks, band, block_rows), bf16),
            pltpu.VMEM((3 * half, LANES), f32),
            pltpu.VMEM((half, LANES), f32),
            pltpu.VMEM((length, length), bf16),
            pltpu.VMEM((2, full, length), bf16),
            pltpu.VMEM((2, depth, width, length), bf16),
            pltpu.VMEM((2, depth, width, length), bf16),
            pltpu.VMEM((2, depth, width, length), bf16),
            pltpu.VMEM((width, length), bf16),
            pltpu.VMEM((2, half, LANES), f32),
            pltpu.VMEM((8, block_rows), f32),
            pltpu.VMEM((2 * depth, 8, LANES), f32),
            pltpu.VMEM((4, 8, LANES), f32),
            dma((5,)),
            dma((2,)),
            dma((2 + BANDS,)),
            dma((96,)),
            dma((BANDS, 4)),
            dma((2, 2 * depth)),
            dma,
            dma,
            dma((4,)),
            dma((2 * BANDS,)),
            dma((BANDS,)),
            dma((2, depth)),
            dma((2, depth)),
            dma((2, depth)),
            dma((2, 2)),
            dma,
            dma,
            dma((2,)),
            dma((2 * depth,)),
            dma((4,)),
            pltpu.SemaphoreType.REGULAR,
        ],
        compiler_params=pltpu.CompilerParams(
            collective_id=0, has_side_effects=True, vmem_limit_bytes=VMEM
        ),
        name="layer",
    )(
        owners,
        kernel,
        inputs.reshape(width, length),
        cotangent.reshape(width, length),
        resets,
        bias_rows,
    )
    rows = 1
    news = pl.pallas_call(
        adam_kernel,
        out_shape=(shape(kernel.shape, f32),) * 3 + (shape(bias_rows.shape, f32),) * 3,
        in_specs=[smem] + [vmem] * 5 + [hbm] * 4,
        out_specs=[hbm] * 3 + [vmem] * 3,
        scratch_shapes=[
            pltpu.VMEM((DEEP, rows, width, block_rows), bf16),
            pltpu.VMEM((3, DEEP, rows, width, block_rows), f32),
            pltpu.VMEM((3, STAGES, rows, width, block_rows), f32),
            dma((DEEP, 4)),
            dma((STAGES, 3)),
        ],
        compiler_params=pltpu.CompilerParams(vmem_limit_bytes=VMEM),
        name="adam",
    )(owners, norm, bt, bias_rows, bias_first, bias_second, gt, kernel, kernel_first, kernel_second)
    kernel_w, kernel_m, kernel_v, bias_w, bias_m, bias_v = news
    return (h_new[None], ig[None], kernel_w, kernel_m, kernel_v, bias_w, bias_m, bias_v, norm[0, 0])


def solution(mesh):
    placed = (
        P("dp", "mp", None),
        P("dp", None),
        P(),
        P("dp", "mp", None),
        P("dp", "mp", None),
        P("dp", "mp", None),
        P("dp", "mp"),
        P("dp", "mp"),
        P("dp", "mp"),
        P("dp", "mp", None),
    )
    fits = mesh.shape["dp"] == 4 and mesh.shape["mp"] == 8
    return jax.shard_map(
        paired if fits else shards,
        mesh=mesh,
        in_specs=placed,
        out_specs=(
            P("dp", "mp", None),
            P("dp", "mp", None),
            P("dp", "mp", None),
            P("dp", "mp", None),
            P("dp", "mp", None),
            P("dp", "mp"),
            P("dp", "mp"),
            P("dp", "mp"),
            P(),
        ),
        check_vma=False,
    )
```

```python
import jax
import jax.numpy as jnp
from jax import lax
from jax.experimental import pallas as pl
from jax.experimental.pallas import tpu as pltpu
from jax.sharding import PartitionSpec as P

D = 2304
STEP = 10


def earlier_count(owned):
    number = owned.shape[0]
    places = jnp.arange(number, dtype=jnp.int32)
    earlier = (owned[:, None] == owned[None, :]) & (places[None, :] < places[:, None])
    return jnp.sum(earlier.astype(jnp.int32), axis=1)


def slot_sources(slot, count):
    places = jnp.arange(slot.shape[0], dtype=jnp.int32)
    hits = slot[None, :] == jnp.arange(count, dtype=jnp.int32)[:, None]
    source = jnp.sum(jnp.where(hits, places[None, :], 0), axis=1)
    return (source, jnp.any(hits, axis=1).astype(jnp.float32))


def shift_later(values):
    return jnp.pad(values, ((0, 0), (0, 0), (1, 0)))[:, :, :-1]


def shift_earlier(values):
    return jnp.pad(values, ((0, 0), (0, 0), (0, 1)))[:, :, 1:]


def combine(earlier, later):
    return (earlier[0] * later[0], later[0] * earlier[1] + later[1])


def pooled(preact, keeping):
    channels = preact.shape[1] // 3
    candidate = jnp.tanh(preact[:, :channels])
    forget = jax.nn.sigmoid(preact[:, channels : 2 * channels])
    output_gate = jax.nn.sigmoid(preact[:, 2 * channels :])
    decay = forget * keeping[:, None, :]
    _, cells = lax.associative_scan(combine, (decay, (1.0 - forget) * candidate), axis=2)
    return output_gate * cells


def adam_step(weights, first, second, grad, decay_rate):
    rate = (2.0 * D) ** (-0.5)
    first_new = 0.9 * first + 0.1 * grad
    second_new = 0.999 * second + 0.001 * grad * grad
    first_hat = first_new / (1.0 - 0.9**STEP)
    second_hat = second_new / (1.0 - 0.999**STEP)
    weights_new = weights - rate * (
        first_hat / (jnp.sqrt(second_hat) + 1e-08) + decay_rate * weights
    )
    return (weights_new, first_new, second_new)


def shards(
    inputs,
    resets,
    owners,
    kernel,
    kernel_first,
    kernel_second,
    bias_rows,
    bias_first,
    bias_second,
    cotangent,
):
    streams, local_width, length = inputs.shape
    slots_own, _, block_rows = kernel.shape
    block_count = owners.shape[0] - 3
    dp_size = lax.axis_size("dp")
    dp_index = lax.axis_index("dp")
    kernel_owner = owners[:block_count]
    bias_owner = owners[block_count:]
    kernel_slot = kernel_owner * slots_own + earlier_count(kernel_owner)
    bias_slot = bias_owner * 3 + earlier_count(bias_owner)
    all_kernel, all_bias = (
        lax.all_gather(kernel.astype(jnp.bfloat16), "dp", axis=0, tiled=True),
        lax.all_gather(bias_rows.astype(jnp.bfloat16), "dp", axis=0, tiled=True),
    )
    per_gate = block_count // 3
    double_width = per_gate * block_rows
    full_width = double_width // 2
    gate_cols = 3 * local_width
    arranged = (
        all_kernel[kernel_slot]
        .reshape(3, per_gate, local_width, block_rows)
        .transpose(0, 2, 1, 3)
        .reshape(gate_cols, double_width)
    )
    paired_t = jnp.concatenate([arranged[:, :full_width], arranged[:, full_width:]], axis=0)
    bias_vec = all_bias[bias_slot].astype(jnp.float32).reshape(gate_cols)
    rows = paired_t
    projected = jnp.einsum(
        "ok,skl->sol",
        rows,
        lax.all_gather(inputs, "mp", axis=1, tiled=True),
        preferred_element_type=jnp.float32,
    )
    preact = (
        projected[:, :gate_cols] + shift_later(projected[:, gate_cols:]) + bias_vec[None, :, None]
    )
    keeping = (1 - resets).astype(jnp.float32)
    result, pullback = jax.vjp(lambda values: pooled(values, keeping), preact)
    pre_grad = pullback(cotangent.astype(jnp.float32))[0].astype(jnp.bfloat16)
    joined = jnp.concatenate([pre_grad, shift_earlier(pre_grad)], axis=1)
    bias_grad = jnp.sum(pre_grad.astype(jnp.float32), axis=(0, 2)).reshape(3, local_width)
    pair_grad = jnp.einsum(
        "sol,skl->ok",
        joined,
        lax.all_gather(inputs, "mp", axis=1, tiled=True),
        preferred_element_type=jnp.float32,
    )
    rows = paired_t
    term_rows = lax.psum_scatter(
        jnp.einsum("ok,sol->ksl", rows, joined, preferred_element_type=jnp.float32),
        "mp",
        scatter_dimension=0,
        tiled=True,
    )
    input_grads = jnp.transpose(term_rows.astype(jnp.bfloat16), (1, 0, 2))
    block_grad = pair_grad.reshape(2, 3, local_width, full_width).transpose(1, 2, 0, 3)
    block_grad = (
        block_grad.reshape(3, local_width, per_gate, block_rows)
        .transpose(0, 2, 1, 3)
        .reshape(block_count, local_width, block_rows)
    )
    kernel_source, kernel_valid = slot_sources(kernel_slot, dp_size * slots_own)
    bias_source, bias_valid = slot_sources(bias_slot, dp_size * 3)
    own_kernel_valid = lax.dynamic_slice_in_dim(kernel_valid, dp_index * slots_own, slots_own)
    own_bias_valid = lax.dynamic_slice_in_dim(bias_valid, dp_index * 3, 3)
    total_kernel, total_bias = lax.psum((block_grad, bias_grad), "dp")
    own_kernel_source = lax.dynamic_slice_in_dim(kernel_source, dp_index * slots_own, slots_own)
    own_bias_source = lax.dynamic_slice_in_dim(bias_source, dp_index * 3, 3)
    own_kernel = total_kernel[own_kernel_source] * own_kernel_valid[:, None, None]
    own_bias = total_bias[own_bias_source] * own_bias_valid[:, None]
    squares = jnp.sum(own_kernel * own_kernel) + jnp.sum(own_bias * own_bias)
    grad_norm = jnp.sqrt(lax.psum(squares, ("dp", "mp")))
    factor = 1.0 / jnp.maximum(grad_norm, 1.0)
    kernel_w, kernel_m, kernel_v = adam_step(
        kernel, kernel_first, kernel_second, own_kernel * factor, 0.1
    )
    bias_w, bias_m, bias_v = adam_step(bias_rows, bias_first, bias_second, own_bias * factor, 0.0)
    kernel_mask = own_kernel_valid[:, None, None] > 0.5
    bias_mask = own_bias_valid[:, None] > 0.5
    return (
        result.astype(jnp.bfloat16),
        input_grads,
        jnp.where(kernel_mask, kernel_w, 0.0),
        jnp.where(kernel_mask, kernel_m, 0.0),
        jnp.where(kernel_mask, kernel_v, 0.0),
        jnp.where(bias_mask, bias_w, 0.0),
        jnp.where(bias_mask, bias_m, 0.0),
        jnp.where(bias_mask, bias_v, 0.0),
        grad_norm,
    )


MESH_ID = pl.DeviceIdType.MESH
LANES = 128
BANDS = 3
IM = 256
DEEP = 8
STAGES = 4
VMEM = 61 * 2**20


def place():
    dp, mp = lax.axis_index("dp"), lax.axis_index("mp")
    return dp // 2, lax.rem(dp, 2), mp // 2, lax.rem(mp, 2)


def partners(y, x, z, c):
    dp, mp = y * 2 + x, z * 2 + c
    return {
        "x": (y * 2 + 1 - x, mp),
        "y": ((1 - y) * 2 + x, mp),
        "xy": ((1 - y) * 2 + 1 - x, mp),
        "core": (dp, z * 2 + 1 - c),
        "up": (dp, mp + 2),
        "down": (dp, mp - 2),
    }


def greet(devices):
    barrier = pltpu.get_barrier_semaphore()
    for device in devices:
        pl.semaphore_signal(barrier, inc=1, device_id=device, device_id_type=MESH_ID)
    pl.semaphore_wait(barrier, len(devices))


class Sends:
    def __init__(self, sems):
        self.sems, self.number, self.made = sems, 0, {}

    def start(self, src, dst, recv, device, when=None):
        slot = self.number
        self.number += 1

        def build():
            return pltpu.make_async_remote_copy(
                src_ref=src(),
                dst_ref=dst(),
                send_sem=self.sems.at[slot],
                recv_sem=recv,
                device_id=device,
                device_id_type=MESH_ID,
            )

        if when is None:
            build().start()
        else:
            pl.when(when)(lambda: build().start())
        self.made[slot] = (build, when)
        return slot

    def wait(self, slots):
        for slot in slots:
            build, when = self.made.pop(slot)
            if when is None:
                build().wait_send()
            else:
                pl.when(when)(lambda build=build: build().wait_send())

    def finish(self):
        self.wait(list(self.made))


def landed(ref, sem, device):
    pltpu.make_async_remote_copy(
        src_ref=ref, dst_ref=ref, send_sem=sem, recv_sem=sem, device_id=device, device_id_type=MESH_ID
    ).wait_recv()


def fill_order(perm):
    length = perm.shape[0]
    tile = 16
    column = lax.broadcasted_iota(jnp.int32, (tile, length), 1)
    wanted = lax.rem(column, LANES) * (length // LANES) + column // LANES
    wanted = wanted - lax.broadcasted_iota(jnp.int32, (tile, length), 0)

    def one(i, _):
        at = pl.ds(pl.multiple_of(i * tile, tile), tile)
        perm[at, :] = jnp.where(wanted == i * tile, 1.0, 0.0).astype(jnp.bfloat16)
        return 0

    lax.fori_loop(0, length // tile, one, 0)


def reorder(src, dst, perm):
    def one(i, _):
        at = pl.ds(pl.multiple_of(i * 256, 256), 256)
        moved = jnp.dot(src[...], perm[:, at], preferred_element_type=jnp.float32)
        dst[:, at] = moved.astype(dst.dtype)
        return 0

    lax.fori_loop(0, perm.shape[1] // 256, one, 0)


def restore(src, dst, perm):
    def one(i, _):
        at = pl.ds(pl.multiple_of(i * 256, 256), 256)
        moved = lax.dot_general(
            src[...], perm[at, :], (((1,), (1,)), ((), ())), preferred_element_type=jnp.float32
        )
        dst[:, at] = moved.astype(dst.dtype)
        return 0

    lax.fori_loop(0, perm.shape[0] // 256, one, 0)


def bias_rank(owners, blocks, g):
    owner = owners[blocks + g]
    rank = jnp.int32(0)
    for h in range(g):
        rank += (owners[blocks + h] == owner).astype(jnp.int32)
    return owner, rank


def sigmoid(v):
    return 0.5 * jnp.tanh(0.5 * v) + 0.5


def later(values):
    return [pltpu.roll(values[-1], 1, 1)] + values[:-1]


def scan_both(decay, fresh, source):
    groups = len(decay)
    held, gain = [fresh[0]], [decay[0]]
    for v in range(1, groups):
        held.append(fresh[v] + decay[v] * held[-1])
        gain.append(decay[v] * gain[-1])
    back, fall = [source[-1]], [None]
    for v in range(groups - 2, -1, -1):
        back.insert(0, source[v] + decay[v + 1] * back[0])
        fall.insert(0, decay[v + 1] if fall[0] is None else decay[v + 1] * fall[0])
    ahead = pltpu.roll(decay[0], LANES - 1, 1)
    level, factor = held[-1], gain[-1]
    behind, drop = back[0], fall[0] * ahead
    d = 1
    while d < LANES:
        level = level + factor * pltpu.roll(level, d, 1)
        behind = behind + drop * pltpu.roll(behind, LANES - d, 1)
        if 2 * d < LANES:
            factor = factor * pltpu.roll(factor, d, 1)
            drop = drop * pltpu.roll(drop, LANES - d, 1)
        d *= 2
    carry = pltpu.roll(level, 1, 1)
    cells = [held[v] + gain[v] * carry for v in range(groups)]
    carry = ahead * pltpu.roll(behind, LANES - 1, 1)
    dc = [back[v] + fall[v] * carry for v in range(groups - 1)] + [back[-1] + carry]
    return cells, dc


def gate_tile(pre_at, bias_at, keep, dh_at, h_at, joined_at, add_bias):
    groups = len(keep)
    lane = lax.broadcasted_iota(jnp.int32, keep[0].shape, 1)

    def pre(g):
        now = [pre_at(0, g, v) for v in range(groups)]
        before = later([pre_at(1, g, v) for v in range(groups)])
        before[0] = jnp.where(lane == 0, 0.0, before[0])
        bias = bias_at(g)
        return [n + b + bias for n, b in zip(now, before)]

    cand = [jnp.tanh(v) for v in pre(0)]
    forget = [sigmoid(v) for v in pre(1)]
    gate = [sigmoid(v) for v in pre(2)]
    decay = [f * k for f, k in zip(forget, keep)]
    dh = [dh_at(v) for v in range(groups)]
    cells, dc = scan_both(
        decay,
        [(1.0 - f) * z for f, z in zip(forget, cand)],
        [d * o for d, o in zip(dh, gate)],
    )
    for v in range(groups):
        h_at(v, gate[v] * cells[v])
    past = later(cells)
    grads = (
        [dc[v] * (1.0 - forget[v]) * (1.0 - cand[v] * cand[v]) for v in range(groups)],
        [
            dc[v] * (keep[v] * past[v] - cand[v]) * (forget[v] * (1.0 - forget[v]))
            for v in range(groups)
        ],
        [dh[v] * cells[v] * (gate[v] * (1.0 - gate[v])) for v in range(groups)],
    )
    for g in range(3):
        narrow = [value.astype(jnp.bfloat16) for value in grads[g]]
        wide = [value.astype(jnp.float32) for value in narrow]
        first = jnp.where(lane == LANES - 1, 0.0, pltpu.roll(wide[0], LANES - 1, 1))
        ahead = wide[1:] + [first]
        total = wide[0]
        for v in range(groups):
            joined_at(0, g, v, narrow[v])
            joined_at(1, g, v, ahead[v].astype(jnp.bfloat16))
            if v:
                total = total + wide[v]
        add_bias(jnp.where(lane == g, jnp.sum(total, axis=1, keepdims=True), 0.0))


def fill_tables(owners, table, table_v, sem, blocks, slots):
    per_half = blocks // 6
    down = lax.broadcasted_iota(jnp.int32, (64, LANES), 0)
    along = lax.broadcasted_iota(jnp.int32, (64, LANES), 1)

    def spell(j, both):
        owner = owners[j]
        return jnp.where(down == j, owner, both[0]), jnp.where(along == j, owner, both[1])

    start = (jnp.full((64, LANES), -1, jnp.int32), jnp.full((64, LANES), -2, jnp.int32))
    rows, columns = lax.fori_loop(0, blocks, spell, start)
    rank = jnp.sum(jnp.where((rows == columns) & (down < along), 1, 0), axis=0, keepdims=True)
    table_v[pl.ds(0, 1), :] = columns[:1] * slots + rank
    table_v[pl.ds(1, 1), :] = jnp.sum(jnp.where(rows == along, 1, 0), axis=0, keepdims=True)
    first = pltpu.make_async_copy(table_v.at[pl.ds(0, 8)], table.at[pl.ds(0, 8)], sem.at[0])
    first.start()
    first.wait()

    def place_of(j, held):
        stands = lax.rem(j, per_half) * 6 + lax.rem(j // per_half, 2) * 3 + j // (2 * per_half)
        return jnp.where(along[:1] == table[0, j], stands, held)

    table_v[pl.ds(8, 1), :] = lax.fori_loop(0, blocks, place_of, jnp.zeros((1, LANES), jnp.int32))
    second = pltpu.make_async_copy(table_v.at[pl.ds(8, 8)], table.at[pl.ds(8, 8)], sem.at[1])
    second.start()
    second.wait()


def layer_kernel(
    owners, w_ref, x_ref, cot_ref, res_ref, bias_ref,
    gt, h_out, ig_out, bt, norm,
    table, table_v, wf, wg0, wg1, wg2, wv, xv, cg, rg, bg, hv, p, jv, gb, bcol, bgrad, perm,
    ig, up_got, down_got, core_got, x_got, b_got, squares, s_got, t_got,
    load_sem, table_sem, own_sem, send_sem, w_sem, xg_sem, c_sem, r_sem, bg_sem,
    y_sem, x_sem, core_sem, up_sem, down_sem, z_send, ix_sem, h_sem, b_sem, s_sem, t_sem, free_sem,
):
    y, x, z, c = place()
    dp, mp = y * 2 + x, z * 2 + c
    who = partners(y, x, z, c)
    slots, width, block_rows = gt.shape
    half = width // 2
    length = h_out.shape[1]
    full = xv.shape[1]
    depth = full // width // 2
    per_half = full // block_rows
    blocks = 6 * per_half
    tile = 16
    groups = length // LANES
    wg = (wg0, wg1, wg2)
    band = wg0.shape[1]
    bands = half // band
    owner_x = (1 - x, x)
    mid = depth // 2 - 1
    mp_peers = [(dp, lax.rem(mp + r, 2 * depth)) for r in range(1, 2 * depth)]
    dp_peers = [who["x"], who["y"], who["xy"]]

    def part(index):
        return pl.ds(pl.multiple_of(index * half, half), half)

    def rows_of(place_z, core):
        return pl.ds(pl.multiple_of((place_z * 2 + core) * width, width), width)

    def piece(n, owner):
        return wg[n].at[pl.ds(owner * slots, slots)]

    def reused(t, give):
        row = (t + (2 * bands if give else 0)) * slots
        return wg[row // (4 * slots)], row % (4 * slots)

    def reused_at(t, give):
        ref, row = reused(t, give)
        return ref.at[pl.ds(row, slots)]

    mine = xv.at[1, rows_of(z, c)]
    x_held = jv.at[pl.ds(0, width), pl.ds(0, length)]
    c_held = [jv.at[pl.ds(width + i * half, half), pl.ds(0, length)] for i in range(2)]
    x_load = pltpu.make_async_copy(x_ref, x_held, load_sem.at[0])
    c_loads = [
        pltpu.make_async_copy(cot_ref.at[part(x)], c_held[0], load_sem.at[1]),
        pltpu.make_async_copy(cot_ref.at[part(1 - x)], c_held[1], load_sem.at[2]),
    ]

    def w_load(i):
        at = pl.multiple_of((x if i % 2 == 0 else 1 - x) * half + (i // 2) * band, 16)
        return pltpu.make_async_copy(
            w_ref.at[:, pl.ds(at, band)], wf.at[i % 2], load_sem.at[3 + i % 2]
        )

    w_load(0).start()
    x_load.start()
    w_load(1).start()
    for load in c_loads:
        load.start()
    greet(mp_peers + dp_peers)
    sends = Sends(send_sem)
    def slice_of(q, place_z, core):
        return xv.at[q, rows_of(place_z, core)]

    def spread(q, place_z, up, down, core):
        ref = lambda: slice_of(q, place_z, c)
        recv = xg_sem.at[q, place_z * 2 + c]
        for name, when in (("up", up), ("down", down), ("core", core)):
            if when is not False:
                sends.start(ref, ref, recv, who[name], when)

    y_pieces, x_pieces = [], []

    def y_piece(n):
        ref = lambda: piece(n, dp)
        y_pieces.append(sends.start(ref, ref, w_sem.at[n, dp], who["y"]))

    def x_piece(n):
        x_pieces.append(
            sends.start(
                lambda: gb.at[n, pl.ds(0, slots)],
                lambda: piece(n, dp),
                w_sem.at[n, dp],
                who["x"],
            )
        )

    def take_weights(i):
        n = i // 2
        w_load(i).wait()

        def cast(r, _):
            value = wf[i % 2, r].astype(jnp.bfloat16)
            if i % 2 == 0:
                wg[n][dp * slots + r] = value
            else:
                gb[n, r] = value
            return 0

        lax.fori_loop(0, slots, cast, 0)
        if i + 2 < 2 * bands:
            w_load(i + 2).start()

    fill_order(perm)
    take_weights(0)
    y_piece(0)
    x_load.wait()
    reorder(x_held, mine, perm)
    spread(1, z, z < depth - 1, z > 0, None)
    sends.start(lambda: mine, lambda: xv.at[0, rows_of(z, c)], xg_sem.at[0, mp], who["x"])
    for i in range(1, 2 * bands):
        take_weights(i)
    for name in ("x", "y", "xy"):
        sends.start(lambda: bias_ref, lambda: bg.at[dp], bg_sem.at[dp], who[name])
    bg[dp] = bias_ref[...]
    for load in c_loads:
        load.wait()
    reorder(c_held[0], cg.at[1], perm)
    reorder(c_held[1], hv.at[0], perm)
    keep_row = 1.0 - jnp.broadcast_to(res_ref[...], (16, length)).astype(jnp.float32)
    rg[1] = jnp.dot(keep_row.astype(jnp.bfloat16), perm[...], preferred_element_type=jnp.float32)[:1]
    sends.start(lambda: rg.at[1], lambda: rg.at[0], r_sem, who["x"])
    fill_tables(owners, table, table_v, table_sem, blocks, slots)
    for owner in (y * 2 + 1 - x, (1 - y) * 2 + x, (1 - y) * 2 + 1 - x):
        landed(bg.at[owner], bg_sem.at[owner], who["x"])
    lane_of = lax.broadcasted_iota(jnp.int32, (half, width), 1)
    row_of = lax.broadcasted_iota(jnp.int32, (half, width), 0)
    diagonal = lane_of == row_of + x * half
    for g in range(3):
        owner, rank = bias_rank(owners, blocks, g)
        held = bg[owner]
        line = jnp.zeros((1, width), jnp.float32)
        for r in range(3):
            line = jnp.where(rank == r, held[r : r + 1], line)
        line = line.astype(jnp.bfloat16).astype(jnp.float32)
        column = jnp.sum(jnp.where(diagonal, line, 0.0), axis=1, keepdims=True)
        bcol[pl.ds(g * half, half), :] = jnp.broadcast_to(column, (half, LANES))
    bgrad[...] = jnp.zeros_like(bgrad)
    squares[...] = jnp.zeros_like(squares)

    def along_z(q, d):
        for at, on, on_z, device, up in (
            (z - d, z >= d, z < depth - 1, who["down"], True),
            (z + d, z + d < depth, z > 0, who["up"], False),
        ):
            if q == 0:
                on = on & (at != mid)

            @pl.when(on)
            def _(at=at, device=device):
                landed(slice_of(q, at, c), xg_sem.at[q, at * 2 + c], device)

            further = on & on_z
            spread(q, at, further if up else False, False if up else further, on)

    def pass_on(n):
        owner = y * 2 + 1 - x
        ref = lambda: piece(n, owner)
        landed(ref(), w_sem.at[n, owner], who["x"])
        if n + 1 < bands:
            x_piece(n + 1)
        y_pieces.append(sends.start(ref, ref, w_sem.at[n, owner], who["y"]))

    def arrange(n):
        for owner in ((1 - y) * 2 + x, (1 - y) * 2 + 1 - x):
            landed(piece(n, owner), w_sem.at[n, owner], who["y"])
        for h in range(2):
            for g in range(3):

                def one(k, _, h=h, g=g):
                    columns = pl.ds(pl.multiple_of(k * block_rows, block_rows), block_rows)
                    first = table[0, g * 2 * per_half + h * per_half + k]
                    wv[pl.ds((n * 6 + h * 3 + g) * band, band), columns] = wg[n][first]
                    return 0

                lax.fori_loop(0, per_half, one, 0)

    def from_core(q):
        for k in range(depth):
            landed(slice_of(q, k, 1 - c), xg_sem.at[q, k * 2 + 1 - c], who["core"])

    def project(q, n):
        rows = pl.ds(n * 6 * band, 6 * band)

        def one(i, _):
            columns = pl.ds(pl.multiple_of(i * 512, 512), 512)
            p[:, columns] = jnp.dot(wv[rows, :], xv[q, :, columns], preferred_element_type=jnp.float32)
            return 0

        lax.fori_loop(0, length // 512, one, 0)

    def gates(q, n):
        lane = lax.broadcasted_iota(jnp.int32, (band, LANES), 1)
        keep = [
            jnp.broadcast_to(rg[q, :, pl.ds(v * LANES, LANES)], (band, LANES))
            for v in range(groups)
        ]
        keep[0] = jnp.where(lane == 0, 0.0, keep[0])

        at = pl.ds(n * band, band)

        def row(h, g):
            return pl.ds((n * 6 + h * 3 + g) * band, band)

        def h_at(v, value):
            hv[q, at, pl.ds(v * LANES, LANES)] = value.astype(jnp.bfloat16)

        def joined_at(h, g, v, value):
            jv[row(h, g), pl.ds(q * length + v * LANES, LANES)] = value

        def add_bias(value):
            bgrad[at, :] += value

        gate_tile(
            lambda h, g, v: p[pl.ds((h * 3 + g) * band, band), pl.ds(v * LANES, LANES)],
            lambda g: bcol[pl.ds(g * half + n * band, band), :],
            keep,
            lambda v: cg[q, at, pl.ds(v * LANES, LANES)].astype(jnp.float32),
            h_at,
            joined_at,
            add_bias,
        )

    def weight_grad(n):
        at = pl.ds(n * 6 * band, 6 * band)
        both = (((1,), (1,)), ((), ()))

        def one(k, _):
            rows = pl.ds(pl.multiple_of(k * block_rows, block_rows), block_rows)
            total = lax.dot_general(
                jv[at, pl.ds(0, length)], xv[0, rows, :], both, preferred_element_type=jnp.float32
            )
            total += lax.dot_general(
                jv[at, pl.ds(length, length)], xv[1, rows, :], both, preferred_element_type=jnp.float32
            )
            total = total.astype(jnp.bfloat16)
            for i in range(6):
                gb[n, k * 6 + i] = total[i * band : (i + 1) * band]
            return 0

        lax.fori_loop(0, per_half, one, 0)

        for q in range(2):

            def pack(r, _, q=q):
                ref, row = reused(n * 2 + q, True)
                ref[row + r] = gb[n, table[8, ((1 - y) * 2 + owner_x[q]) * slots + r]]
                return 0

            lax.fori_loop(0, slots, pack, 0)

    def y_send(t):
        sends.start(
            lambda: reused_at(t, True),
            lambda: reused_at(t, False),
            y_sem.at[t],
            who["y"],
        )

    def input_grad(q):
        number = full // IM
        order = sorted(range(number), key=lambda k: min(k, number - 1 - k))
        waiting = list(range(depth))
        for place_of, k in enumerate(order):
            ig[q, pl.ds(k * IM, IM), :] = lax.dot_general(
                wv[:, pl.ds(k * IM, IM)],
                jv[:, pl.ds(q * length, length)],
                (((0,), (0,)), ((), ())),
                preferred_element_type=jnp.float32,
            ).astype(jnp.bfloat16)
            for d in list(waiting):
                needs = set(range(2 * d * width // IM, ((2 * d + 2) * width - 1) // IM + 1))
                if needs <= set(order[: place_of + 1]):
                    waiting.remove(d)
                    sends.start(
                        lambda d=d: ig.at[q, rows_of(d, 1 - c)],
                        lambda d=d: core_got.at[q, d],
                        core_sem.at[q, d],
                        who["core"],
                    )

    def add_tiles(refs):
        def one(i, _):
            at = pl.ds(pl.multiple_of(i * tile, tile), tile)
            total = refs[0][at, :].astype(jnp.float32)
            for ref in refs[1:]:
                total += ref[at, :].astype(jnp.float32)
            refs[0][at, :] = total.astype(jnp.bfloat16)
            return 0

        lax.fori_loop(0, width // tile, one, 0)

    def z_send_of(q, dest, got, recv, device, sem):
        return pltpu.make_async_remote_copy(
            src_ref=ig.at[q, rows_of(dest, c)],
            dst_ref=got.at[q, dest],
            send_sem=sem,
            recv_sem=recv.at[q, dest],
            device_id=device,
            device_id_type=MESH_ID,
        )

    up_items = [(0, d) for d in range(depth - 1, 0, -1) if d != mid]
    up_items += [(1, d) for d in range(depth - 1, 0, -1)]
    down_items = [(0, d) for d in range(depth - 1) if d != mid]
    down_items += [(1, d) for d in range(depth - 1)]

    def z_tick(t, first=True, rest=True):
        for index, (items, after, got, recv, source, target) in enumerate(
            (
                (up_items, z, up_got, up_sem, who["down"], who["up"]),
                (down_items, depth - 1 - z, down_got, down_sem, who["up"], who["down"]),
            )
        ):
            item = t - after
            q = jnp.int32(0)
            dest = jnp.int32(0)
            on = item < 0
            for i, (q_of, dest_of) in enumerate(items):
                goes = z < dest_of if index == 0 else z > dest_of
                q = jnp.where(item == i, q_of, q)
                dest = jnp.where(item == i, dest_of, dest)
                on = (on & (item != i)) | (goes & (item == i))
            on = on & (item >= 0) & (item < len(items))
            if not (first and rest):
                on = on & ((after == 0) if first else (after > 0))

            @pl.when(on)
            def _(index=index, after=after, got=got, recv=recv, source=source, target=target, q=q, dest=dest):
                landed(core_got.at[q, dest], core_sem.at[q, dest], who["core"])
                mine = ig.at[q, rows_of(dest, c)]

                @pl.when(after == 0)
                def _():
                    add_tiles((mine, core_got.at[q, dest]))

                @pl.when(after > 0)
                def _():
                    landed(got.at[q, dest], recv.at[q, dest], source)
                    add_tiles((mine, core_got.at[q, dest], got.at[q, dest]))

                z_send_of(q, dest, got, recv, target, z_send.at[index, q, dest]).start()

    def x_first():
        mine = ig.at[0, rows_of(mid, c)]
        landed(core_got.at[0, mid], core_sem.at[0, mid], who["core"])
        add_tiles((mine, core_got.at[0, mid]))
        sends.start(lambda: mine, lambda: up_got.at[0, mid], up_sem.at[0, mid], who["x"])

    def x_first_got():
        landed(up_got.at[0, mid], up_sem.at[0, mid], who["x"])
        add_tiles((ig.at[1, rows_of(mid, c)], up_got.at[0, mid]))

    def z_last(q):
        mine = ig.at[q, rows_of(z, c)]
        core = core_got.at[q, z]

        def joint(when, extra, above, below):
            @pl.when(when)
            def _():
                landed(core, core_sem.at[q, z], who["core"])
                refs = (mine, core)
                if extra:
                    landed(x_got, ix_sem, who["x"])
                    refs += (x_got,)
                if below:
                    landed(up_got.at[q, z], up_sem.at[q, z], who["down"])
                    refs += (up_got.at[q, z],)
                if above:
                    landed(down_got.at[q, z], down_sem.at[q, z], who["up"])
                    refs += (down_got.at[q, z],)
                add_tiles(refs)

        extra = q == 1
        joint(z == 0, extra, True, False)
        joint(z == depth - 1, extra, False, True)
        joint((z > 0) & (z < depth - 1) & (z != mid), extra, True, True)
        if q == 1:
            joint(z == mid, False, True, True)
            restore(mine, x_got, perm)
            copy = pltpu.make_async_copy(x_got, ig_out, own_sem.at[1])
            copy.start()
            own_copies.append(copy)
        else:
            sends.start(lambda: mine, lambda: x_got, ix_sem, who["x"], z != mid)

    own_copies = []
    next_piece = {2: 3, 4: 5}

    def own_chunk(t):
        n, q = t // 2, t % 2
        landed(reused_at(t, False), y_sem.at[t], who["y"])
        ref, row = reused(t, False)
        if t in next_piece:
            y_send(next_piece[t])
        owner = y * 2 + owner_x[q]

        def one(r, _):
            valid = jnp.broadcast_to(r < table[1, owner], (band, block_rows))
            total = gb[n, table[8, owner * slots + r]].astype(jnp.float32)
            total += ref[row + r].astype(jnp.float32)
            total = jnp.where(valid, total, 0.0)
            ref[row + r] = total.astype(jnp.bfloat16)
            squares[...] += jnp.sum((total * total).reshape(band // 8, 8, block_rows), axis=0)
            return 0

        lax.fori_loop(0, slots, one, 0)
        src = lambda: reused_at(t, False)
        dst = lambda: gt.at[:, pl.ds(pl.multiple_of(x * half + n * band, 16), band)]
        if q == 0:
            sends.start(src, dst, x_sem.at[n], who["x"])
        else:
            copy = pltpu.make_async_copy(src(), dst(), own_sem.at[2 + n])
            copy.start()
            own_copies.append(copy)

    def bias_sum():
        landed(b_got.at[0], b_sem.at[0], who["y"])
        total = bgrad[...] + b_got[0]
        b_got[1] = total
        bt[x] = total
        sends.start(lambda: b_got.at[1], lambda: bt.at[x], b_sem.at[1], who["x"])
        counted = jnp.broadcast_to(y == 0, (half, LANES))
        each = jnp.where(counted, total * total, 0.0)
        squares[:, pl.ds(0, LANES)] += jnp.sum(each.reshape(half // 8, 8, LANES), axis=0)

    landed(xv.at[0, rows_of(z, c)], xg_sem.at[0, mp], who["x"])
    spread(0, z, (z < depth - 1) & (z != mid), (z > 0) & (z != mid), None)
    cot_sent = sends.start(lambda: hv.at[0], lambda: cg.at[0], c_sem, who["x"])
    x_piece(0)
    y_piece(1)
    along_z(1, 1)
    for d in range(1, depth):
        along_z(0, d)
        if d == 1:
            y_piece(2)
        if d <= 2:
            pass_on(d - 1)
            if d + 1 < depth - 1:
                along_z(1, d + 1)
    pass_on(2)
    sends.start(
        lambda: slice_of(1, mid, c),
        lambda: slice_of(0, mid, c),
        xg_sem.at[0, mid * 2 + c],
        who["x"],
        z != mid,
    )
    along_z(1, depth - 1)
    landed(cg.at[0], c_sem, who["x"])
    landed(rg.at[0], r_sem, who["x"])
    sends.wait([cot_sent])
    from_core(1)
    def layer_part(q, n):
        project(q, n)
        gates(q, n)

    def give_part(n):
        weight_grad(n)
        if n == 0:
            pl.semaphore_wait(free_sem, 1)
            y_send(0)
            y_send(1)

    ticks = 2 * depth - 3
    arrange(0)
    layer_part(1, 0)
    arrange(1)
    sends.wait([y_pieces[k] for k in (0, 1, 3, 4)] + x_pieces)
    pl.semaphore_signal(free_sem, inc=1, device_id=who["y"], device_id_type=MESH_ID)
    layer_part(1, 1)

    @pl.when(z != mid)
    def _():
        landed(slice_of(0, mid, c), xg_sem.at[0, mid * 2 + c], who["x"])

    spread(0, mid, False, False, z != mid)
    from_core(0)
    layer_part(0, 0)
    give_part(0)
    layer_part(0, 1)
    arrange(2)
    sends.wait([y_pieces[k] for k in (2, 5)])
    layer_part(0, 2)
    input_grad(0)
    z_tick(0)
    x_first()
    give_part(1)
    y_send(2)
    z_tick(1, rest=False)
    layer_part(1, 2)
    sends.start(lambda: bgrad, lambda: b_got.at[0], b_sem.at[0], who["y"])
    input_grad(1)
    z_tick(1, first=False)
    own_chunk(0)
    give_part(2)
    y_send(4)
    x_first_got()
    z_tick(2)
    own_chunk(1)
    for q in (0, 1):
        restore(hv.at[q], cg.at[q], perm)
    sends.start(lambda: cg.at[0], lambda: h_out.at[part(x)], h_sem, who["x"])
    h_own = pltpu.make_async_copy(cg.at[1], h_out.at[part(x)], own_sem.at[0])
    h_own.start()
    own_copies.append(h_own)
    bias_sum()
    own_chunk(2)
    z_last(0)
    left = [4, 3, 5]
    for t in range(depth - 1, ticks):
        z_tick(t)
        if left:
            own_chunk(left.pop(0))
    for t in left:
        own_chunk(t)
    total = squares[:, pl.ds(0, LANES)] + squares[:, pl.ds(LANES, LANES)]
    s_got[mp] = total
    for device in mp_peers:
        sends.start(lambda: s_got.at[mp], lambda: s_got.at[mp], s_sem.at[mp], device)
    for device in mp_peers:
        landed(s_got.at[device[1]], s_sem.at[device[1]], device)
    total = s_got[0]
    for k in range(1, 2 * depth):
        total = total + s_got[k]
    t_got[dp] = total
    for device in dp_peers:
        sends.start(lambda: t_got.at[dp], lambda: t_got.at[dp], t_sem.at[dp], device)
    z_last(1)
    for device in dp_peers:
        landed(t_got.at[device[0]], t_sem.at[device[0]], device)
    total = t_got[0]
    for k in range(1, 4):
        total = total + t_got[k]
    norm[...] = jnp.broadcast_to(jnp.sqrt(jnp.sum(total, keepdims=True)), norm.shape)
    for n in range(bands):
        landed(gt.at[:, pl.ds(pl.multiple_of((1 - x) * half + n * band, 16), band)], x_sem.at[n], who["x"])
    landed(h_out.at[part(1 - x)], h_sem, who["x"])
    landed(bt.at[1 - x], b_sem.at[1], who["x"])

    for index, (items, got, recv, target) in enumerate(
        ((up_items, up_got, up_sem, who["up"]), (down_items, down_got, down_sem, who["down"]))
    ):
        for q, dest in items:

            @pl.when(z < dest if index == 0 else z > dest)
            def _(index=index, got=got, recv=recv, target=target, q=q, dest=dest):
                z_send_of(q, dest, got, recv, target, z_send.at[index, q, dest]).wait_send()

    for copy in own_copies:
        copy.wait()
    sends.finish()


def adam_turn(weights, first, second, grad, decay_rate):
    rate = (2.0 * D) ** (-0.5)
    first_new = 0.9 * first + 0.1 * grad
    second_new = 0.999 * second + (0.001 * grad) * grad
    second_hat = second_new * (1.0 / (1.0 - 0.999**STEP))
    root = second_hat * lax.rsqrt(jnp.maximum(second_hat, 1e-37)) + 1e-08
    turn = pl.reciprocal(root, approx=True)
    turn = turn * (2.0 - root * turn)
    step = (first_new * (rate / (1.0 - 0.9**STEP))) * turn
    return (weights * (1.0 - rate * decay_rate) - step, first_new, second_new)


def adam_kernel(
    owners, norm, bt, bw, bm, bv, g, w, m, v, h_in, ig_in,
    w_new, m_new, v_new, bw_new, bm_new, bv_new, h_out, ig_out, norm_out,
    g_held, held, made, kept, in_sem, out_sem, pass_sem,
):
    deep, rows, width, block_rows = g_held.shape
    stages = made.shape[1]
    turns = g.shape[0] // rows
    half = width // 2
    blocks = owners.shape[0] - 3
    me = lax.axis_index("dp")

    def taken(i):
        slot = lax.rem(i, deep)
        at = pl.ds(i * rows, rows)
        copies = [pltpu.make_async_copy(g.at[at], g_held.at[slot], in_sem.at[slot, 3])]
        for k, ref in enumerate((w, m, v)):
            copies.append(pltpu.make_async_copy(ref.at[at], held.at[k, slot], in_sem.at[slot, k]))
        return copies

    def given(i):
        slot = lax.rem(i, stages)
        at = pl.ds(i * rows, rows)
        return [
            pltpu.make_async_copy(made.at[k, slot], ref.at[at], out_sem.at[slot, k])
            for k, ref in enumerate((w_new, m_new, v_new))
        ]

    for i in range(min(deep, turns)):
        for copy in taken(jnp.int32(i)):
            copy.start()
    come = [
        pltpu.make_async_copy(ref, kept.at[k], pass_sem.at[k]) for k, ref in enumerate((h_in, ig_in))
    ]
    leave = [
        pltpu.make_async_copy(kept.at[k], ref, pass_sem.at[2 + k])
        for k, ref in enumerate((h_out, ig_out))
    ]
    for copy in come:
        copy.start()
    norm_out[...] = norm[:1, :1]
    number = jnp.int32(0)
    for j in range(blocks):
        number += (owners[j] == me).astype(jnp.int32)
    factor = 1.0 / jnp.maximum(norm[:1, :1], 1.0)
    lane_of = lax.broadcasted_iota(jnp.int32, (half, width), 1)
    row_of = lax.broadcasted_iota(jnp.int32, (half, width), 0)
    row = lax.broadcasted_iota(jnp.int32, (3, width), 0)
    grads = jnp.zeros((3, width), jnp.float32)
    filled = jnp.zeros((3, width), jnp.int32)
    for gate in range(3):
        owner, rank = bias_rank(owners, blocks, gate)
        line = jnp.zeros((1, width), jnp.float32)
        for h in range(2):
            column = bt[h][:, gate : gate + 1]
            line += jnp.sum(
                jnp.where(lane_of == row_of + h * half, column, 0.0), axis=0, keepdims=True
            )
        here = (row == rank) & jnp.broadcast_to(owner == me, (3, width))
        grads = jnp.where(here, line, grads)
        filled = jnp.where(here, 1, filled)
    news = adam_step(bw[...], bm[...], bv[...], grads * factor, 0.0)
    for ref, new in zip((bw_new, bm_new, bv_new), news):
        ref[...] = jnp.where(filled > 0, new, 0.0)

    def turn(i, _):
        slot, stage = lax.rem(i, deep), lax.rem(i, stages)
        for copy in taken(i):
            copy.wait()

        @pl.when(i >= stages)
        def _():
            for copy in given(i - stages):
                copy.wait()

        for r in range(rows):
            grad = g_held[slot, r].astype(jnp.float32) * factor
            valid = jnp.broadcast_to(i * rows + r < number, (width, block_rows))
            news = adam_turn(held[0, slot, r], held[1, slot, r], held[2, slot, r], grad, 0.1)
            for k, new in enumerate(news):
                made[k, stage, r] = jnp.where(valid, new, 0.0)
        for copy in given(i):
            copy.start()

        @pl.when(i + deep < turns)
        def _():
            for copy in taken(i + deep):
                copy.start()

        @pl.when(i == turns // 2)
        def _():
            for k in range(2):
                come[k].wait()
                leave[k].start()

        return 0

    lax.fori_loop(0, turns, turn, 0)
    for i in range(max(0, turns - stages), turns):
        for copy in given(jnp.int32(i)):
            copy.wait()
    for copy in leave:
        copy.wait()


def paired(
    inputs, resets, owners, kernel, kernel_first, kernel_second, bias_rows, bias_first, bias_second, cotangent
):
    _, width, length = inputs.shape
    slots, _, block_rows = kernel.shape
    blocks = owners.shape[0] - 3
    full = width * lax.axis_size("mp")
    depth = lax.axis_size("mp") // 2
    half = width // 2
    bf16, f32 = jnp.bfloat16, jnp.float32
    shape = jax.ShapeDtypeStruct
    hbm = pl.BlockSpec(memory_space=pltpu.MemorySpace.HBM)
    vmem = pl.BlockSpec(memory_space=pltpu.VMEM)
    smem = pl.BlockSpec(memory_space=pltpu.SMEM)
    dma = pltpu.SemaphoreType.DMA
    band = half // BANDS
    gt, h_new, ig, bt, norm = pl.pallas_call(
        layer_kernel,
        out_shape=(
            shape((slots, width, block_rows), bf16),
            shape((width, length), bf16),
            shape((width, length), bf16),
            shape((2, half, LANES), f32),
            shape((8, LANES), f32),
        ),
        in_specs=[smem] + [hbm] * 3 + [vmem] * 2,
        out_specs=[hbm, hbm, hbm, vmem, vmem],
        scratch_shapes=[
            pltpu.SMEM((16, LANES), jnp.int32),
            pltpu.VMEM((16, LANES), jnp.int32),
            pltpu.VMEM((2, slots, band, block_rows), f32),
            pltpu.VMEM((4 * slots, band, block_rows), bf16),
            pltpu.VMEM((4 * slots, band, block_rows), bf16),
            pltpu.VMEM((4 * slots, band, block_rows), bf16),
            pltpu.VMEM((6 * half, full), bf16),
            pltpu.VMEM((2, full, length), bf16),
            pltpu.VMEM((2, half, length), bf16),
            pltpu.VMEM((2, 1, length), f32),
            pltpu.VMEM((4, 3, width), f32),
            pltpu.VMEM((2, half, length), bf16),
            pltpu.VMEM((6 * band, length), f32),
            pltpu.VMEM((6 * half, 2 * length), bf16),
            pltpu.VMEM((BANDS, blocks, band, block_rows), bf16),
            pltpu.VMEM((3 * half, LANES), f32),
            pltpu.VMEM((half, LANES), f32),
            pltpu.VMEM((length, length), bf16),
            pltpu.VMEM((2, full, length), bf16),
            pltpu.VMEM((2, depth, width, length), bf16),
            pltpu.VMEM((2, depth, width, length), bf16),
            pltpu.VMEM((2, depth, width, length), bf16),
            pltpu.VMEM((width, length), bf16),
            pltpu.VMEM((2, half, LANES), f32),
            pltpu.VMEM((8, block_rows), f32),
            pltpu.VMEM((2 * depth, 8, LANES), f32),
            pltpu.VMEM((4, 8, LANES), f32),
            dma((5,)),
            dma((2,)),
            dma((2 + BANDS,)),
            dma((96,)),
            dma((BANDS, 4)),
            dma((2, 2 * depth)),
            dma,
            dma,
            dma((4,)),
            dma((2 * BANDS,)),
            dma((BANDS,)),
            dma((2, depth)),
            dma((2, depth)),
            dma((2, depth)),
            dma((2, 2, depth)),
            dma,
            dma,
            dma((2,)),
            dma((2 * depth,)),
            dma((4,)),
            pltpu.SemaphoreType.REGULAR,
        ],
        compiler_params=pltpu.CompilerParams(
            collective_id=0, has_side_effects=True, vmem_limit_bytes=VMEM
        ),
        name="layer",
    )(
        owners,
        kernel,
        inputs.reshape(width, length),
        cotangent.reshape(width, length),
        resets,
        bias_rows,
    )
    rows = 1
    news = pl.pallas_call(
        adam_kernel,
        out_shape=(shape(kernel.shape, f32),) * 3
        + (shape(bias_rows.shape, f32),) * 3
        + (shape((width, length), bf16),) * 2
        + (shape((1, 1), f32),),
        in_specs=[smem] + [vmem] * 5 + [hbm] * 6,
        out_specs=[hbm] * 3 + [vmem] * 3 + [hbm] * 2 + [vmem],
        scratch_shapes=[
            pltpu.VMEM((DEEP, rows, width, block_rows), bf16),
            pltpu.VMEM((3, DEEP, rows, width, block_rows), f32),
            pltpu.VMEM((3, STAGES, rows, width, block_rows), f32),
            pltpu.VMEM((2, width, length), bf16),
            dma((DEEP, 4)),
            dma((STAGES, 3)),
            dma((4,)),
        ],
        compiler_params=pltpu.CompilerParams(vmem_limit_bytes=VMEM),
        name="adam",
    )(
        owners, norm, bt, bias_rows, bias_first, bias_second, gt, kernel, kernel_first, kernel_second, h_new, ig
    )
    *updated, h_last, ig_last, norm_last = news
    return (h_last[None], ig_last[None], *updated, norm_last[0, 0])


def solution(mesh):
    placed = (
        P("dp", "mp", None),
        P("dp", None),
        P(),
        P("dp", "mp", None),
        P("dp", "mp", None),
        P("dp", "mp", None),
        P("dp", "mp"),
        P("dp", "mp"),
        P("dp", "mp"),
        P("dp", "mp", None),
    )
    fits = mesh.shape["dp"] == 4 and mesh.shape["mp"] == 8
    return jax.shard_map(
        paired if fits else shards,
        mesh=mesh,
        in_specs=placed,
        out_specs=(
            P("dp", "mp", None),
            P("dp", "mp", None),
            P("dp", "mp", None),
            P("dp", "mp", None),
            P("dp", "mp", None),
            P("dp", "mp"),
            P("dp", "mp"),
            P("dp", "mp"),
            P(),
        ),
        check_vma=False,
    )
```

```python
import jax
import jax.numpy as jnp
from jax import lax
from jax.experimental import pallas as pl
from jax.experimental.pallas import tpu as pltpu
from jax.sharding import PartitionSpec as P

D = 2304
STEP = 10


def earlier_count(owned):
    number = owned.shape[0]
    places = jnp.arange(number, dtype=jnp.int32)
    earlier = (owned[:, None] == owned[None, :]) & (places[None, :] < places[:, None])
    return jnp.sum(earlier.astype(jnp.int32), axis=1)


def slot_sources(slot, count):
    places = jnp.arange(slot.shape[0], dtype=jnp.int32)
    hits = slot[None, :] == jnp.arange(count, dtype=jnp.int32)[:, None]
    source = jnp.sum(jnp.where(hits, places[None, :], 0), axis=1)
    return (source, jnp.any(hits, axis=1).astype(jnp.float32))


def shift_later(values):
    return jnp.pad(values, ((0, 0), (0, 0), (1, 0)))[:, :, :-1]


def shift_earlier(values):
    return jnp.pad(values, ((0, 0), (0, 0), (0, 1)))[:, :, 1:]


def combine(earlier, later):
    return (earlier[0] * later[0], later[0] * earlier[1] + later[1])


def pooled(preact, keeping):
    channels = preact.shape[1] // 3
    candidate = jnp.tanh(preact[:, :channels])
    forget = jax.nn.sigmoid(preact[:, channels : 2 * channels])
    output_gate = jax.nn.sigmoid(preact[:, 2 * channels :])
    decay = forget * keeping[:, None, :]
    _, cells = lax.associative_scan(combine, (decay, (1.0 - forget) * candidate), axis=2)
    return output_gate * cells


def adam_step(weights, first, second, grad, decay_rate):
    rate = (2.0 * D) ** (-0.5)
    first_new = 0.9 * first + 0.1 * grad
    second_new = 0.999 * second + 0.001 * grad * grad
    first_hat = first_new / (1.0 - 0.9**STEP)
    second_hat = second_new / (1.0 - 0.999**STEP)
    weights_new = weights - rate * (
        first_hat / (jnp.sqrt(second_hat) + 1e-08) + decay_rate * weights
    )
    return (weights_new, first_new, second_new)


def shards(
    inputs,
    resets,
    owners,
    kernel,
    kernel_first,
    kernel_second,
    bias_rows,
    bias_first,
    bias_second,
    cotangent,
):
    streams, local_width, length = inputs.shape
    slots_own, _, block_rows = kernel.shape
    block_count = owners.shape[0] - 3
    dp_size = lax.axis_size("dp")
    dp_index = lax.axis_index("dp")
    kernel_owner = owners[:block_count]
    bias_owner = owners[block_count:]
    kernel_slot = kernel_owner * slots_own + earlier_count(kernel_owner)
    bias_slot = bias_owner * 3 + earlier_count(bias_owner)
    all_kernel, all_bias = (
        lax.all_gather(kernel.astype(jnp.bfloat16), "dp", axis=0, tiled=True),
        lax.all_gather(bias_rows.astype(jnp.bfloat16), "dp", axis=0, tiled=True),
    )
    per_gate = block_count // 3
    double_width = per_gate * block_rows
    full_width = double_width // 2
    gate_cols = 3 * local_width
    arranged = (
        all_kernel[kernel_slot]
        .reshape(3, per_gate, local_width, block_rows)
        .transpose(0, 2, 1, 3)
        .reshape(gate_cols, double_width)
    )
    paired_t = jnp.concatenate([arranged[:, :full_width], arranged[:, full_width:]], axis=0)
    bias_vec = all_bias[bias_slot].astype(jnp.float32).reshape(gate_cols)
    rows = paired_t
    projected = jnp.einsum(
        "ok,skl->sol",
        rows,
        lax.all_gather(inputs, "mp", axis=1, tiled=True),
        preferred_element_type=jnp.float32,
    )
    preact = (
        projected[:, :gate_cols] + shift_later(projected[:, gate_cols:]) + bias_vec[None, :, None]
    )
    keeping = (1 - resets).astype(jnp.float32)
    result, pullback = jax.vjp(lambda values: pooled(values, keeping), preact)
    pre_grad = pullback(cotangent.astype(jnp.float32))[0].astype(jnp.bfloat16)
    joined = jnp.concatenate([pre_grad, shift_earlier(pre_grad)], axis=1)
    bias_grad = jnp.sum(pre_grad.astype(jnp.float32), axis=(0, 2)).reshape(3, local_width)
    pair_grad = jnp.einsum(
        "sol,skl->ok",
        joined,
        lax.all_gather(inputs, "mp", axis=1, tiled=True),
        preferred_element_type=jnp.float32,
    )
    rows = paired_t
    term_rows = lax.psum_scatter(
        jnp.einsum("ok,sol->ksl", rows, joined, preferred_element_type=jnp.float32),
        "mp",
        scatter_dimension=0,
        tiled=True,
    )
    input_grads = jnp.transpose(term_rows.astype(jnp.bfloat16), (1, 0, 2))
    block_grad = pair_grad.reshape(2, 3, local_width, full_width).transpose(1, 2, 0, 3)
    block_grad = (
        block_grad.reshape(3, local_width, per_gate, block_rows)
        .transpose(0, 2, 1, 3)
        .reshape(block_count, local_width, block_rows)
    )
    kernel_source, kernel_valid = slot_sources(kernel_slot, dp_size * slots_own)
    bias_source, bias_valid = slot_sources(bias_slot, dp_size * 3)
    own_kernel_valid = lax.dynamic_slice_in_dim(kernel_valid, dp_index * slots_own, slots_own)
    own_bias_valid = lax.dynamic_slice_in_dim(bias_valid, dp_index * 3, 3)
    total_kernel, total_bias = lax.psum((block_grad, bias_grad), "dp")
    own_kernel_source = lax.dynamic_slice_in_dim(kernel_source, dp_index * slots_own, slots_own)
    own_bias_source = lax.dynamic_slice_in_dim(bias_source, dp_index * 3, 3)
    own_kernel = total_kernel[own_kernel_source] * own_kernel_valid[:, None, None]
    own_bias = total_bias[own_bias_source] * own_bias_valid[:, None]
    squares = jnp.sum(own_kernel * own_kernel) + jnp.sum(own_bias * own_bias)
    grad_norm = jnp.sqrt(lax.psum(squares, ("dp", "mp")))
    factor = 1.0 / jnp.maximum(grad_norm, 1.0)
    kernel_w, kernel_m, kernel_v = adam_step(
        kernel, kernel_first, kernel_second, own_kernel * factor, 0.1
    )
    bias_w, bias_m, bias_v = adam_step(bias_rows, bias_first, bias_second, own_bias * factor, 0.0)
    kernel_mask = own_kernel_valid[:, None, None] > 0.5
    bias_mask = own_bias_valid[:, None] > 0.5
    return (
        result.astype(jnp.bfloat16),
        input_grads,
        jnp.where(kernel_mask, kernel_w, 0.0),
        jnp.where(kernel_mask, kernel_m, 0.0),
        jnp.where(kernel_mask, kernel_v, 0.0),
        jnp.where(bias_mask, bias_w, 0.0),
        jnp.where(bias_mask, bias_m, 0.0),
        jnp.where(bias_mask, bias_v, 0.0),
        grad_norm,
    )


MESH_ID = pl.DeviceIdType.MESH
LANES = 128
BANDS = 3
IM = 256
DEEP = 8
STAGES = 4
VMEM = 61 * 2**20


def place():
    dp, mp = lax.axis_index("dp"), lax.axis_index("mp")
    return dp // 2, lax.rem(dp, 2), mp // 2, lax.rem(mp, 2)


def partners(y, x, z, c):
    dp, mp = y * 2 + x, z * 2 + c
    return {
        "x": (y * 2 + 1 - x, mp),
        "y": ((1 - y) * 2 + x, mp),
        "xy": ((1 - y) * 2 + 1 - x, mp),
        "core": (dp, z * 2 + 1 - c),
        "up": (dp, mp + 2),
        "down": (dp, mp - 2),
    }


def greet(devices):
    barrier = pltpu.get_barrier_semaphore()
    for device in devices:
        pl.semaphore_signal(barrier, inc=1, device_id=device, device_id_type=MESH_ID)
    pl.semaphore_wait(barrier, len(devices))


class Sends:
    def __init__(self, sems):
        self.sems, self.number, self.made = sems, 0, {}

    def start(self, src, dst, recv, device, when=None):
        slot = self.number
        self.number += 1

        def build():
            return pltpu.make_async_remote_copy(
                src_ref=src(),
                dst_ref=dst(),
                send_sem=self.sems.at[slot],
                recv_sem=recv,
                device_id=device,
                device_id_type=MESH_ID,
            )

        if when is None:
            build().start()
        else:
            pl.when(when)(lambda: build().start())
        self.made[slot] = (build, when)
        return slot

    def wait(self, slots):
        for slot in slots:
            build, when = self.made.pop(slot)
            if when is None:
                build().wait_send()
            else:
                pl.when(when)(lambda build=build: build().wait_send())

    def finish(self):
        self.wait(list(self.made))


def landed(ref, sem, device):
    pltpu.make_async_remote_copy(
        src_ref=ref, dst_ref=ref, send_sem=sem, recv_sem=sem, device_id=device, device_id_type=MESH_ID
    ).wait_recv()


def fill_order(perm):
    length = perm.shape[0]
    tile = 16
    column = lax.broadcasted_iota(jnp.int32, (tile, length), 1)
    wanted = lax.rem(column, LANES) * (length // LANES) + column // LANES
    wanted = wanted - lax.broadcasted_iota(jnp.int32, (tile, length), 0)

    def one(i, _):
        at = pl.ds(pl.multiple_of(i * tile, tile), tile)
        perm[at, :] = jnp.where(wanted == i * tile, 1.0, 0.0).astype(jnp.bfloat16)
        return 0

    lax.fori_loop(0, length // tile, one, 0)


def reorder(src, dst, perm):
    def one(i, _):
        at = pl.ds(pl.multiple_of(i * 256, 256), 256)
        moved = jnp.dot(src[...], perm[:, at], preferred_element_type=jnp.float32)
        dst[:, at] = moved.astype(dst.dtype)
        return 0

    lax.fori_loop(0, perm.shape[1] // 256, one, 0)


def restore(src, dst, perm):
    def one(i, _):
        at = pl.ds(pl.multiple_of(i * 256, 256), 256)
        moved = lax.dot_general(
            src[...], perm[at, :], (((1,), (1,)), ((), ())), preferred_element_type=jnp.float32
        )
        dst[:, at] = moved.astype(dst.dtype)
        return 0

    lax.fori_loop(0, perm.shape[0] // 256, one, 0)


def bias_rank(owners, blocks, g):
    owner = owners[blocks + g]
    rank = jnp.int32(0)
    for h in range(g):
        rank += (owners[blocks + h] == owner).astype(jnp.int32)
    return owner, rank


def sigmoid(v):
    return 0.5 * jnp.tanh(0.5 * v) + 0.5


def later(values):
    return [pltpu.roll(values[-1], 1, 1)] + values[:-1]


def scan_both(decay, fresh, source):
    groups = len(decay)
    held, gain = [fresh[0]], [decay[0]]
    for v in range(1, groups):
        held.append(fresh[v] + decay[v] * held[-1])
        gain.append(decay[v] * gain[-1])
    back, fall = [source[-1]], [None]
    for v in range(groups - 2, -1, -1):
        back.insert(0, source[v] + decay[v + 1] * back[0])
        fall.insert(0, decay[v + 1] if fall[0] is None else decay[v + 1] * fall[0])
    ahead = pltpu.roll(decay[0], LANES - 1, 1)
    level, factor = held[-1], gain[-1]
    behind, drop = back[0], fall[0] * ahead
    d = 1
    while d < LANES:
        level = level + factor * pltpu.roll(level, d, 1)
        behind = behind + drop * pltpu.roll(behind, LANES - d, 1)
        if 2 * d < LANES:
            factor = factor * pltpu.roll(factor, d, 1)
            drop = drop * pltpu.roll(drop, LANES - d, 1)
        d *= 2
    carry = pltpu.roll(level, 1, 1)
    cells = [held[v] + gain[v] * carry for v in range(groups)]
    carry = ahead * pltpu.roll(behind, LANES - 1, 1)
    dc = [back[v] + fall[v] * carry for v in range(groups - 1)] + [back[-1] + carry]
    return cells, dc


def gate_tile(pre_at, bias_at, keep, dh_at, h_at, joined_at, add_bias):
    groups = len(keep)
    lane = lax.broadcasted_iota(jnp.int32, keep[0].shape, 1)

    def pre(g):
        now = [pre_at(0, g, v) for v in range(groups)]
        before = later([pre_at(1, g, v) for v in range(groups)])
        before[0] = jnp.where(lane == 0, 0.0, before[0])
        bias = bias_at(g)
        return [n + b + bias for n, b in zip(now, before)]

    cand = [jnp.tanh(v) for v in pre(0)]
    forget = [sigmoid(v) for v in pre(1)]
    gate = [sigmoid(v) for v in pre(2)]
    decay = [f * k for f, k in zip(forget, keep)]
    dh = [dh_at(v) for v in range(groups)]
    cells, dc = scan_both(
        decay,
        [(1.0 - f) * z for f, z in zip(forget, cand)],
        [d * o for d, o in zip(dh, gate)],
    )
    for v in range(groups):
        h_at(v, gate[v] * cells[v])
    past = later(cells)
    grads = (
        [dc[v] * (1.0 - forget[v]) * (1.0 - cand[v] * cand[v]) for v in range(groups)],
        [
            dc[v] * (keep[v] * past[v] - cand[v]) * (forget[v] * (1.0 - forget[v]))
            for v in range(groups)
        ],
        [dh[v] * cells[v] * (gate[v] * (1.0 - gate[v])) for v in range(groups)],
    )
    for g in range(3):
        narrow = [value.astype(jnp.bfloat16) for value in grads[g]]
        wide = [value.astype(jnp.float32) for value in narrow]
        first = jnp.where(lane == LANES - 1, 0.0, pltpu.roll(wide[0], LANES - 1, 1))
        ahead = wide[1:] + [first]
        total = wide[0]
        for v in range(groups):
            joined_at(0, g, v, narrow[v])
            joined_at(1, g, v, ahead[v].astype(jnp.bfloat16))
            if v:
                total = total + wide[v]
        add_bias(jnp.where(lane == g, jnp.sum(total, axis=1, keepdims=True), 0.0))


def fill_tables(owners, table, table_v, sem, blocks, slots):
    per_half = blocks // 6
    down = lax.broadcasted_iota(jnp.int32, (64, LANES), 0)
    along = lax.broadcasted_iota(jnp.int32, (64, LANES), 1)

    def spell(j, both):
        owner = owners[j]
        return jnp.where(down == j, owner, both[0]), jnp.where(along == j, owner, both[1])

    start = (jnp.full((64, LANES), -1, jnp.int32), jnp.full((64, LANES), -2, jnp.int32))
    rows, columns = lax.fori_loop(0, blocks, spell, start)
    rank = jnp.sum(jnp.where((rows == columns) & (down < along), 1, 0), axis=0, keepdims=True)
    table_v[pl.ds(0, 1), :] = columns[:1] * slots + rank
    table_v[pl.ds(1, 1), :] = jnp.sum(jnp.where(rows == along, 1, 0), axis=0, keepdims=True)
    first = pltpu.make_async_copy(table_v.at[pl.ds(0, 8)], table.at[pl.ds(0, 8)], sem.at[0])
    first.start()
    first.wait()

    def place_of(j, held):
        stands = lax.rem(j, per_half) * 6 + lax.rem(j // per_half, 2) * 3 + j // (2 * per_half)
        return jnp.where(along[:1] == table[0, j], stands, held)

    table_v[pl.ds(8, 1), :] = lax.fori_loop(0, blocks, place_of, jnp.zeros((1, LANES), jnp.int32))
    second = pltpu.make_async_copy(table_v.at[pl.ds(8, 8)], table.at[pl.ds(8, 8)], sem.at[1])
    second.start()
    second.wait()


def layer_kernel(
    owners, w_ref, x_ref, cot_ref, res_ref, bias_ref,
    gt, h_out, ig_out, bt, norm,
    table, table_v, wf, wg0, wg1, wg2, wv, xv, cg, rg, bg, hv, p, jv, gb, bcol, bgrad, perm,
    ig, up_got, down_got, core_got, x_got, b_got, squares, s_got, t_got,
    load_sem, table_sem, own_sem, send_sem, w_sem, xg_sem, c_sem, r_sem, bg_sem,
    y_sem, x_sem, core_sem, up_sem, down_sem, z_send, ix_sem, h_sem, b_sem, s_sem, t_sem, free_sem,
):
    y, x, z, c = place()
    dp, mp = y * 2 + x, z * 2 + c
    who = partners(y, x, z, c)
    slots, width, block_rows = gt.shape
    half = width // 2
    length = h_out.shape[1]
    full = xv.shape[1]
    depth = full // width // 2
    per_half = full // block_rows
    blocks = 6 * per_half
    tile = 16
    groups = length // LANES
    wg = (wg0, wg1, wg2)
    band = wg0.shape[1]
    bands = half // band
    owner_x = (1 - x, x)
    mid = depth // 2 - 1
    mp_peers = [(dp, lax.rem(mp + r, 2 * depth)) for r in range(1, 2 * depth)]
    dp_peers = [who["x"], who["y"], who["xy"]]

    def part(index):
        return pl.ds(pl.multiple_of(index * half, half), half)

    def rows_of(place_z, core):
        return pl.ds(pl.multiple_of((place_z * 2 + core) * width, width), width)

    def piece(n, owner):
        return wg[n].at[pl.ds(owner * slots, slots)]

    def reused(t, give):
        row = (t + (2 * bands if give else 0)) * slots
        return wg[row // (4 * slots)], row % (4 * slots)

    def reused_at(t, give):
        ref, row = reused(t, give)
        return ref.at[pl.ds(row, slots)]

    mine = xv.at[1, rows_of(z, c)]
    x_held = jv.at[pl.ds(0, width), pl.ds(0, length)]
    c_held = [jv.at[pl.ds(width + i * half, half), pl.ds(0, length)] for i in range(2)]
    x_load = pltpu.make_async_copy(x_ref, x_held, load_sem.at[0])
    c_loads = [
        pltpu.make_async_copy(cot_ref.at[part(x)], c_held[0], load_sem.at[1]),
        pltpu.make_async_copy(cot_ref.at[part(1 - x)], c_held[1], load_sem.at[2]),
    ]

    def w_load(i):
        at = pl.multiple_of((x if i % 2 == 0 else 1 - x) * half + (i // 2) * band, 16)
        return pltpu.make_async_copy(
            w_ref.at[:, pl.ds(at, band)], wf.at[i % 2], load_sem.at[3 + i % 2]
        )

    w_load(0).start()
    x_load.start()
    w_load(1).start()
    for load in c_loads:
        load.start()
    greet(mp_peers + dp_peers)
    sends = Sends(send_sem)
    def slice_of(q, place_z, core):
        return xv.at[q, rows_of(place_z, core)]

    def spread(q, place_z, up, down, core):
        ref = lambda: slice_of(q, place_z, c)
        recv = xg_sem.at[q, place_z * 2 + c]
        for name, when in (("up", up), ("down", down), ("core", core)):
            if when is not False:
                sends.start(ref, ref, recv, who[name], when)

    y_pieces, x_pieces = [], []

    def y_piece(n):
        ref = lambda: piece(n, dp)
        y_pieces.append(sends.start(ref, ref, w_sem.at[n, dp], who["y"]))

    def x_piece(n):
        x_pieces.append(
            sends.start(
                lambda: gb.at[n, pl.ds(0, slots)],
                lambda: piece(n, dp),
                w_sem.at[n, dp],
                who["x"],
            )
        )

    def take_weights(i):
        n = i // 2
        w_load(i).wait()

        def cast(r, _):
            value = wf[i % 2, r].astype(jnp.bfloat16)
            if i % 2 == 0:
                wg[n][dp * slots + r] = value
            else:
                gb[n, r] = value
            return 0

        lax.fori_loop(0, slots, cast, 0)
        if i + 2 < 2 * bands:
            w_load(i + 2).start()

    fill_order(perm)
    take_weights(0)
    y_piece(0)
    x_load.wait()
    reorder(x_held, mine, perm)
    spread(1, z, z < depth - 1, z > 0, None)
    sends.start(lambda: mine, lambda: xv.at[0, rows_of(z, c)], xg_sem.at[0, mp], who["x"])
    for i in range(1, 2 * bands):
        take_weights(i)
    for name in ("x", "y", "xy"):
        sends.start(lambda: bias_ref, lambda: bg.at[dp], bg_sem.at[dp], who[name])
    bg[dp] = bias_ref[...]
    for load in c_loads:
        load.wait()
    reorder(c_held[0], cg.at[1], perm)
    reorder(c_held[1], hv.at[0], perm)
    keep_row = 1.0 - jnp.broadcast_to(res_ref[...], (16, length)).astype(jnp.float32)
    rg[1] = jnp.dot(keep_row.astype(jnp.bfloat16), perm[...], preferred_element_type=jnp.float32)[:1]
    sends.start(lambda: rg.at[1], lambda: rg.at[0], r_sem, who["x"])
    fill_tables(owners, table, table_v, table_sem, blocks, slots)
    for owner in (y * 2 + 1 - x, (1 - y) * 2 + x, (1 - y) * 2 + 1 - x):
        landed(bg.at[owner], bg_sem.at[owner], who["x"])
    lane_of = lax.broadcasted_iota(jnp.int32, (half, width), 1)
    row_of = lax.broadcasted_iota(jnp.int32, (half, width), 0)
    diagonal = lane_of == row_of + x * half
    for g in range(3):
        owner, rank = bias_rank(owners, blocks, g)
        held = bg[owner]
        line = jnp.zeros((1, width), jnp.float32)
        for r in range(3):
            line = jnp.where(rank == r, held[r : r + 1], line)
        line = line.astype(jnp.bfloat16).astype(jnp.float32)
        column = jnp.sum(jnp.where(diagonal, line, 0.0), axis=1, keepdims=True)
        bcol[pl.ds(g * half, half), :] = jnp.broadcast_to(column, (half, LANES))
    bgrad[...] = jnp.zeros_like(bgrad)
    squares[...] = jnp.zeros_like(squares)

    def along_z(q, d):
        for at, on, on_z, device, up in (
            (z - d, z >= d, z < depth - 1, who["down"], True),
            (z + d, z + d < depth, z > 0, who["up"], False),
        ):
            if q == 0:
                on = on & (at != mid)

            @pl.when(on)
            def _(at=at, device=device):
                landed(slice_of(q, at, c), xg_sem.at[q, at * 2 + c], device)

            further = on & on_z
            spread(q, at, further if up else False, False if up else further, on)

    def pass_on(n):
        owner = y * 2 + 1 - x
        ref = lambda: piece(n, owner)
        landed(ref(), w_sem.at[n, owner], who["x"])
        if n + 1 < bands:
            x_piece(n + 1)
        y_pieces.append(sends.start(ref, ref, w_sem.at[n, owner], who["y"]))

    def arrange(n):
        for owner in ((1 - y) * 2 + x, (1 - y) * 2 + 1 - x):
            landed(piece(n, owner), w_sem.at[n, owner], who["y"])
        for h in range(2):
            for g in range(3):

                def one(k, _, h=h, g=g):
                    columns = pl.ds(pl.multiple_of(k * block_rows, block_rows), block_rows)
                    first = table[0, g * 2 * per_half + h * per_half + k]
                    wv[pl.ds((n * 6 + h * 3 + g) * band, band), columns] = wg[n][first]
                    return 0

                lax.fori_loop(0, per_half, one, 0)

    def from_core(q):
        for k in range(depth):
            landed(slice_of(q, k, 1 - c), xg_sem.at[q, k * 2 + 1 - c], who["core"])

    def project(q, n):
        rows = pl.ds(n * 6 * band, 6 * band)

        p[...] = jnp.dot(wv[rows, :], xv[q], preferred_element_type=jnp.float32)

    def gates(q, n):
        lane = lax.broadcasted_iota(jnp.int32, (band, LANES), 1)
        keep = [
            jnp.broadcast_to(rg[q, :, pl.ds(v * LANES, LANES)], (band, LANES))
            for v in range(groups)
        ]
        keep[0] = jnp.where(lane == 0, 0.0, keep[0])

        at = pl.ds(n * band, band)

        def row(h, g):
            return pl.ds((n * 6 + h * 3 + g) * band, band)

        def h_at(v, value):
            hv[q, at, pl.ds(v * LANES, LANES)] = value.astype(jnp.bfloat16)

        def joined_at(h, g, v, value):
            jv[row(h, g), pl.ds(q * length + v * LANES, LANES)] = value

        def add_bias(value):
            bgrad[at, :] += value

        gate_tile(
            lambda h, g, v: p[pl.ds((h * 3 + g) * band, band), pl.ds(v * LANES, LANES)],
            lambda g: bcol[pl.ds(g * half + n * band, band), :],
            keep,
            lambda v: cg[q, at, pl.ds(v * LANES, LANES)].astype(jnp.float32),
            h_at,
            joined_at,
            add_bias,
        )

    def weight_grad(n):
        at = pl.ds(n * 6 * band, 6 * band)
        both = (((1,), (1,)), ((), ()))

        def one(k, _):
            rows = pl.ds(pl.multiple_of(k * block_rows, block_rows), block_rows)
            total = lax.dot_general(
                jv[at, pl.ds(0, length)], xv[0, rows, :], both, preferred_element_type=jnp.float32
            )
            total += lax.dot_general(
                jv[at, pl.ds(length, length)], xv[1, rows, :], both, preferred_element_type=jnp.float32
            )
            total = total.astype(jnp.bfloat16)
            for i in range(6):
                gb[n, k * 6 + i] = total[i * band : (i + 1) * band]
            return 0

        lax.fori_loop(0, per_half, one, 0)

        for q in range(2):

            def pack(r, _, q=q):
                ref, row = reused(n * 2 + q, True)
                ref[row + r] = gb[n, table[8, ((1 - y) * 2 + owner_x[q]) * slots + r]]
                return 0

            lax.fori_loop(0, slots, pack, 0)

    def y_send(t):
        sends.start(
            lambda: reused_at(t, True),
            lambda: reused_at(t, False),
            y_sem.at[t],
            who["y"],
        )

    def input_grad(q):
        number = full // IM
        order = sorted(range(number), key=lambda k: min(k, number - 1 - k))
        waiting = list(range(depth))
        for place_of, k in enumerate(order):
            ig[q, pl.ds(k * IM, IM), :] = lax.dot_general(
                wv[:, pl.ds(k * IM, IM)],
                jv[:, pl.ds(q * length, length)],
                (((0,), (0,)), ((), ())),
                preferred_element_type=jnp.float32,
            ).astype(jnp.bfloat16)
            for d in list(waiting):
                needs = set(range(2 * d * width // IM, ((2 * d + 2) * width - 1) // IM + 1))
                if needs <= set(order[: place_of + 1]):
                    waiting.remove(d)
                    sends.start(
                        lambda d=d: ig.at[q, rows_of(d, 1 - c)],
                        lambda d=d: core_got.at[q, d],
                        core_sem.at[q, d],
                        who["core"],
                    )

    def add_tiles(refs):
        def one(i, _):
            at = pl.ds(pl.multiple_of(i * tile, tile), tile)
            total = refs[0][at, :].astype(jnp.float32)
            for ref in refs[1:]:
                total += ref[at, :].astype(jnp.float32)
            refs[0][at, :] = total.astype(jnp.bfloat16)
            return 0

        lax.fori_loop(0, width // tile, one, 0)

    def z_send_of(q, dest, got, recv, device, sem):
        return pltpu.make_async_remote_copy(
            src_ref=ig.at[q, rows_of(dest, c)],
            dst_ref=got.at[q, dest],
            send_sem=sem,
            recv_sem=recv.at[q, dest],
            device_id=device,
            device_id_type=MESH_ID,
        )

    up_items = [(0, d) for d in range(depth - 1, 0, -1) if d != mid]
    up_items += [(1, d) for d in range(depth - 1, 0, -1)]
    down_items = [(0, d) for d in range(depth - 1) if d != mid]
    down_items += [(1, d) for d in range(depth - 1)]

    def z_tick(t, first=True, rest=True):
        for index, (items, after, got, recv, source, target) in enumerate(
            (
                (up_items, z, up_got, up_sem, who["down"], who["up"]),
                (down_items, depth - 1 - z, down_got, down_sem, who["up"], who["down"]),
            )
        ):
            item = t - after
            q = jnp.int32(0)
            dest = jnp.int32(0)
            on = item < 0
            for i, (q_of, dest_of) in enumerate(items):
                goes = z < dest_of if index == 0 else z > dest_of
                q = jnp.where(item == i, q_of, q)
                dest = jnp.where(item == i, dest_of, dest)
                on = (on & (item != i)) | (goes & (item == i))
            on = on & (item >= 0) & (item < len(items))
            if not (first and rest):
                on = on & ((after == 0) if first else (after > 0))

            @pl.when(on)
            def _(index=index, after=after, got=got, recv=recv, source=source, target=target, q=q, dest=dest):
                landed(core_got.at[q, dest], core_sem.at[q, dest], who["core"])
                mine = ig.at[q, rows_of(dest, c)]

                @pl.when(after == 0)
                def _():
                    add_tiles((mine, core_got.at[q, dest]))

                @pl.when(after > 0)
                def _():
                    landed(got.at[q, dest], recv.at[q, dest], source)
                    add_tiles((mine, core_got.at[q, dest], got.at[q, dest]))

                z_send_of(q, dest, got, recv, target, z_send.at[index, q, dest]).start()

    def x_first():
        mine = ig.at[0, rows_of(mid, c)]
        landed(core_got.at[0, mid], core_sem.at[0, mid], who["core"])
        add_tiles((mine, core_got.at[0, mid]))
        sends.start(lambda: mine, lambda: up_got.at[0, mid], up_sem.at[0, mid], who["x"])

    def x_first_got():
        landed(up_got.at[0, mid], up_sem.at[0, mid], who["x"])
        add_tiles((ig.at[1, rows_of(mid, c)], up_got.at[0, mid]))

    def z_last(q):
        mine = ig.at[q, rows_of(z, c)]
        core = core_got.at[q, z]

        def joint(when, extra, above, below):
            @pl.when(when)
            def _():
                landed(core, core_sem.at[q, z], who["core"])
                refs = (mine, core)
                if extra:
                    landed(x_got, ix_sem, who["x"])
                    refs += (x_got,)
                if below:
                    landed(up_got.at[q, z], up_sem.at[q, z], who["down"])
                    refs += (up_got.at[q, z],)
                if above:
                    landed(down_got.at[q, z], down_sem.at[q, z], who["up"])
                    refs += (down_got.at[q, z],)
                add_tiles(refs)

        extra = q == 1
        joint(z == 0, extra, True, False)
        joint(z == depth - 1, extra, False, True)
        joint((z > 0) & (z < depth - 1) & (z != mid), extra, True, True)
        if q == 1:
            joint(z == mid, False, True, True)
            restore(mine, x_got, perm)
            copy = pltpu.make_async_copy(x_got, ig_out, own_sem.at[1])
            copy.start()
            own_copies.append(copy)
        else:
            sends.start(lambda: mine, lambda: x_got, ix_sem, who["x"], z != mid)

    own_copies = []
    next_piece = {2: 3, 4: 5}

    def own_chunk(t):
        n, q = t // 2, t % 2
        landed(reused_at(t, False), y_sem.at[t], who["y"])
        ref, row = reused(t, False)
        if t in next_piece:
            y_send(next_piece[t])
        owner = y * 2 + owner_x[q]

        def one(r, _):
            valid = jnp.broadcast_to(r < table[1, owner], (band, block_rows))
            total = gb[n, table[8, owner * slots + r]].astype(jnp.float32)
            total += ref[row + r].astype(jnp.float32)
            total = jnp.where(valid, total, 0.0)
            ref[row + r] = total.astype(jnp.bfloat16)
            squares[...] += jnp.sum((total * total).reshape(band // 8, 8, block_rows), axis=0)
            return 0

        lax.fori_loop(0, slots, one, 0)
        src = lambda: reused_at(t, False)
        dst = lambda: gt.at[:, pl.ds(pl.multiple_of(x * half + n * band, 16), band)]
        if q == 0:
            sends.start(src, dst, x_sem.at[n], who["x"])
        else:
            copy = pltpu.make_async_copy(src(), dst(), own_sem.at[2 + n])
            copy.start()
            own_copies.append(copy)

    def bias_sum():
        landed(b_got.at[0], b_sem.at[0], who["y"])
        total = bgrad[...] + b_got[0]
        b_got[1] = total
        bt[x] = total
        sends.start(lambda: b_got.at[1], lambda: bt.at[x], b_sem.at[1], who["x"])
        counted = jnp.broadcast_to(y == 0, (half, LANES))
        each = jnp.where(counted, total * total, 0.0)
        squares[:, pl.ds(0, LANES)] += jnp.sum(each.reshape(half // 8, 8, LANES), axis=0)

    landed(xv.at[0, rows_of(z, c)], xg_sem.at[0, mp], who["x"])
    spread(0, z, (z < depth - 1) & (z != mid), (z > 0) & (z != mid), None)
    cot_sent = sends.start(lambda: hv.at[0], lambda: cg.at[0], c_sem, who["x"])
    x_piece(0)
    y_piece(1)
    along_z(1, 1)
    for d in range(1, depth):
        along_z(0, d)
        if d == 1:
            y_piece(2)
        if d <= 2:
            pass_on(d - 1)
            if d + 1 < depth - 1:
                along_z(1, d + 1)
    pass_on(2)
    sends.start(
        lambda: slice_of(1, mid, c),
        lambda: slice_of(0, mid, c),
        xg_sem.at[0, mid * 2 + c],
        who["x"],
        z != mid,
    )
    along_z(1, depth - 1)
    landed(cg.at[0], c_sem, who["x"])
    landed(rg.at[0], r_sem, who["x"])
    sends.wait([cot_sent])
    from_core(1)
    def layer_part(q, n):
        project(q, n)
        gates(q, n)

    def give_part(n):
        weight_grad(n)
        if n == 0:
            pl.semaphore_wait(free_sem, 1)
            y_send(0)
            y_send(1)

    ticks = 2 * depth - 3
    arrange(0)
    layer_part(1, 0)
    arrange(1)
    sends.wait([y_pieces[k] for k in (0, 1, 3, 4)] + x_pieces)
    pl.semaphore_signal(free_sem, inc=1, device_id=who["y"], device_id_type=MESH_ID)
    layer_part(1, 1)

    @pl.when(z != mid)
    def _():
        landed(slice_of(0, mid, c), xg_sem.at[0, mid * 2 + c], who["x"])

    spread(0, mid, False, False, z != mid)
    from_core(0)
    layer_part(0, 0)
    give_part(0)
    layer_part(0, 1)
    arrange(2)
    sends.wait([y_pieces[k] for k in (2, 5)])
    layer_part(0, 2)
    input_grad(0)
    z_tick(0)
    x_first()
    give_part(1)
    y_send(2)
    z_tick(1, rest=False)
    layer_part(1, 2)
    sends.start(lambda: bgrad, lambda: b_got.at[0], b_sem.at[0], who["y"])
    input_grad(1)
    z_tick(1, first=False)
    own_chunk(0)
    give_part(2)
    y_send(4)
    z_tick(2, rest=False)
    x_first_got()
    z_tick(2, first=False)
    z_tick(3, rest=False)
    own_chunk(1)
    for q in (0, 1):
        restore(hv.at[q], cg.at[q], perm)
    sends.start(lambda: cg.at[0], lambda: h_out.at[part(x)], h_sem, who["x"])
    h_own = pltpu.make_async_copy(cg.at[1], h_out.at[part(x)], own_sem.at[0])
    h_own.start()
    own_copies.append(h_own)
    bias_sum()
    own_chunk(2)
    z_last(0)
    left = [4, 3, 5]
    for t in range(depth - 1, ticks):
        z_tick(t, first=t > depth - 1)
        if left:
            own_chunk(left.pop(0))
    for t in left:
        own_chunk(t)
    total = squares[:, pl.ds(0, LANES)] + squares[:, pl.ds(LANES, LANES)]
    s_got[mp] = total
    for device in mp_peers:
        sends.start(lambda: s_got.at[mp], lambda: s_got.at[mp], s_sem.at[mp], device)
    for device in mp_peers:
        landed(s_got.at[device[1]], s_sem.at[device[1]], device)
    total = s_got[0]
    for k in range(1, 2 * depth):
        total = total + s_got[k]
    t_got[dp] = total
    for device in dp_peers:
        sends.start(lambda: t_got.at[dp], lambda: t_got.at[dp], t_sem.at[dp], device)
    z_last(1)
    for device in dp_peers:
        landed(t_got.at[device[0]], t_sem.at[device[0]], device)
    total = t_got[0]
    for k in range(1, 4):
        total = total + t_got[k]
    norm[...] = jnp.broadcast_to(jnp.sqrt(jnp.sum(total, keepdims=True)), norm.shape)
    for n in range(bands):
        landed(gt.at[:, pl.ds(pl.multiple_of((1 - x) * half + n * band, 16), band)], x_sem.at[n], who["x"])
    landed(h_out.at[part(1 - x)], h_sem, who["x"])
    landed(bt.at[1 - x], b_sem.at[1], who["x"])

    for index, (items, got, recv, target) in enumerate(
        ((up_items, up_got, up_sem, who["up"]), (down_items, down_got, down_sem, who["down"]))
    ):
        for q, dest in items:

            @pl.when(z < dest if index == 0 else z > dest)
            def _(index=index, got=got, recv=recv, target=target, q=q, dest=dest):
                z_send_of(q, dest, got, recv, target, z_send.at[index, q, dest]).wait_send()

    for copy in own_copies:
        copy.wait()
    sends.finish()


def adam_turn(weights, first, second, grad, decay_rate):
    rate = (2.0 * D) ** (-0.5)
    first_new = 0.9 * first + 0.1 * grad
    second_new = 0.999 * second + (0.001 * grad) * grad
    second_hat = second_new * (1.0 / (1.0 - 0.999**STEP))
    root = second_hat * lax.rsqrt(jnp.maximum(second_hat, 1e-37)) + 1e-08
    turn = pl.reciprocal(root, approx=True)
    turn = turn * (2.0 - root * turn)
    step = (first_new * (rate / (1.0 - 0.9**STEP))) * turn
    return (weights * (1.0 - rate * decay_rate) - step, first_new, second_new)


def adam_kernel(
    owners, norm, bt, bw, bm, bv, g, w, m, v, h_in, ig_in,
    w_new, m_new, v_new, bw_new, bm_new, bv_new, h_out, ig_out, norm_out,
    g_held, held, made, kept, in_sem, out_sem, pass_sem,
):
    deep, rows, width, block_rows = g_held.shape
    stages = made.shape[1]
    turns = g.shape[0] // rows
    half = width // 2
    blocks = owners.shape[0] - 3
    me = lax.axis_index("dp")

    def taken(i):
        slot = lax.rem(i, deep)
        at = pl.ds(i * rows, rows)
        copies = [pltpu.make_async_copy(g.at[at], g_held.at[slot], in_sem.at[slot, 3])]
        for k, ref in enumerate((w, m, v)):
            copies.append(pltpu.make_async_copy(ref.at[at], held.at[k, slot], in_sem.at[slot, k]))
        return copies

    def given(i):
        slot = lax.rem(i, stages)
        at = pl.ds(i * rows, rows)
        return [
            pltpu.make_async_copy(made.at[k, slot], ref.at[at], out_sem.at[slot, k])
            for k, ref in enumerate((w_new, m_new, v_new))
        ]

    for i in range(min(deep, turns)):
        for copy in taken(jnp.int32(i)):
            copy.start()
    come = [
        pltpu.make_async_copy(ref, kept.at[k], pass_sem.at[k]) for k, ref in enumerate((h_in, ig_in))
    ]
    leave = [
        pltpu.make_async_copy(kept.at[k], ref, pass_sem.at[2 + k])
        for k, ref in enumerate((h_out, ig_out))
    ]
    for copy in come:
        copy.start()
    norm_out[...] = norm[:1, :1]
    number = jnp.int32(0)
    for j in range(blocks):
        number += (owners[j] == me).astype(jnp.int32)
    factor = 1.0 / jnp.maximum(norm[:1, :1], 1.0)
    lane_of = lax.broadcasted_iota(jnp.int32, (half, width), 1)
    row_of = lax.broadcasted_iota(jnp.int32, (half, width), 0)
    row = lax.broadcasted_iota(jnp.int32, (3, width), 0)
    grads = jnp.zeros((3, width), jnp.float32)
    filled = jnp.zeros((3, width), jnp.int32)
    for gate in range(3):
        owner, rank = bias_rank(owners, blocks, gate)
        line = jnp.zeros((1, width), jnp.float32)
        for h in range(2):
            column = bt[h][:, gate : gate + 1]
            line += jnp.sum(
                jnp.where(lane_of == row_of + h * half, column, 0.0), axis=0, keepdims=True
            )
        here = (row == rank) & jnp.broadcast_to(owner == me, (3, width))
        grads = jnp.where(here, line, grads)
        filled = jnp.where(here, 1, filled)
    news = adam_step(bw[...], bm[...], bv[...], grads * factor, 0.0)
    for ref, new in zip((bw_new, bm_new, bv_new), news):
        ref[...] = jnp.where(filled > 0, new, 0.0)

    def turn(i, _):
        slot, stage = lax.rem(i, deep), lax.rem(i, stages)
        for copy in taken(i):
            copy.wait()

        @pl.when(i >= stages)
        def _():
            for copy in given(i - stages):
                copy.wait()

        for r in range(rows):
            grad = g_held[slot, r].astype(jnp.float32) * factor
            valid = jnp.broadcast_to(i * rows + r < number, (width, block_rows))
            news = adam_turn(held[0, slot, r], held[1, slot, r], held[2, slot, r], grad, 0.1)
            for k, new in enumerate(news):
                made[k, stage, r] = jnp.where(valid, new, 0.0)
        for copy in given(i):
            copy.start()

        @pl.when(i + deep < turns)
        def _():
            for copy in taken(i + deep):
                copy.start()

        @pl.when(i == turns // 2)
        def _():
            for k in range(2):
                come[k].wait()
                leave[k].start()

        return 0

    lax.fori_loop(0, turns, turn, 0)
    for i in range(max(0, turns - stages), turns):
        for copy in given(jnp.int32(i)):
            copy.wait()
    for copy in leave:
        copy.wait()


def paired(
    inputs, resets, owners, kernel, kernel_first, kernel_second, bias_rows, bias_first, bias_second, cotangent
):
    _, width, length = inputs.shape
    slots, _, block_rows = kernel.shape
    blocks = owners.shape[0] - 3
    full = width * lax.axis_size("mp")
    depth = lax.axis_size("mp") // 2
    half = width // 2
    bf16, f32 = jnp.bfloat16, jnp.float32
    shape = jax.ShapeDtypeStruct
    hbm = pl.BlockSpec(memory_space=pltpu.MemorySpace.HBM)
    vmem = pl.BlockSpec(memory_space=pltpu.VMEM)
    smem = pl.BlockSpec(memory_space=pltpu.SMEM)
    dma = pltpu.SemaphoreType.DMA
    band = half // BANDS
    gt, h_new, ig, bt, norm = pl.pallas_call(
        layer_kernel,
        out_shape=(
            shape((slots, width, block_rows), bf16),
            shape((width, length), bf16),
            shape((width, length), bf16),
            shape((2, half, LANES), f32),
            shape((8, LANES), f32),
        ),
        in_specs=[smem] + [hbm] * 3 + [vmem] * 2,
        out_specs=[hbm, hbm, hbm, vmem, vmem],
        scratch_shapes=[
            pltpu.SMEM((16, LANES), jnp.int32),
            pltpu.VMEM((16, LANES), jnp.int32),
            pltpu.VMEM((2, slots, band, block_rows), f32),
            pltpu.VMEM((4 * slots, band, block_rows), bf16),
            pltpu.VMEM((4 * slots, band, block_rows), bf16),
            pltpu.VMEM((4 * slots, band, block_rows), bf16),
            pltpu.VMEM((6 * half, full), bf16),
            pltpu.VMEM((2, full, length), bf16),
            pltpu.VMEM((2, half, length), bf16),
            pltpu.VMEM((2, 1, length), f32),
            pltpu.VMEM((4, 3, width), f32),
            pltpu.VMEM((2, half, length), bf16),
            pltpu.VMEM((6 * band, length), f32),
            pltpu.VMEM((6 * half, 2 * length), bf16),
            pltpu.VMEM((BANDS, blocks, band, block_rows), bf16),
            pltpu.VMEM((3 * half, LANES), f32),
            pltpu.VMEM((half, LANES), f32),
            pltpu.VMEM((length, length), bf16),
            pltpu.VMEM((2, full, length), bf16),
            pltpu.VMEM((2, depth, width, length), bf16),
            pltpu.VMEM((2, depth, width, length), bf16),
            pltpu.VMEM((2, depth, width, length), bf16),
            pltpu.VMEM((width, length), bf16),
            pltpu.VMEM((2, half, LANES), f32),
            pltpu.VMEM((8, block_rows), f32),
            pltpu.VMEM((2 * depth, 8, LANES), f32),
            pltpu.VMEM((4, 8, LANES), f32),
            dma((5,)),
            dma((2,)),
            dma((2 + BANDS,)),
            dma((96,)),
            dma((BANDS, 4)),
            dma((2, 2 * depth)),
            dma,
            dma,
            dma((4,)),
            dma((2 * BANDS,)),
            dma((BANDS,)),
            dma((2, depth)),
            dma((2, depth)),
            dma((2, depth)),
            dma((2, 2, depth)),
            dma,
            dma,
            dma((2,)),
            dma((2 * depth,)),
            dma((4,)),
            pltpu.SemaphoreType.REGULAR,
        ],
        compiler_params=pltpu.CompilerParams(
            collective_id=0, has_side_effects=True, vmem_limit_bytes=VMEM
        ),
        name="layer",
    )(
        owners,
        kernel,
        inputs.reshape(width, length),
        cotangent.reshape(width, length),
        resets,
        bias_rows,
    )
    rows = 1
    news = pl.pallas_call(
        adam_kernel,
        out_shape=(shape(kernel.shape, f32),) * 3
        + (shape(bias_rows.shape, f32),) * 3
        + (shape((width, length), bf16),) * 2
        + (shape((1, 1), f32),),
        in_specs=[smem] + [vmem] * 5 + [hbm] * 6,
        out_specs=[hbm] * 3 + [vmem] * 3 + [hbm] * 2 + [vmem],
        scratch_shapes=[
            pltpu.VMEM((DEEP, rows, width, block_rows), bf16),
            pltpu.VMEM((3, DEEP, rows, width, block_rows), f32),
            pltpu.VMEM((3, STAGES, rows, width, block_rows), f32),
            pltpu.VMEM((2, width, length), bf16),
            dma((DEEP, 4)),
            dma((STAGES, 3)),
            dma((4,)),
        ],
        compiler_params=pltpu.CompilerParams(vmem_limit_bytes=VMEM),
        name="adam",
    )(
        owners, norm, bt, bias_rows, bias_first, bias_second, gt, kernel, kernel_first, kernel_second, h_new, ig
    )
    *updated, h_last, ig_last, norm_last = news
    return (h_last[None], ig_last[None], *updated, norm_last[0, 0])


def solution(mesh):
    placed = (
        P("dp", "mp", None),
        P("dp", None),
        P(),
        P("dp", "mp", None),
        P("dp", "mp", None),
        P("dp", "mp", None),
        P("dp", "mp"),
        P("dp", "mp"),
        P("dp", "mp"),
        P("dp", "mp", None),
    )
    fits = mesh.shape["dp"] == 4 and mesh.shape["mp"] == 8
    return jax.shard_map(
        paired if fits else shards,
        mesh=mesh,
        in_specs=placed,
        out_specs=(
            P("dp", "mp", None),
            P("dp", "mp", None),
            P("dp", "mp", None),
            P("dp", "mp", None),
            P("dp", "mp", None),
            P("dp", "mp"),
            P("dp", "mp"),
            P("dp", "mp"),
            P(),
        ),
        check_vma=False,
    )
```
